512 devices in a mesh: tile: 64 (over z_hi, y, core), head: 8 (over x, z_lo).
Axes of the slice: x: 4, y: 8, z: 8 (z_hi: 4, z_lo: 2; z = z_hi * 2 + z_lo), core: 2. Of those that a mesh axis runs over, the one named last changes fastest.
Arguments:
- queries: bfloat16 [16384, 3072], P('tile', 'head'), may hold values from -32 to 32, as said below
- key_rows: bfloat16 [16384, 3072], P('tile', 'head'), may hold values from -32 to 32, as said below
- value_rows: bfloat16 [16384, 3072], P('tile', 'head'), may hold values from -18 to 18
- windows: int32 [64, 3], P('tile'), may hold values from 0 to 1
- residual: bfloat16 [16384, 3072], P('tile', 'head'), may hold values from -6 to 6
- out_weight: bfloat16 [3072, 3072], P('head'), may hold values from -0.109375 to 0.109375
- gate_scale: float32 [3072], P('head'), may hold values from 1 to 4
Outputs:
- layer_out: bfloat16 [16384, 3072], P('tile', 'head')
The draws below stay inside these ranges and needn't reach their ends.
Inputs may be any that keep to these rules, and one draw needn't show every extreme that they name: `queries`: queries per head. `key_rows`: keys per head.
All inputs are finite; a program needn't handle non-finite values.
Results may differ from the reference program's by a relative error of at most 0.017.
Values may be sent and summed in bfloat16 or wider, within the bound.
No kernel may reach another device: no remote copies, remote signals or barrier semaphores. Data moves between devices by JAX's collectives and lax.ppermute only.
A program may use at most 64 MiB of HBM per device.

```python
import math
import jax
import jax.numpy as jnp
from jax import lax

D = 3072
HEADS = 24
HD = 128
HEIGHT_TILES = 4
WT = 1
TILE = 256
TOK_DEV = 256
TOKENS = 16384
TIME_TILES = 16
TILES = 64
N_TILE = 64
N_HEAD = 8


def draw_queries(key, part):
    key = jax.random.fold_in(key, 11)
    fresh = jnp.clip(jax.random.normal(key, (TOKENS, HEADS * HD), jnp.float32), -6.0, 6.0)
    return fresh.astype(jnp.bfloat16)


def draw_key_rows(key, part):
    key = jax.random.fold_in(key, 12)
    fresh = jnp.clip(jax.random.normal(key, (TOKENS, HEADS * HD), jnp.float32), -6.0, 6.0)
    return fresh.astype(jnp.bfloat16)


def touch_ends(entries, key, low, high):
    longest = entries.shape.index(max(entries.shape))
    spots = []
    for shift in (0, 1):
        where = [jax.random.randint(jax.random.fold_in(key, axis), (), 0, length) for axis, length in enumerate(entries.shape)]
        where[longest] = (where[longest] + shift) % entries.shape[longest]
        spots.append(tuple(where))
    return entries.at[spots[0]].set(low).at[spots[1]].set(high)


def level_of(stream_key, shape, pieces, smallest, high):
    def one(position, parts):
        steps = jax.random.uniform(jax.random.fold_in(jax.random.fold_in(stream_key, 6), position), (parts,), jnp.float32, smallest / len(pieces), high / len(pieces))
        return jnp.repeat(jnp.exp(steps), shape[position] // parts).reshape((-1,) + (1,) * (len(shape) - position - 1))

    gain = one(*pieces[0])
    for cut in pieces[1:]:
        gain = gain * one(*cut)
    return gain


def normal_values(own_key, dims, scale, limit, shards=(), kind=jnp.bfloat16):
    values = jax.random.normal(own_key, dims, jnp.float32) * scale
    if len(shards) > 0:
        values = level_of(own_key, dims, shards, -0.22, 0.18) * values
    return jnp.clip(values, min=-limit, max=limit).astype(kind)


def setup_inputs(seed: int = 0) -> dict:
    seeds = jax.random.split(jax.random.key(seed), 8)
    queries = draw_queries(jax.random.fold_in(seeds[7], 71), 0)
    key_rows = draw_key_rows(jax.random.fold_in(seeds[7], 71), 0)
    value_rows = normal_values(seeds[2], (TOKENS, HEADS * HD), 3.0, 18.0, ((0, 64), (1, 8)))
    windows = touch_ends(jax.random.randint(seeds[3], (TILES, 3), 0, 2), jax.random.fold_in(seeds[3], 1), 0, 1).astype(jnp.int32)
    residual = normal_values(seeds[4], (TOKENS, D), 1.0, 6.0, ((0, 64), (1, 8)))
    out_weight = normal_values(seeds[5], (HEADS * HD, D), (HEADS * HD) ** -0.5, 0.109375, ((0, 8),))
    gate_scale = jnp.clip(jnp.exp(math.log(4.0) - 1.3862944 * jax.random.uniform(seeds[6], (D,), jnp.float32) ** level_of(seeds[6], (D,), ((0, 8),), -0.2, 0.2)), 1.0, 4.0)
    return dict(queries=queries, key_rows=key_rows, value_rows=value_rows, windows=windows, residual=residual, out_weight=out_weight, gate_scale=gate_scale)


OFFSETS = [(-1, -1), (-1, 0), (-1, 1), (0, -1), (0, 0), (0, 1), (1, -1), (1, 0), (1, 1)]


def build_mask(place, window_block, time_tiles, width_tiles, tile_len):
    time_pos = place // HEIGHT_TILES
    height_pos = place % HEIGHT_TILES
    step_time = jnp.array([offset[0] for offset in OFFSETS], jnp.int32)
    step_height = jnp.array([offset[1] for offset in OFFSETS], jnp.int32)
    inside = (time_pos + step_time >= 0) & (time_pos + step_time < time_tiles)
    inside = inside & (height_pos + step_height >= 0) & (height_pos + step_height < HEIGHT_TILES)
    tile_range = jnp.arange(width_tiles, dtype=jnp.int32)
    width_gap = jnp.abs(tile_range[None, :] - tile_range[:, None])
    allowed = inside[None, :, None]
    allowed = allowed & (jnp.abs(step_time)[None, :, None] <= window_block[:, 0][:, None, None])
    allowed = allowed & (jnp.abs(step_height)[None, :, None] <= window_block[:, 1][:, None, None])
    allowed = allowed & (width_gap[:, None, :] <= window_block[:, 2][:, None, None])
    flat = allowed.reshape(width_tiles, 9 * width_tiles)
    return jnp.repeat(jnp.repeat(flat, tile_len, axis=0), tile_len, axis=1)


def reference(queries, key_rows, value_rows, windows, residual, out_weight, gate_scale):
    width = HEADS * HD
    pads = ((1, 1), (1, 1), (0, 0), (0, 0))
    grid_keys = jnp.pad(key_rows.reshape(TIME_TILES, HEIGHT_TILES, TOK_DEV, width), pads)
    grid_values = jnp.pad(value_rows.reshape(TIME_TILES, HEIGHT_TILES, TOK_DEV, width), pads)
    scale = HD ** -0.5

    def one_place(place):
        time_pos = (place // HEIGHT_TILES).astype(jnp.int32)
        height_pos = (place % HEIGHT_TILES).astype(jnp.int32)
        zero = jnp.zeros((), jnp.int32)
        start = (place * TOK_DEV).astype(jnp.int32)
        query_block = lax.dynamic_slice_in_dim(queries, start, TOK_DEV, 0)
        query_block = query_block.astype(jnp.float32).reshape(TOK_DEV, HEADS, HD)
        window_block = lax.dynamic_slice_in_dim(windows, (place * WT).astype(jnp.int32), WT, 0)
        key_block = lax.dynamic_slice(grid_keys, (time_pos, height_pos, zero, zero), (3, 3, TOK_DEV, width))
        key_block = key_block.reshape(9 * TOK_DEV, HEADS, HD).astype(jnp.float32)
        value_block = lax.dynamic_slice(grid_values, (time_pos, height_pos, zero, zero), (3, 3, TOK_DEV, width))
        value_block = value_block.reshape(9 * TOK_DEV, HEADS, HD).astype(jnp.float32)
        token_mask = build_mask(place, window_block, TIME_TILES, WT, TILE)
        scores = jnp.einsum("qhd,khd->hqk", query_block, key_block) * scale
        scores = jnp.where(token_mask[None], scores, -1e30)
        largest = jnp.max(scores, axis=2, keepdims=True)
        weights = jnp.where(token_mask[None], jnp.exp(scores - largest), 0.0)
        row_total = jnp.sum(weights, axis=2)
        probs = lax.optimization_barrier(weights.astype(jnp.bfloat16)).astype(jnp.float32)
        head_mix = jnp.einsum("hqk,khd->qhd", probs, value_block)
        result = head_mix / jnp.transpose(row_total)[:, :, None]
        return result.astype(jnp.bfloat16).reshape(TOK_DEV, width)

    attention = lax.map(one_place, jnp.arange(N_TILE, dtype=jnp.int32)).reshape(TOKENS, width)
    group_rows = width // N_HEAD
    projected = jnp.zeros((TOKENS, D), jnp.float32)
    for group_index in range(N_HEAD):
        low = group_index * group_rows
        group_term = jnp.dot(attention[:, low:low + group_rows], out_weight[low:low + group_rows], preferred_element_type=jnp.float32)
        rounded = lax.optimization_barrier(group_term.astype(jnp.bfloat16))
        projected = projected + rounded.astype(jnp.float32)
    return (residual.astype(jnp.float32) + gate_scale * projected).astype(jnp.bfloat16)
```

```python
import functools

import jax
import jax.numpy as jnp
from jax import lax
from jax.experimental import pallas as pl
from jax.experimental.pallas import tpu as pltpu
from jax.sharding import PartitionSpec as P

HD = 128
HEIGHT_TILES = 4
SIDE = 16
LOG2E = 1.4426950408889634
MASKED = -1e30
MESH_AXES = ("tile", "head")
VMEM = pltpu.VMEM
SMEM = pltpu.SMEM


def params(megabytes):
    return pltpu.CompilerParams(vmem_limit_bytes=megabytes * 1024 * 1024)


def swap_times(block, first_time):
    tiles = lax.axis_size("tile")
    times = tiles // HEIGHT_TILES
    route = []
    for time in range(first_time, times - 1, 2):
        for height in range(HEIGHT_TILES):
            low, high = time * HEIGHT_TILES + height, (time + 1) * HEIGHT_TILES + height
            route += [(low, high), (high, low)]
    return lax.ppermute(block, "tile", route)


def to_height(block, step):
    tiles = lax.axis_size("tile")
    route = [(i, i + step) for i in range(tiles) if 0 <= i % HEIGHT_TILES + step < HEIGHT_TILES]
    return lax.ppermute(block, "tile", route)


def pack_kernel(windows_ref, q_ref, out_ref):
    rows = q_ref.shape[0]
    out_ref[:rows] = q_ref[...]
    extent = windows_ref[0, 0].astype(jnp.float32)
    out_ref[rows:] = jnp.full((SIDE, q_ref.shape[1]), extent, jnp.float32).astype(out_ref.dtype)


def pack_queries(windows, queries):
    rows, width = queries.shape
    return pl.pallas_call(
        pack_kernel,
        out_shape=jax.ShapeDtypeStruct((rows + SIDE, width), queries.dtype),
        in_specs=[pl.BlockSpec(memory_space=SMEM), pl.BlockSpec(memory_space=VMEM)],
        out_specs=pl.BlockSpec(memory_space=VMEM),
        name="pack_queries",
    )(windows, queries)


def column(values, index):
    return values[:, index : index + 1]


def scores_kernel(windows_ref, q_ref, above_ref, below_ref, k0_ref, k1_ref, k2_ref, probs_ref, stats_ref):
    rows = q_ref.shape[0]
    time = lax.axis_index("tile") // HEIGHT_TILES
    times = lax.axis_size("tile") // HEIGHT_TILES
    has_first = jnp.where((time > 0) & (time < times - 1), 0.0, MASKED)
    own = jnp.where(windows_ref[0, 0] >= 1, 0.0, MASKED)
    sides = [own] + [
        jnp.where(jnp.max(ref[rows:].astype(jnp.float32)) > 0.5, 0.0, MASKED) for ref in (above_ref, below_ref)
    ]
    keys = [k0_ref[...], k1_ref[...], k2_ref[...]]
    scale = HD**-0.5 * LOG2E
    lane = lax.broadcasted_iota(jnp.int32, (rows, HD), 1)
    stats = jnp.zeros((rows, HD), jnp.float32)
    for place, ref in enumerate((q_ref, above_ref, below_ref)):
        block = ref[:rows]
        parts = []
        for key, bias in zip(keys, (None, sides[place] + has_first, sides[place])):
            part = lax.dot_general(block, key, (((1,), (1,)), ((), ())), preferred_element_type=jnp.float32) * scale
            parts.append(part if bias is None else part + bias)
        largest = jnp.max(jnp.maximum(jnp.maximum(parts[0], parts[1]), parts[2]), axis=1, keepdims=True)
        weights = [jnp.exp2(part - largest) for part in parts]
        total = jnp.sum(weights[0] + weights[1] + weights[2], axis=1, keepdims=True)
        for index, weight in enumerate(weights):
            probs_ref[place, :, index * rows : (index + 1) * rows] = weight.astype(probs_ref.dtype)
        stats = jnp.where(lane == 2 * place, largest, stats)
        stats = jnp.where(lane == 2 * place + 1, total, stats)
    stats_ref[0] = stats


def scores(windows, queries, above, below, key_rows, keys_first, keys_second):
    rows, width = queries.shape
    heads = width // HD
    own = pl.BlockSpec((rows, HD), lambda head: (0, head))
    sent = pl.BlockSpec((rows + SIDE, HD), lambda head: (0, head))
    return pl.pallas_call(
        scores_kernel,
        grid=(heads,),
        out_shape=(
            jax.ShapeDtypeStruct((3 * heads, rows, 3 * rows), jnp.bfloat16),
            jax.ShapeDtypeStruct((heads, rows, HD), jnp.float32),
        ),
        in_specs=[pl.BlockSpec(memory_space=SMEM), own, sent, sent, own, own, own],
        out_specs=(
            pl.BlockSpec((3, rows, 3 * rows), lambda head: (head, 0, 0)),
            pl.BlockSpec((1, rows, HD), lambda head: (head, 0, 0)),
        ),
        compiler_params=params(24),
        cost_estimate=pl.CostEstimate(flops=2 * 9 * heads * rows * rows * HD, bytes_accessed=6_000_000, transcendentals=9 * heads * rows * rows),
        name="scores",
    )(windows, queries, above, below, key_rows, keys_first, keys_second)


def split_float(value):
    high = value.astype(jnp.bfloat16).astype(jnp.float32)
    rest = value - high
    middle = rest.astype(jnp.bfloat16).astype(jnp.float32)
    return high, middle, (rest - middle).astype(jnp.bfloat16).astype(jnp.float32)


def mix_kernel(probs_ref, stats_ref, v0_ref, v1_ref, v2_ref, own_ref, above_ref, below_ref):
    rows = v0_ref.shape[0]
    stats = stats_ref[0]
    lane = lax.broadcasted_iota(jnp.int32, (rows, HD), 1)
    for place, ref in enumerate((own_ref, above_ref, below_ref)):
        mix = jnp.zeros((rows, HD), jnp.float32)
        for index, value_ref in enumerate((v0_ref, v1_ref, v2_ref)):
            mix += jnp.dot(
                probs_ref[place, :, index * rows : (index + 1) * rows],
                value_ref[...],
                preferred_element_type=jnp.float32,
            )
        if place == 0:
            ref[...] = mix
            continue
        total = column(stats, 2 * place + 1)
        ref[:rows] = (mix / total).astype(ref.dtype)
        side = jnp.zeros((rows, HD), jnp.float32)
        pieces = split_float(column(stats, 2 * place)) + split_float(total)
        for index, piece in enumerate(pieces):
            side = jnp.where(lane == index, piece, side)
        side = jnp.transpose(side)
        ref[rows : rows + 8] = side[:8, :HD].astype(ref.dtype)
        ref[rows + 8 :] = side[:8, HD:].astype(ref.dtype)


def mix(probs, stats, value_rows, values_first, values_second):
    rows, width = value_rows.shape
    heads = width // HD
    own = pl.BlockSpec((rows, HD), lambda head: (0, head))
    sent = pl.BlockSpec((rows + SIDE, HD), lambda head: (0, head))
    return pl.pallas_call(
        mix_kernel,
        grid=(heads,),
        out_shape=(
            jax.ShapeDtypeStruct((rows, width), jnp.float32),
            jax.ShapeDtypeStruct((rows + SIDE, width), jnp.bfloat16),
            jax.ShapeDtypeStruct((rows + SIDE, width), jnp.bfloat16),
        ),
        in_specs=[
            pl.BlockSpec((3, rows, 3 * rows), lambda head: (head, 0, 0)),
            pl.BlockSpec((1, rows, HD), lambda head: (head, 0, 0)),
            own,
            own,
            own,
        ],
        out_specs=(own, sent, sent),
        compiler_params=params(24),
        cost_estimate=pl.CostEstimate(flops=2 * 9 * heads * rows * rows * HD, bytes_accessed=6_000_000, transcendentals=0),
        name="mix",
    )(probs, stats, value_rows, values_first, values_second)


def project_kernel(windows_ref, own_ref, stats_ref, above_ref, below_ref, weight_ref, out_ref, attention_ref):
    rows, width = own_ref.shape

    @pl.when(pl.program_id(0) == 0)
    def merge():
        height = lax.axis_index("tile") % HEIGHT_TILES
        wide = windows_ref[0, 1] >= 1
        valid = (wide & (height > 0), wide & (height < HEIGHT_TILES - 1))
        for head in range(width // HD):
            low = head * HD
            stats = stats_ref[head]
            largest, total = [column(stats, 0)], [column(stats, 1)]
            for ref, flag in zip((above_ref, below_ref), valid):
                side = ref[rows:, low : low + HD].astype(jnp.float32)
                side = jnp.concatenate([jnp.transpose(side[:8]), jnp.transpose(side[8:])], axis=0)
                peak = column(side, 0) + column(side, 1) + column(side, 2)
                count = column(side, 3) + column(side, 4) + column(side, 5)
                largest.append(jnp.where(flag, peak, MASKED))
                total.append(jnp.where(flag, count, 0.0))
            peak = jnp.maximum(jnp.maximum(largest[0], largest[1]), largest[2])
            shrink = jnp.exp2(largest[0] - peak)
            shares = [total[i] * jnp.exp2(largest[i] - peak) for i in (1, 2)]
            merged = own_ref[:, low : low + HD] * shrink
            for share, ref in zip(shares, (above_ref, below_ref)):
                merged += ref[:rows, low : low + HD].astype(jnp.float32) * share
            merged = merged / (total[0] * shrink + shares[0] + shares[1])
            attention_ref[:, low : low + HD] = merged.astype(jnp.bfloat16)

    out_ref[0] = jnp.dot(attention_ref[...], weight_ref[...], preferred_element_type=jnp.float32).astype(out_ref.dtype)


def project(windows, own, stats, above, below, out_weight):
    rows, width = own.shape
    features = out_weight.shape[1]
    groups = features // width
    whole = lambda shape: pl.BlockSpec(shape, lambda group: (0,) * len(shape))
    return pl.pallas_call(
        project_kernel,
        grid=(groups,),
        out_shape=jax.ShapeDtypeStruct((groups, rows, width), jnp.bfloat16),
        in_specs=[
            pl.BlockSpec(memory_space=SMEM),
            whole(own.shape),
            whole(stats.shape),
            whole(above.shape),
            whole(below.shape),
            pl.BlockSpec((width, width), lambda group: (0, group)),
        ],
        out_specs=pl.BlockSpec((1, rows, width), lambda group: (group, 0, 0)),
        scratch_shapes=[pltpu.VMEM((rows, width), jnp.bfloat16)],
        compiler_params=params(24),
        cost_estimate=pl.CostEstimate(flops=2 * rows * width * features, bytes_accessed=5_000_000, transcendentals=0),
        name="project",
    )(windows, own, stats, above, below, out_weight)


def finish_kernel(terms_ref, residual_ref, gate_ref, out_ref):
    total = jnp.sum(terms_ref[...].astype(jnp.float32), axis=0)
    out_ref[...] = (residual_ref[...].astype(jnp.float32) + gate_ref[...] * total).astype(out_ref.dtype)


def finish(terms, residual, gate_scale):
    groups, rows, width = terms.shape
    steps = 2
    part = rows // steps
    return pl.pallas_call(
        finish_kernel,
        grid=(steps,),
        out_shape=jax.ShapeDtypeStruct((rows, width), residual.dtype),
        in_specs=[
            pl.BlockSpec((groups, part, width), lambda step: (0, step, 0)),
            pl.BlockSpec((part, width), lambda step: (step, 0)),
            pl.BlockSpec((1, width), lambda step: (0, 0)),
        ],
        out_specs=pl.BlockSpec((part, width), lambda step: (step, 0)),
        compiler_params=params(24),
        cost_estimate=pl.CostEstimate(flops=10 * groups * rows * width, bytes_accessed=2_000_000, transcendentals=0),
        name="finish",
    )(terms, residual, gate_scale.reshape(1, width))


def shards(queries, key_rows, value_rows, windows, residual, out_weight, gate_scale):
    keys_first, keys_second = swap_times(key_rows, 1), swap_times(key_rows, 0)
    values_first, values_second = swap_times(value_rows, 1), swap_times(value_rows, 0)
    packed = pack_queries(windows, queries)
    from_above, from_below = to_height(packed, 1), to_height(packed, -1)
    probs, stats = scores(windows, queries, from_above, from_below, key_rows, keys_first, keys_second)
    own, for_above, for_below = mix(probs, stats, value_rows, values_first, values_second)
    terms = project(windows, own, stats, to_height(for_below, 1), to_height(for_above, -1), out_weight)
    terms = lax.all_to_all(terms, "head", 0, 0)
    return finish(terms, residual, gate_scale)


def solution(mesh):
    return jax.shard_map(
        shards,
        mesh=mesh,
        in_specs=(
            P("tile", "head"),
            P("tile", "head"),
            P("tile", "head"),
            P("tile", None),
            P("tile", "head"),
            P("head", None),
            P("head"),
        ),
        out_specs=P("tile", "head"),
        check_vma=False,
    )
```

```python
import functools

import jax
import jax.numpy as jnp
from jax import lax
from jax.experimental import pallas as pl
from jax.experimental.pallas import tpu as pltpu
from jax.sharding import PartitionSpec as P

HD = 128
HEIGHT_TILES = 4
SIDE = 16
LOG2E = 1.4426950408889634
MASKED = -1e30
MESH_AXES = ("tile", "head")
VMEM = pltpu.VMEM
SMEM = pltpu.SMEM


def params(megabytes):
    return pltpu.CompilerParams(vmem_limit_bytes=megabytes * 1024 * 1024)


def places():
    tiles = lax.axis_size("tile")
    return [(tile, *divmod(tile, HEIGHT_TILES), tiles // HEIGHT_TILES) for tile in range(tiles)]


def time_partner(time, height, later):
    odd = (height < HEIGHT_TILES // 2) != later
    return time + 1 if time % 2 == int(odd) else time - 1


def swap_times(block, later):
    route = []
    for tile, time, height, times in places():
        partner = time_partner(time, height, later)
        if 0 <= partner < times:
            route.append((tile, partner * HEIGHT_TILES + height))
    return lax.ppermute(block, "tile", route)


def swap_pair(block):
    return lax.ppermute(block, "tile", [(tile, tile ^ 1) for tile, *_ in places()])


def swap_middle(block):
    route = [(tile, tile + (1 if height == 1 else -1)) for tile, _, height, _ in places() if height in (1, 2)]
    return lax.ppermute(block, "tile", route)


def pack_kernel(windows_ref, q_ref, k_ref, packed_ref, key_ref):
    rows = q_ref.shape[0]
    packed_ref[:rows] = q_ref[...]
    extent = windows_ref[0, 0].astype(jnp.float32)
    packed_ref[rows:] = jnp.full((SIDE, q_ref.shape[1]), extent, jnp.float32).astype(packed_ref.dtype)
    key_ref[...] = k_ref[...]


def pack_queries(windows, queries, key_rows):
    rows, width = queries.shape
    whole = pl.BlockSpec(memory_space=VMEM)
    return pl.pallas_call(
        pack_kernel,
        out_shape=(
            jax.ShapeDtypeStruct((rows + SIDE, width), queries.dtype),
            jax.ShapeDtypeStruct((rows, width), queries.dtype),
        ),
        in_specs=[pl.BlockSpec(memory_space=SMEM), whole, whole],
        out_specs=(whole, whole),
        name="pack_queries",
    )(windows, queries, key_rows)


def column(values, index):
    return values[:, index : index + 1]


def scores_kernel(q_ref, pair_ref, middle_ref, k0_ref, k1_ref, k2_ref, probs_ref, stats_ref):
    rows = k0_ref.shape[0]
    tile = lax.axis_index("tile")
    time, height = tile // HEIGHT_TILES, tile % HEIGHT_TILES
    times = lax.axis_size("tile") // HEIGHT_TILES
    inner = (time > 0) & (time < times - 1)
    lower = height < HEIGHT_TILES // 2
    keys = [k0_ref[...], k1_ref[...], k2_ref[...]]
    scale = HD**-0.5 * LOG2E
    lane = lax.broadcasted_iota(jnp.int32, (rows, HD), 1)
    stats = jnp.zeros((rows, HD), jnp.float32)
    for place, ref in enumerate((q_ref, pair_ref, middle_ref)):
        wide = jnp.max(ref[rows:].astype(jnp.float32)) > 0.5
        biases = (0.0, jnp.where(wide & (inner | ~lower), 0.0, MASKED), jnp.where(wide & (inner | lower), 0.0, MASKED))
        block = ref[:rows]
        parts = [
            lax.dot_general(block, key, (((1,), (1,)), ((), ())), preferred_element_type=jnp.float32) for key in keys
        ]
        peaks = [jnp.max(part, axis=1, keepdims=True) * scale + bias for part, bias in zip(parts, biases)]
        largest = jnp.maximum(jnp.maximum(peaks[0], peaks[1]), peaks[2])
        weights = [jnp.exp2(part * scale + (bias - largest)) for part, bias in zip(parts, biases)]
        total = jnp.sum(weights[0] + weights[1] + weights[2], axis=1, keepdims=True)
        for index, weight in enumerate(weights):
            probs_ref[place, :, index * rows : (index + 1) * rows] = weight.astype(probs_ref.dtype)
        stats = jnp.where(lane == 2 * place, largest, stats)
        stats = jnp.where(lane == 2 * place + 1, total, stats)
    stats_ref[0] = stats


def scores(queries, from_pair, from_middle, key_rows, keys_first, keys_second):
    rows, width = key_rows.shape
    heads = width // HD
    own = pl.BlockSpec((rows, HD), lambda head: (0, head))
    sent = pl.BlockSpec((rows + SIDE, HD), lambda head: (0, head))
    return pl.pallas_call(
        scores_kernel,
        grid=(heads,),
        out_shape=(
            jax.ShapeDtypeStruct((3 * heads, rows, 3 * rows), jnp.bfloat16),
            jax.ShapeDtypeStruct((heads, rows, HD), jnp.float32),
        ),
        in_specs=[sent, sent, sent, own, own, own],
        out_specs=(
            pl.BlockSpec((3, rows, 3 * rows), lambda head: (head, 0, 0)),
            pl.BlockSpec((1, rows, HD), lambda head: (head, 0, 0)),
        ),
        compiler_params=params(24),
        cost_estimate=pl.CostEstimate(flops=2 * 9 * heads * rows * rows * HD, bytes_accessed=6_000_000, transcendentals=9 * heads * rows * rows),
        name="scores",
    )(queries, from_pair, from_middle, key_rows, keys_first, keys_second)


def split_float(value):
    high = value.astype(jnp.bfloat16).astype(jnp.float32)
    rest = value - high
    middle = rest.astype(jnp.bfloat16).astype(jnp.float32)
    return high, middle, (rest - middle).astype(jnp.bfloat16).astype(jnp.float32)


def mix_kernel(probs_ref, stats_ref, v0_ref, v1_ref, v2_ref, own_ref, own_stats_ref, pair_ref, middle_ref):
    rows = v0_ref.shape[0]
    stats = jnp.transpose(stats_ref[0])[:8]
    own_stats_ref[0] = stats
    line = lax.broadcasted_iota(jnp.int32, (8, rows), 0)
    for place, ref in enumerate((own_ref, pair_ref, middle_ref)):
        mix = jnp.zeros((rows, HD), jnp.float32)
        for index, value_ref in enumerate((v0_ref, v1_ref, v2_ref)):
            mix += jnp.dot(
                probs_ref[place, :, index * rows : (index + 1) * rows],
                value_ref[...],
                preferred_element_type=jnp.float32,
            )
        if place == 0:
            ref[...] = mix
            continue
        ref[:rows] = mix.astype(ref.dtype)
        side = jnp.zeros((8, rows), jnp.float32)
        pieces = split_float(stats[2 * place : 2 * place + 1]) + split_float(stats[2 * place + 1 : 2 * place + 2])
        for index, piece in enumerate(pieces):
            side = jnp.where(line == index, piece, side)
        ref[rows:] = jnp.concatenate([side[:, :HD], side[:, HD:]], axis=0).astype(ref.dtype)


def mix(probs, stats, value_rows, values_first, values_second):
    rows, width = value_rows.shape
    heads = width // HD
    own = pl.BlockSpec((rows, HD), lambda head: (0, head))
    sent = pl.BlockSpec((rows + SIDE, HD), lambda head: (0, head))
    return pl.pallas_call(
        mix_kernel,
        grid=(heads,),
        out_shape=(
            jax.ShapeDtypeStruct((rows, width), jnp.float32),
            jax.ShapeDtypeStruct((heads, 8, rows), jnp.float32),
            jax.ShapeDtypeStruct((rows + SIDE, width), jnp.bfloat16),
            jax.ShapeDtypeStruct((rows + SIDE, width), jnp.bfloat16),
        ),
        in_specs=[
            pl.BlockSpec((3, rows, 3 * rows), lambda head: (head, 0, 0)),
            pl.BlockSpec((1, rows, HD), lambda head: (head, 0, 0)),
            own,
            own,
            own,
        ],
        out_specs=(own, pl.BlockSpec((1, 8, rows), lambda head: (head, 0, 0)), sent, sent),
        compiler_params=params(24),
        cost_estimate=pl.CostEstimate(flops=2 * 9 * heads * rows * rows * HD, bytes_accessed=6_000_000, transcendentals=0),
        name="mix",
    )(probs, stats, value_rows, values_first, values_second)


def merge_shares(windows_ref, stats_ref, pair_ref, middle_ref, rows, heads):
    height = lax.axis_index("tile") % HEIGHT_TILES
    wide = windows_ref[0, 1] >= 1
    valid = (wide, wide & (height > 0) & (height < HEIGHT_TILES - 1))
    line = lax.broadcasted_iota(jnp.int32, (16, rows), 0)
    shares = jnp.zeros((16, rows), jnp.float32)
    for head in range(heads):
        low = head * HD
        stats = stats_ref[head]
        largest, total = [stats[0:1]], [stats[1:2]]
        for ref, flag in zip((pair_ref, middle_ref), valid):
            side = ref[rows:, low : low + HD].astype(jnp.float32)
            side = jnp.concatenate([side[:8], side[8:]], axis=1)
            largest.append(jnp.where(flag, side[0:1] + side[1:2] + side[2:3], MASKED))
            total.append(jnp.where(flag, side[3:4] + side[4:5] + side[5:6], 0.0))
        peak = jnp.maximum(jnp.maximum(largest[0], largest[1]), largest[2])
        factors = [jnp.exp2(value - peak) for value in largest]
        whole = total[0] * factors[0] + total[1] * factors[1] + total[2] * factors[2]
        for index, factor in enumerate(factors):
            shares = jnp.where(line == 3 * head + index, factor / whole, shares)
    return jnp.transpose(shares)


def project_kernel(windows_ref, own_ref, stats_ref, pair_ref, middle_ref, weight_ref, out_ref):
    rows, width = own_ref.shape
    heads = width // HD
    shares = merge_shares(windows_ref, stats_ref, pair_ref, middle_ref, rows, heads)
    merged = []
    for head in range(heads):
        low = head * HD
        value = own_ref[:, low : low + HD] * column(shares, 3 * head)
        for index, ref in enumerate((pair_ref, middle_ref)):
            value += ref[:rows, low : low + HD].astype(jnp.float32) * column(shares, 3 * head + 1 + index)
        merged.append(value.astype(jnp.bfloat16))
    attention = jnp.concatenate(merged, axis=1)
    for group in range(out_ref.shape[0]):
        out_ref[group] = jnp.dot(
            attention, weight_ref[:, group * width : (group + 1) * width], preferred_element_type=jnp.float32
        ).astype(out_ref.dtype)


def project(windows, own, stats, pair, middle, out_weight):
    rows, width = own.shape
    features = out_weight.shape[1]
    whole = pl.BlockSpec(memory_space=VMEM)
    return pl.pallas_call(
        project_kernel,
        out_shape=jax.ShapeDtypeStruct((features // width, rows, width), jnp.bfloat16),
        in_specs=[pl.BlockSpec(memory_space=SMEM)] + [whole] * 5,
        out_specs=whole,
        compiler_params=params(24),
        cost_estimate=pl.CostEstimate(flops=2 * rows * width * features, bytes_accessed=5_000_000, transcendentals=0),
        name="project",
    )(windows, own, stats, pair, middle, out_weight)


def finish_kernel(terms_ref, residual_ref, gate_ref, out_ref):
    total = jnp.sum(terms_ref[...].astype(jnp.float32), axis=0)
    out_ref[...] = (residual_ref[...].astype(jnp.float32) + gate_ref[...] * total).astype(out_ref.dtype)


def finish(terms, residual, gate_scale):
    groups, rows, width = terms.shape
    steps = 2
    part = rows // steps
    return pl.pallas_call(
        finish_kernel,
        grid=(steps,),
        out_shape=jax.ShapeDtypeStruct((rows, width), residual.dtype),
        in_specs=[
            pl.BlockSpec((groups, part, width), lambda step: (0, step, 0)),
            pl.BlockSpec((part, width), lambda step: (step, 0)),
            pl.BlockSpec((1, width), lambda step: (0, 0)),
        ],
        out_specs=pl.BlockSpec((part, width), lambda step: (step, 0)),
        compiler_params=params(24),
        cost_estimate=pl.CostEstimate(flops=10 * groups * rows * width, bytes_accessed=2_000_000, transcendentals=0),
        name="finish",
    )(terms, residual, gate_scale.reshape(1, width))


def shards(queries, key_rows, value_rows, windows, residual, out_weight, gate_scale):
    keys_first, keys_second = swap_times(key_rows, False), swap_times(key_rows, True)
    values_first, values_second = swap_times(value_rows, False), swap_times(value_rows, True)
    packed, keys = pack_queries(windows, queries, key_rows)
    probs, stats = scores(packed, swap_pair(packed), swap_middle(packed), keys, keys_first, keys_second)
    own, stats, for_pair, for_middle = mix(probs, stats, value_rows, values_first, values_second)
    terms = project(windows, own, stats, swap_pair(for_pair), swap_middle(for_middle), out_weight)
    terms = lax.all_to_all(terms, "head", 0, 0)
    return finish(terms, residual, gate_scale)


def solution(mesh):
    return jax.shard_map(
        shards,
        mesh=mesh,
        in_specs=(
            P("tile", "head"),
            P("tile", "head"),
            P("tile", "head"),
            P("tile", None),
            P("tile", "head"),
            P("head", None),
            P("head"),
        ),
        out_specs=P("tile", "head"),
        check_vma=False,
    )
```

```python
import functools

import jax
import jax.numpy as jnp
from jax import lax
from jax.experimental import pallas as pl
from jax.experimental.pallas import tpu as pltpu
from jax.sharding import PartitionSpec as P

HD = 128
HEIGHT_TILES = 4
SIDE = 16
LOG2E = 1.4426950408889634
MASKED = -1e30
MESH_AXES = ("tile", "head")
VMEM = pltpu.VMEM
SMEM = pltpu.SMEM


def params(megabytes):
    return pltpu.CompilerParams(vmem_limit_bytes=megabytes * 1024 * 1024)


def places():
    tiles = lax.axis_size("tile")
    return [(tile, *divmod(tile, HEIGHT_TILES), tiles // HEIGHT_TILES) for tile in range(tiles)]


def time_partner(time, height, later):
    odd = (height < HEIGHT_TILES // 2) != later
    return time + 1 if time % 2 == int(odd) else time - 1


def swap_times(block, later):
    route = []
    for tile, time, height, times in places():
        partner = time_partner(time, height, later)
        if 0 <= partner < times:
            route.append((tile, partner * HEIGHT_TILES + height))
    return lax.ppermute(block, "tile", route)


def swap_pair(block):
    return lax.ppermute(block, "tile", [(tile, tile ^ 1) for tile, *_ in places()])


def swap_middle(block):
    route = [(tile, tile + (1 if height == 1 else -1)) for tile, _, height, _ in places() if height in (1, 2)]
    return lax.ppermute(block, "tile", route)


def pack_kernel(windows_ref, q_ref, k_ref, v_ref, packed_ref, block_ref):
    rows = q_ref.shape[0]
    block_ref[:rows] = k_ref[...]
    block_ref[rows:] = v_ref[...]
    packed_ref[:rows] = q_ref[...]
    extent = windows_ref[0, 0].astype(jnp.float32)
    packed_ref[rows:] = jnp.full((SIDE, q_ref.shape[1]), extent, jnp.float32).astype(packed_ref.dtype)


def pack(windows, queries, key_rows, value_rows):
    rows, width = queries.shape
    whole = pl.BlockSpec(memory_space=VMEM)
    return pl.pallas_call(
        pack_kernel,
        out_shape=(
            jax.ShapeDtypeStruct((rows + SIDE, width), queries.dtype),
            jax.ShapeDtypeStruct((2 * rows, width), queries.dtype),
        ),
        in_specs=[pl.BlockSpec(memory_space=SMEM)] + [whole] * 3,
        out_specs=(whole, whole),
        name="pack",
    )(windows, queries, key_rows, value_rows)


def column(values, index):
    return values[:, index : index + 1]


def split_float(value):
    high = value.astype(jnp.bfloat16).astype(jnp.float32)
    rest = value - high
    middle = rest.astype(jnp.bfloat16).astype(jnp.float32)
    return high, middle, (rest - middle).astype(jnp.bfloat16).astype(jnp.float32)


def attend_kernel(stage, *refs):
    query_refs, block_ref, refs = refs[:3], refs[3], refs[4:]
    if stage > 0:
        old_mix_ref, old_stats_ref = refs[:2]
        refs = refs[2:]
    rows, width = block_ref.shape[0] // 2, block_ref.shape[1]
    tile = lax.axis_index("tile")
    time, height = tile // HEIGHT_TILES, tile % HEIGHT_TILES
    inner = (time > 0) & (time < lax.axis_size("tile") // HEIGHT_TILES - 1)
    lower = height < HEIGHT_TILES // 2
    present = (None, inner | ~lower, inner | lower)[stage]
    scale = HD**-0.5 * LOG2E
    line = lax.broadcasted_iota(jnp.int32, (8, rows), 0)
    lane = lax.broadcasted_iota(jnp.int32, (rows, HD), 1)
    spread = lambda value: jnp.broadcast_to(value, (rows, HD))
    if stage > 0:
        biases = []
        for ref in query_refs:
            wide = jnp.max(ref[rows:].astype(jnp.float32)) > 0.5
            biases.append(jnp.where(wide & present, 0.0, MASKED))
    for head in range(width // HD):
        low = head * HD
        keys, values = block_ref[:rows, low : low + HD], block_ref[rows:, low : low + HD]
        stats = jnp.zeros((rows, HD), jnp.float32)
        for place, ref in enumerate(query_refs):
            part = lax.dot_general(
                ref[:rows, low : low + HD], keys, (((1,), (1,)), ((), ())), preferred_element_type=jnp.float32
            )
            largest = spread(jnp.max(part, axis=1, keepdims=True)) * scale
            bias = 0.0
            index = 3 * head + place
            if stage > 0:
                bias = biases[place]
                largest = jnp.maximum(largest + bias, old_stats_ref[2 * index])
            offset = jnp.concatenate([bias - largest] * (rows // HD), axis=1)
            weights = jnp.exp2(part * scale + offset)
            total = spread(jnp.sum(weights, axis=1, keepdims=True))
            mix = jnp.dot(weights.astype(values.dtype), values, preferred_element_type=jnp.float32)
            if stage > 0:
                shrink = jnp.exp2(old_stats_ref[2 * index] - largest)
                total += old_stats_ref[2 * index + 1] * shrink
                mix += old_mix_ref[index] * shrink
            if stage < 2:
                refs[0][index] = mix
                refs[1][2 * index] = largest
                refs[1][2 * index + 1] = total
                continue
            stats = jnp.where(lane == 2 * place, largest, stats)
            stats = jnp.where(lane == 2 * place + 1, total, stats)
            if place == 0:
                refs[0][:, low : low + HD] = mix
            else:
                refs[1 + place][:rows, low : low + HD] = mix.astype(refs[1 + place].dtype)
        if stage < 2:
            continue
        stats = jnp.transpose(stats)[:8]
        refs[1][head] = stats
        for place in (1, 2):
            side = jnp.zeros((8, rows), jnp.float32)
            pieces = split_float(stats[2 * place : 2 * place + 1]) + split_float(stats[2 * place + 1 : 2 * place + 2])
            for index, piece in enumerate(pieces):
                side = jnp.where(line == index, piece, side)
            side = jnp.concatenate([side[:, :HD], side[:, HD:]], axis=0)
            refs[1 + place][rows:, low : low + HD] = side.astype(refs[1 + place].dtype)


def attend(stage, queries, block, before=()):
    rows, width = block.shape[0] // 2, block.shape[1]
    heads = width // HD
    whole = pl.BlockSpec(memory_space=VMEM)
    if stage < 2:
        out_shape = (
            jax.ShapeDtypeStruct((3 * heads, rows, HD), jnp.float32),
            jax.ShapeDtypeStruct((6 * heads, rows, HD), jnp.float32),
        )
    else:
        out_shape = (
            jax.ShapeDtypeStruct((rows, width), jnp.float32),
            jax.ShapeDtypeStruct((heads, 8, rows), jnp.float32),
            jax.ShapeDtypeStruct((rows + SIDE, width), jnp.bfloat16),
            jax.ShapeDtypeStruct((rows + SIDE, width), jnp.bfloat16),
        )
    return pl.pallas_call(
        functools.partial(attend_kernel, stage),
        out_shape=out_shape,
        in_specs=[whole] * (4 + len(before)),
        out_specs=(whole,) * len(out_shape),
        compiler_params=params(24),
        cost_estimate=pl.CostEstimate(flops=12 * heads * rows * rows * HD, bytes_accessed=2_000_000, transcendentals=3 * heads * rows * rows),
        name=("attend_own", "attend_first", "attend_second")[stage],
    )(*queries, block, *before)


def merge_shares(windows_ref, stats_ref, pair_ref, middle_ref, rows, heads):
    height = lax.axis_index("tile") % HEIGHT_TILES
    wide = windows_ref[0, 1] >= 1
    valid = (wide, wide & (height > 0) & (height < HEIGHT_TILES - 1))
    line = lax.broadcasted_iota(jnp.int32, (16, rows), 0)
    shares = jnp.zeros((16, rows), jnp.float32)
    for head in range(heads):
        low = head * HD
        stats = stats_ref[head]
        largest, total = [stats[0:1]], [stats[1:2]]
        for ref, flag in zip((pair_ref, middle_ref), valid):
            side = ref[rows:, low : low + HD].astype(jnp.float32)
            side = jnp.concatenate([side[:8], side[8:]], axis=1)
            largest.append(jnp.where(flag, side[0:1] + side[1:2] + side[2:3], MASKED))
            total.append(jnp.where(flag, side[3:4] + side[4:5] + side[5:6], 0.0))
        peak = jnp.maximum(jnp.maximum(largest[0], largest[1]), largest[2])
        factors = [jnp.exp2(value - peak) for value in largest]
        whole = total[0] * factors[0] + total[1] * factors[1] + total[2] * factors[2]
        for index, factor in enumerate(factors):
            shares = jnp.where(line == 3 * head + index, factor / whole, shares)
    return jnp.transpose(shares)


def project_kernel(windows_ref, own_ref, stats_ref, pair_ref, middle_ref, weight_ref, out_ref):
    rows, width = own_ref.shape
    heads = width // HD
    shares = merge_shares(windows_ref, stats_ref, pair_ref, middle_ref, rows, heads)
    merged = []
    for head in range(heads):
        low = head * HD
        value = own_ref[:, low : low + HD] * column(shares, 3 * head)
        for index, ref in enumerate((pair_ref, middle_ref)):
            value += ref[:rows, low : low + HD].astype(jnp.float32) * column(shares, 3 * head + 1 + index)
        merged.append(value.astype(jnp.bfloat16))
    attention = jnp.concatenate(merged, axis=1)
    for group in range(out_ref.shape[0]):
        out_ref[group] = jnp.dot(
            attention, weight_ref[:, group * width : (group + 1) * width], preferred_element_type=jnp.float32
        ).astype(out_ref.dtype)


def project(windows, own, stats, pair, middle, out_weight):
    rows, width = own.shape
    features = out_weight.shape[1]
    whole = pl.BlockSpec(memory_space=VMEM)
    return pl.pallas_call(
        project_kernel,
        out_shape=jax.ShapeDtypeStruct((features // width, rows, width), jnp.bfloat16),
        in_specs=[pl.BlockSpec(memory_space=SMEM)] + [whole] * 5,
        out_specs=whole,
        compiler_params=params(24),
        cost_estimate=pl.CostEstimate(flops=2 * rows * width * features, bytes_accessed=5_000_000, transcendentals=0),
        name="project",
    )(windows, own, stats, pair, middle, out_weight)


def finish_kernel(terms_ref, residual_ref, gate_ref, out_ref):
    total = jnp.sum(terms_ref[...].astype(jnp.float32), axis=0)
    out_ref[...] = (residual_ref[...].astype(jnp.float32) + gate_ref[...] * total).astype(out_ref.dtype)


def finish(terms, residual, gate_scale):
    groups, rows, width = terms.shape
    steps = 2
    part = rows // steps
    return pl.pallas_call(
        finish_kernel,
        grid=(steps,),
        out_shape=jax.ShapeDtypeStruct((rows, width), residual.dtype),
        in_specs=[
            pl.BlockSpec((groups, part, width), lambda step: (0, step, 0)),
            pl.BlockSpec((part, width), lambda step: (step, 0)),
            pl.BlockSpec((1, width), lambda step: (0, 0)),
        ],
        out_specs=pl.BlockSpec((part, width), lambda step: (step, 0)),
        compiler_params=params(24),
        cost_estimate=pl.CostEstimate(flops=10 * groups * rows * width, bytes_accessed=2_000_000, transcendentals=0),
        name="finish",
    )(terms, residual, gate_scale.reshape(1, width))


def shards(queries, key_rows, value_rows, windows, residual, out_weight, gate_scale):
    packed, block = pack(windows, queries, key_rows, value_rows)
    first, second = swap_times(block, False), swap_times(block, True)
    asked = (packed, swap_pair(packed), swap_middle(packed))
    before = attend(0, asked, block)
    before = attend(1, asked, first, before)
    own, stats, for_pair, for_middle = attend(2, asked, second, before)
    terms = project(windows, own, stats, swap_pair(for_pair), swap_middle(for_middle), out_weight)
    terms = lax.all_to_all(terms, "head", 0, 0)
    return finish(terms, residual, gate_scale)


def solution(mesh):
    return jax.shard_map(
        shards,
        mesh=mesh,
        in_specs=(
            P("tile", "head"),
            P("tile", "head"),
            P("tile", "head"),
            P("tile", None),
            P("tile", "head"),
            P("head", None),
            P("head"),
        ),
        out_specs=P("tile", "head"),
        check_vma=False,
    )
```

```python
import functools

import jax
import jax.numpy as jnp
from jax import lax
from jax.experimental import pallas as pl
from jax.experimental.pallas import tpu as pltpu
from jax.sharding import PartitionSpec as P

HD = 128
HEIGHT_TILES = 4
SIDE = 16
LOG2E = 1.4426950408889634
MASKED = -1e30
MESH_AXES = ("tile", "head")
VMEM = pltpu.VMEM
SMEM = pltpu.SMEM


def params(megabytes):
    return pltpu.CompilerParams(vmem_limit_bytes=megabytes * 1024 * 1024)


def places():
    tiles = lax.axis_size("tile")
    return [(tile, *divmod(tile, HEIGHT_TILES), tiles // HEIGHT_TILES) for tile in range(tiles)]


def time_partner(time, height, later):
    odd = (height < HEIGHT_TILES // 2) != later
    return time + 1 if time % 2 == int(odd) else time - 1


def swap_times(block, later):
    route = []
    for tile, time, height, times in places():
        partner = time_partner(time, height, later)
        if 0 <= partner < times:
            route.append((tile, partner * HEIGHT_TILES + height))
    return lax.ppermute(block, "tile", route)


def swap_pair(block):
    return lax.ppermute(block, "tile", [(tile, tile ^ 1) for tile, *_ in places()])


def swap_middle(block):
    route = [(tile, tile + (1 if height == 1 else -1)) for tile, _, height, _ in places() if height in (1, 2)]
    return lax.ppermute(block, "tile", route)


def pack_kernel(windows_ref, q_ref, k_ref, v_ref, packed_ref, block_ref):
    rows = q_ref.shape[0]
    block_ref[:rows] = k_ref[...]
    block_ref[rows:] = v_ref[...]
    packed_ref[:rows] = q_ref[...]
    extent = windows_ref[0, 0].astype(jnp.float32)
    packed_ref[rows:] = jnp.full((SIDE, q_ref.shape[1]), extent, jnp.float32).astype(packed_ref.dtype)


def pack(windows, queries, key_rows, value_rows):
    rows, width = queries.shape
    whole = pl.BlockSpec(memory_space=VMEM)
    return pl.pallas_call(
        pack_kernel,
        out_shape=(
            jax.ShapeDtypeStruct((rows + SIDE, width), queries.dtype),
            jax.ShapeDtypeStruct((2 * rows, width), queries.dtype),
        ),
        in_specs=[pl.BlockSpec(memory_space=SMEM)] + [whole] * 3,
        out_specs=(whole, whole),
        name="pack",
    )(windows, queries, key_rows, value_rows)


def column(values, index):
    return values[:, index : index + 1]


def split_float(value):
    high = value.astype(jnp.bfloat16).astype(jnp.float32)
    rest = value - high
    middle = rest.astype(jnp.bfloat16).astype(jnp.float32)
    return high, middle, (rest - middle).astype(jnp.bfloat16).astype(jnp.float32)


def wide_window(ref, rows):
    return jnp.max(ref[rows:].astype(jnp.float32)) > 0.5


def presence():
    tile = lax.axis_index("tile")
    time, height = tile // HEIGHT_TILES, tile % HEIGHT_TILES
    inner = (time > 0) & (time < lax.axis_size("tile") // HEIGHT_TILES - 1)
    lower = height < HEIGHT_TILES // 2
    return inner | ~lower, inner | lower


def raw_scores(query, keys):
    return lax.dot_general(query, keys, (((1,), (1,)), ((), ())), preferred_element_type=jnp.float32)


def put_message(ref, head, mix, stats, row):
    rows = mix.shape[0]
    low = head * HD
    line = lax.broadcasted_iota(jnp.int32, (8, rows), 0)
    ref[:rows, low : low + HD] = mix.astype(ref.dtype)
    side = jnp.zeros((8, rows), jnp.float32)
    for index, piece in enumerate(split_float(stats[row : row + 1]) + split_float(stats[row + 1 : row + 2])):
        side = jnp.where(line == index, piece, side)
    ref[rows:, low : low + HD] = jnp.concatenate([side[:, :HD], side[:, HD:]], axis=0).astype(ref.dtype)


def attend_kernel(stage, places, *refs):
    query_refs, block_ref, refs = refs[:2], refs[2], refs[3:]
    if stage > 0:
        old_mix_ref, old_stats_ref = refs[:2]
        refs = refs[2:]
    rows, width = block_ref.shape[0] // 2, block_ref.shape[1]
    scale = HD**-0.5 * LOG2E
    lane = lax.broadcasted_iota(jnp.int32, (rows, HD), 1)
    spread = lambda value: jnp.broadcast_to(value, (rows, HD))
    for place in places:
        ref = query_refs[place]
        bias = 0.0
        if stage > 0:
            bias = jnp.where(wide_window(ref, rows) & presence()[stage - 1], 0.0, MASKED)
        for head in range(width // HD):
            low = head * HD
            keys, values = block_ref[:rows, low : low + HD], block_ref[rows:, low : low + HD]
            part = raw_scores(ref[:rows, low : low + HD], keys)
            largest = spread(jnp.max(part, axis=1, keepdims=True)) * scale
            index = 2 * head + place
            if stage > 0:
                largest = jnp.maximum(largest + bias, old_stats_ref[2 * index])
            offset = jnp.concatenate([bias - largest] * (rows // HD), axis=1)
            weights = jnp.exp2(part * scale + offset)
            total = spread(jnp.sum(weights, axis=1, keepdims=True))
            mix = jnp.dot(weights.astype(values.dtype), values, preferred_element_type=jnp.float32)
            if stage > 0:
                shrink = jnp.exp2(old_stats_ref[2 * index] - largest)
                total += old_stats_ref[2 * index + 1] * shrink
                mix += old_mix_ref[index] * shrink
            if stage < 2:
                refs[0][index] = mix
                refs[1][2 * index] = largest
                refs[1][2 * index + 1] = total
                continue
            stats = jnp.transpose(jnp.where(lane == 0, largest, jnp.where(lane == 1, total, 0.0)))[:8]
            if place == 0:
                refs[0][:, low : low + HD] = mix
                refs[1][head] = stats
            else:
                put_message(refs[0], head, mix, stats, 0)


def attend(stage, queries, block, before=(), places=(0, 1)):
    rows, width = block.shape[0] // 2, block.shape[1]
    heads = width // HD
    whole = pl.BlockSpec(memory_space=VMEM)
    if stage < 2:
        out_shape = (
            jax.ShapeDtypeStruct((2 * heads, rows, HD), jnp.float32),
            jax.ShapeDtypeStruct((4 * heads, rows, HD), jnp.float32),
        )
    elif places == (0,):
        out_shape = (
            jax.ShapeDtypeStruct((rows, width), jnp.float32),
            jax.ShapeDtypeStruct((heads, 8, rows), jnp.float32),
        )
    else:
        out_shape = (jax.ShapeDtypeStruct((rows + SIDE, width), jnp.bfloat16),)
    cost = len(places) * heads * rows * rows
    return pl.pallas_call(
        functools.partial(attend_kernel, stage, places),
        out_shape=out_shape,
        in_specs=[whole] * (3 + len(before)),
        out_specs=(whole,) * len(out_shape),
        compiler_params=params(24),
        cost_estimate=pl.CostEstimate(flops=4 * HD * cost, bytes_accessed=2_000_000, transcendentals=cost),
        name=("attend_own", "attend_first", "attend_second")[stage] + "_".join(map(str, places)),
    )(*queries, block, *before)


def gate_kernel(in_ref, out_ref):
    pass


def gate(array):
    anywhere = pl.BlockSpec(memory_space=pl.ANY)
    return pl.pallas_call(
        gate_kernel,
        out_shape=jax.ShapeDtypeStruct(array.shape, array.dtype),
        in_specs=[anywhere],
        out_specs=anywhere,
        input_output_aliases={0: 0},
        cost_estimate=pl.CostEstimate(flops=20_000_000_000, bytes_accessed=0, transcendentals=0),
        name="gate",
    )(array)


def middle_kernel(query_ref, own_ref, first_ref, second_ref, after_ref, out_ref):
    rows, width = own_ref.shape[0] // 2, own_ref.shape[1]
    scale = HD**-0.5 * LOG2E
    lane = lax.broadcasted_iota(jnp.int32, (rows, HD), 1)
    wide = wide_window(query_ref, rows)
    biases = [0.0] + [jnp.where(wide & present, 0.0, MASKED) for present in presence()]
    for head in range(width // HD):
        low = head * HD
        query = query_ref[:rows, low : low + HD]
        parts = [raw_scores(query, ref[:rows, low : low + HD]) for ref in (own_ref, first_ref, second_ref)]
        peaks = [jnp.max(part, axis=1, keepdims=True) * scale + bias for part, bias in zip(parts, biases)]
        largest = jnp.maximum(jnp.maximum(peaks[0], peaks[1]), peaks[2])
        weights = [jnp.exp2(part * scale + (bias - largest)) for part, bias in zip(parts, biases)]
        total = jnp.sum(weights[0] + weights[1] + weights[2], axis=1, keepdims=True)
        mix = jnp.zeros((rows, HD), jnp.float32)
        for weight, ref in zip(weights, (own_ref, first_ref, second_ref)):
            mix += jnp.dot(weight.astype(ref.dtype), ref[rows:, low : low + HD], preferred_element_type=jnp.float32)
        stats = jnp.where(lane == 0, largest, jnp.where(lane == 1, total, 0.0))
        put_message(out_ref, head, mix, jnp.transpose(stats)[:8], 0)


def attend_middle(query, own, first, second, after):
    rows, width = own.shape[0] // 2, own.shape[1]
    heads = width // HD
    whole = pl.BlockSpec(memory_space=VMEM)
    return pl.pallas_call(
        middle_kernel,
        out_shape=jax.ShapeDtypeStruct((rows + SIDE, width), jnp.bfloat16),
        in_specs=[whole] * 4 + [pl.BlockSpec(memory_space=pl.ANY)],
        out_specs=whole,
        compiler_params=params(24),
        cost_estimate=pl.CostEstimate(flops=12 * heads * rows * rows * HD, bytes_accessed=2_000_000, transcendentals=3 * heads * rows * rows),
        name="attend_middle",
    )(query, own, first, second, after)


def merge_shares(windows_ref, stats_ref, pair_ref, middle_ref, rows, heads):
    height = lax.axis_index("tile") % HEIGHT_TILES
    wide = windows_ref[0, 1] >= 1
    valid = (wide, wide & (height > 0) & (height < HEIGHT_TILES - 1))
    line = lax.broadcasted_iota(jnp.int32, (16, rows), 0)
    shares = jnp.zeros((16, rows), jnp.float32)
    for head in range(heads):
        low = head * HD
        stats = stats_ref[head]
        largest, total = [stats[0:1]], [stats[1:2]]
        for ref, flag in zip((pair_ref, middle_ref), valid):
            side = ref[rows:, low : low + HD].astype(jnp.float32)
            side = jnp.concatenate([side[:8], side[8:]], axis=1)
            largest.append(jnp.where(flag, side[0:1] + side[1:2] + side[2:3], MASKED))
            total.append(jnp.where(flag, side[3:4] + side[4:5] + side[5:6], 0.0))
        peak = jnp.maximum(jnp.maximum(largest[0], largest[1]), largest[2])
        factors = [jnp.exp2(value - peak) for value in largest]
        whole = total[0] * factors[0] + total[1] * factors[1] + total[2] * factors[2]
        for index, factor in enumerate(factors):
            shares = jnp.where(line == 3 * head + index, factor / whole, shares)
    return jnp.transpose(shares)


def project_kernel(windows_ref, own_ref, stats_ref, pair_ref, middle_ref, weight_ref, out_ref):
    rows, width = own_ref.shape
    heads = width // HD
    shares = merge_shares(windows_ref, stats_ref, pair_ref, middle_ref, rows, heads)
    merged = []
    for head in range(heads):
        low = head * HD
        value = own_ref[:, low : low + HD] * column(shares, 3 * head)
        for index, ref in enumerate((pair_ref, middle_ref)):
            value += ref[:rows, low : low + HD].astype(jnp.float32) * column(shares, 3 * head + 1 + index)
        merged.append(value.astype(jnp.bfloat16))
    attention = jnp.concatenate(merged, axis=1)
    for group in range(out_ref.shape[0]):
        out_ref[group] = jnp.dot(
            attention, weight_ref[:, group * width : (group + 1) * width], preferred_element_type=jnp.float32
        ).astype(out_ref.dtype)


def project(windows, own, stats, pair, middle, out_weight):
    rows, width = own.shape
    features = out_weight.shape[1]
    whole = pl.BlockSpec(memory_space=VMEM)
    return pl.pallas_call(
        project_kernel,
        out_shape=jax.ShapeDtypeStruct((features // width, rows, width), jnp.bfloat16),
        in_specs=[pl.BlockSpec(memory_space=SMEM)] + [whole] * 5,
        out_specs=whole,
        compiler_params=params(24),
        cost_estimate=pl.CostEstimate(flops=2 * rows * width * features, bytes_accessed=5_000_000, transcendentals=0),
        name="project",
    )(windows, own, stats, pair, middle, out_weight)


def finish_kernel(terms_ref, residual_ref, gate_ref, out_ref):
    total = jnp.sum(terms_ref[...].astype(jnp.float32), axis=0)
    out_ref[...] = (residual_ref[...].astype(jnp.float32) + gate_ref[...] * total).astype(out_ref.dtype)


def finish(terms, residual, gate_scale):
    groups, rows, width = terms.shape
    steps = 2
    part = rows // steps
    return pl.pallas_call(
        finish_kernel,
        grid=(steps,),
        out_shape=jax.ShapeDtypeStruct((rows, width), residual.dtype),
        in_specs=[
            pl.BlockSpec((groups, part, width), lambda step: (0, step, 0)),
            pl.BlockSpec((part, width), lambda step: (step, 0)),
            pl.BlockSpec((1, width), lambda step: (0, 0)),
        ],
        out_specs=pl.BlockSpec((part, width), lambda step: (step, 0)),
        compiler_params=params(24),
        cost_estimate=pl.CostEstimate(flops=10 * groups * rows * width, bytes_accessed=2_000_000, transcendentals=0),
        name="finish",
    )(terms, residual, gate_scale.reshape(1, width))


def shards(queries, key_rows, value_rows, windows, residual, out_weight, gate_scale):
    packed, block = pack(windows, queries, key_rows, value_rows)
    first, second = swap_times(block, False), swap_times(block, True)
    asked = (packed, swap_pair(packed))
    before = attend(0, asked, block)
    before = attend(1, asked, first, before)
    for_middle = attend_middle(swap_middle(packed), block, first, second, before[1])
    (for_pair,) = attend(2, asked, second, before, (1,))
    own, stats = attend(2, asked, second, before, (0,))
    from_middle = gate(swap_middle(for_middle))
    terms = project(windows, own, stats, swap_pair(for_pair), from_middle, out_weight)
    terms = lax.all_to_all(terms, "head", 0, 0)
    return finish(terms, residual, gate_scale)


def solution(mesh):
    return jax.shard_map(
        shards,
        mesh=mesh,
        in_specs=(
            P("tile", "head"),
            P("tile", "head"),
            P("tile", "head"),
            P("tile", None),
            P("tile", "head"),
            P("head", None),
            P("head"),
        ),
        out_specs=P("tile", "head"),
        check_vma=False,
    )
```

```python
import functools

import jax
import jax.numpy as jnp
from jax import lax
from jax.experimental import pallas as pl
from jax.experimental.pallas import tpu as pltpu
from jax.sharding import PartitionSpec as P

HD = 128
HEIGHT_TILES = 4
SIDE = 16
LOG2E = 1.4426950408889634
MASKED = -1e30
MESH_AXES = ("tile", "head")
VMEM = pltpu.VMEM
SMEM = pltpu.SMEM


def params(megabytes):
    return pltpu.CompilerParams(vmem_limit_bytes=megabytes * 1024 * 1024)


def places():
    tiles = lax.axis_size("tile")
    return [(tile, *divmod(tile, HEIGHT_TILES), tiles // HEIGHT_TILES) for tile in range(tiles)]


def time_partner(time, height, later):
    odd = (height < HEIGHT_TILES // 2) != later
    return time + 1 if time % 2 == int(odd) else time - 1


def swap_times(block, later):
    route = []
    for tile, time, height, times in places():
        partner = time_partner(time, height, later)
        if 0 <= partner < times:
            route.append((tile, partner * HEIGHT_TILES + height))
    return lax.ppermute(block, "tile", route)


def swap_pair(block):
    return lax.ppermute(block, "tile", [(tile, tile ^ 1) for tile, *_ in places()])


def swap_middle(block):
    route = [(tile, tile + (1 if height == 1 else -1)) for tile, _, height, _ in places() if height in (1, 2)]
    return lax.ppermute(block, "tile", route)


def pack_kernel(windows_ref, q_ref, k_ref, v_ref, packed_ref, block_ref):
    rows = q_ref.shape[0]
    block_ref[:rows] = k_ref[...]
    block_ref[rows:] = v_ref[...]
    packed_ref[:rows] = q_ref[...]
    for axis in (0, 1):
        extent = windows_ref[0, axis].astype(jnp.float32)
        packed_ref[rows:, axis * HD : (axis + 1) * HD] = jnp.full((SIDE, HD), extent, jnp.float32).astype(packed_ref.dtype)
    packed_ref[rows:, 2 * HD :] = jnp.zeros((SIDE, q_ref.shape[1] - 2 * HD), packed_ref.dtype)


def pack(windows, queries, key_rows, value_rows):
    rows, width = queries.shape
    whole = pl.BlockSpec(memory_space=VMEM)
    return pl.pallas_call(
        pack_kernel,
        out_shape=(
            jax.ShapeDtypeStruct((rows + SIDE, width), queries.dtype),
            jax.ShapeDtypeStruct((2 * rows, width), queries.dtype),
        ),
        in_specs=[pl.BlockSpec(memory_space=SMEM)] + [whole] * 3,
        out_specs=(whole, whole),
        name="pack",
    )(windows, queries, key_rows, value_rows)


def column(values, index):
    return values[:, index : index + 1]


def split_float(value):
    high = value.astype(jnp.bfloat16).astype(jnp.float32)
    rest = value - high
    middle = rest.astype(jnp.bfloat16).astype(jnp.float32)
    return high, middle, (rest - middle).astype(jnp.bfloat16).astype(jnp.float32)


def wide_window(ref, rows, axis=0):
    return jnp.max(ref[rows:, axis * HD : (axis + 1) * HD].astype(jnp.float32)) > 0.5


def presence():
    tile = lax.axis_index("tile")
    time, height = tile // HEIGHT_TILES, tile % HEIGHT_TILES
    inner = (time > 0) & (time < lax.axis_size("tile") // HEIGHT_TILES - 1)
    lower = height < HEIGHT_TILES // 2
    return inner | ~lower, inner | lower


def raw_scores(query, keys):
    return lax.dot_general(query, keys, (((1,), (1,)), ((), ())), preferred_element_type=jnp.float32)


def put_message(ref, head, mix, stats, row):
    rows = mix.shape[0]
    low = head * HD
    line = lax.broadcasted_iota(jnp.int32, (8, rows), 0)
    ref[:rows, low : low + HD] = mix.astype(ref.dtype)
    side = jnp.zeros((8, rows), jnp.float32)
    for index, piece in enumerate(split_float(stats[row : row + 1]) + split_float(stats[row + 1 : row + 2])):
        side = jnp.where(line == index, piece, side)
    ref[rows:, low : low + HD] = jnp.concatenate([side[:, :HD], side[:, HD:]], axis=0).astype(ref.dtype)


def attend_kernel(stage, places, *refs):
    query_refs, block_ref, refs = refs[:2], refs[2], refs[3:]
    if stage == 0:
        weight_ref, refs, held_ref, sem = refs[0], refs[1:3], refs[3], refs[4]
        copy = pltpu.make_async_copy(weight_ref, held_ref, sem)
        copy.start()
    if stage > 0:
        old_mix_ref, old_stats_ref = refs[:2]
        refs = refs[2:]
    rows, width = block_ref.shape[0] // 2, block_ref.shape[1]
    scale = HD**-0.5 * LOG2E
    lane = lax.broadcasted_iota(jnp.int32, (rows, HD), 1)
    spread = lambda value: jnp.broadcast_to(value, (rows, HD))
    for place in places:
        ref = query_refs[place]
        bias = 0.0
        if stage > 0:
            bias = jnp.where(wide_window(ref, rows) & presence()[stage - 1], 0.0, MASKED)
        for head in range(width // HD):
            low = head * HD
            keys, values = block_ref[:rows, low : low + HD], block_ref[rows:, low : low + HD]
            part = raw_scores(ref[:rows, low : low + HD], keys)
            largest = spread(jnp.max(part, axis=1, keepdims=True)) * scale
            index = 2 * head + place
            if stage > 0:
                largest = jnp.maximum(largest + bias, old_stats_ref[2 * index])
            offset = jnp.concatenate([bias - largest] * (rows // HD), axis=1)
            weights = jnp.exp2(part * scale + offset)
            total = spread(jnp.sum(weights, axis=1, keepdims=True))
            mix = jnp.dot(weights.astype(values.dtype), values, preferred_element_type=jnp.float32)
            if stage > 0:
                shrink = jnp.exp2(old_stats_ref[2 * index] - largest)
                total += old_stats_ref[2 * index + 1] * shrink
                mix += old_mix_ref[index] * shrink
            if stage < 2:
                refs[0][index] = mix
                refs[1][2 * index] = largest
                refs[1][2 * index + 1] = total
                continue
            stats = jnp.transpose(jnp.where(lane == 0, largest, jnp.where(lane == 1, total, 0.0)))[:8]
            if place == 0:
                refs[0][:, low : low + HD] = mix
                line = lax.broadcasted_iota(jnp.int32, stats.shape, 0)
                refs[1][head] = jnp.where(line == 2, jnp.where(wide_window(ref, rows, 1), 1.0, 0.0), stats)
            else:
                put_message(refs[0], head, mix, stats, 0)
    if stage == 0:
        copy.wait()


def attend(stage, queries, block, before=(), places=(0, 1), out_weight=None):
    rows, width = block.shape[0] // 2, block.shape[1]
    heads = width // HD
    whole = pl.BlockSpec(memory_space=VMEM)
    if stage < 2:
        out_shape = (
            jax.ShapeDtypeStruct((2 * heads, rows, HD), jnp.float32),
            jax.ShapeDtypeStruct((4 * heads, rows, HD), jnp.float32),
        )
    elif places == (0,):
        out_shape = (
            jax.ShapeDtypeStruct((rows, width), jnp.float32),
            jax.ShapeDtypeStruct((heads, 8, rows), jnp.float32),
        )
    else:
        out_shape = (jax.ShapeDtypeStruct((rows + SIDE, width), jnp.bfloat16),)
    cost = len(places) * heads * rows * rows
    extra, extra_specs, scratch = (), [], []
    if stage == 0:
        extra, extra_specs = (out_weight,), [pl.BlockSpec(memory_space=pl.ANY)]
        out_shape += (jax.ShapeDtypeStruct(out_weight.shape, out_weight.dtype),)
        scratch = [pltpu.SemaphoreType.DMA]
    return pl.pallas_call(
        functools.partial(attend_kernel, stage, places),
        out_shape=out_shape,
        in_specs=[whole] * 3 + extra_specs + [whole] * len(before),
        out_specs=(whole,) * len(out_shape),
        scratch_shapes=scratch,
        compiler_params=params(24),
        cost_estimate=pl.CostEstimate(flops=4 * HD * cost, bytes_accessed=2_000_000, transcendentals=cost),
        name=("attend_own", "attend_first", "attend_second")[stage] + "_".join(map(str, places)),
    )(*queries, block, *extra, *before)


def gate_kernel(in_ref, out_ref):
    pass


def gate(array):
    anywhere = pl.BlockSpec(memory_space=pl.ANY)
    return pl.pallas_call(
        gate_kernel,
        out_shape=jax.ShapeDtypeStruct(array.shape, array.dtype),
        in_specs=[anywhere],
        out_specs=anywhere,
        input_output_aliases={0: 0},
        cost_estimate=pl.CostEstimate(flops=3_500_000_000, bytes_accessed=0, transcendentals=0),
        name="gate",
    )(array)


def middle_kernel(query_ref, own_ref, first_ref, second_ref, after_ref, out_ref):
    rows, width = own_ref.shape[0] // 2, own_ref.shape[1]
    scale = HD**-0.5 * LOG2E
    lane = lax.broadcasted_iota(jnp.int32, (rows, HD), 1)
    height = lax.axis_index("tile") % HEIGHT_TILES
    inside = (height > 0) & (height < HEIGHT_TILES - 1)

    @pl.when(inside)
    def compute():
        wide = wide_window(query_ref, rows)
        biases = [0.0] + [jnp.where(wide & present, 0.0, MASKED) for present in presence()]
        for head in range(width // HD):
            low = head * HD
            query = query_ref[:rows, low : low + HD]
            parts = [raw_scores(query, ref[:rows, low : low + HD]) for ref in (own_ref, first_ref, second_ref)]
            peaks = [jnp.max(part, axis=1, keepdims=True) * scale + bias for part, bias in zip(parts, biases)]
            largest = jnp.maximum(jnp.maximum(peaks[0], peaks[1]), peaks[2])
            weights = [jnp.exp2(part * scale + (bias - largest)) for part, bias in zip(parts, biases)]
            total = jnp.sum(weights[0] + weights[1] + weights[2], axis=1, keepdims=True)
            mix = jnp.zeros((rows, HD), jnp.float32)
            for weight, ref in zip(weights, (own_ref, first_ref, second_ref)):
                mix += jnp.dot(weight.astype(ref.dtype), ref[rows:, low : low + HD], preferred_element_type=jnp.float32)
            stats = jnp.where(lane == 0, largest, jnp.where(lane == 1, total, 0.0))
            put_message(out_ref, head, mix, jnp.transpose(stats)[:8], 0)

    @pl.when(jnp.logical_not(inside))
    def skip():
        out_ref[...] = jnp.zeros_like(out_ref)


def attend_middle(query, own, first, second, after):
    rows, width = own.shape[0] // 2, own.shape[1]
    heads = width // HD
    whole = pl.BlockSpec(memory_space=VMEM)
    return pl.pallas_call(
        middle_kernel,
        out_shape=jax.ShapeDtypeStruct((rows + SIDE, width), jnp.bfloat16),
        in_specs=[whole] * 4 + [pl.BlockSpec(memory_space=pl.ANY)],
        out_specs=whole,
        compiler_params=params(24),
        cost_estimate=pl.CostEstimate(flops=12 * heads * rows * rows * HD, bytes_accessed=2_000_000, transcendentals=3 * heads * rows * rows),
        name="attend_middle",
    )(query, own, first, second, after)


def merge_shares(stats_ref, pair_ref, middle_ref, rows, heads):
    height = lax.axis_index("tile") % HEIGHT_TILES
    inside = jnp.where((height > 0) & (height < HEIGHT_TILES - 1), 1.0, 0.0)
    line = lax.broadcasted_iota(jnp.int32, (16, rows), 0)
    shares = jnp.zeros((16, rows), jnp.float32)
    for head in range(heads):
        low = head * HD
        stats = stats_ref[head]
        largest, total = [stats[0:1]], [stats[1:2]]
        wide = stats[2:3]
        for ref, flag in ((pair_ref, wide > 0.5), (middle_ref, wide * inside > 0.5)):
            side = ref[rows:, low : low + HD].astype(jnp.float32)
            side = jnp.concatenate([side[:8], side[8:]], axis=1)
            largest.append(jnp.where(flag, side[0:1] + side[1:2] + side[2:3], MASKED))
            total.append(jnp.where(flag, side[3:4] + side[4:5] + side[5:6], 0.0))
        peak = jnp.maximum(jnp.maximum(largest[0], largest[1]), largest[2])
        factors = [jnp.exp2(value - peak) for value in largest]
        whole = total[0] * factors[0] + total[1] * factors[1] + total[2] * factors[2]
        for index, factor in enumerate(factors):
            shares = jnp.where(line == 3 * head + index, factor / whole, shares)
    return jnp.transpose(shares)


def project_kernel(own_ref, stats_ref, pair_ref, middle_ref, weight_ref, out_ref):
    rows, width = own_ref.shape
    heads = width // HD
    shares = merge_shares(stats_ref, pair_ref, middle_ref, rows, heads)
    merged = []
    for head in range(heads):
        low = head * HD
        value = own_ref[:, low : low + HD] * column(shares, 3 * head)
        for index, ref in enumerate((pair_ref, middle_ref)):
            value += ref[:rows, low : low + HD].astype(jnp.float32) * column(shares, 3 * head + 1 + index)
        merged.append(value.astype(jnp.bfloat16))
    attention = jnp.concatenate(merged, axis=1)
    for group in range(out_ref.shape[0]):
        out_ref[group] = jnp.dot(
            attention, weight_ref[:, group * width : (group + 1) * width], preferred_element_type=jnp.float32
        ).astype(out_ref.dtype)


def project(own, stats, pair, middle, out_weight):
    rows, width = own.shape
    features = out_weight.shape[1]
    whole = pl.BlockSpec(memory_space=VMEM)
    return pl.pallas_call(
        project_kernel,
        out_shape=jax.ShapeDtypeStruct((features // width, rows, width), jnp.bfloat16),
        in_specs=[whole] * 5,
        out_specs=whole,
        compiler_params=params(24),
        cost_estimate=pl.CostEstimate(flops=2 * rows * width * features, bytes_accessed=5_000_000, transcendentals=0),
        name="project",
    )(own, stats, pair, middle, out_weight)


def finish_kernel(terms_ref, residual_ref, gate_ref, out_ref):
    total = jnp.sum(terms_ref[...].astype(jnp.float32), axis=0)
    out_ref[...] = (residual_ref[...].astype(jnp.float32) + gate_ref[...] * total).astype(out_ref.dtype)


def finish(terms, residual, gate_scale):
    groups, rows, width = terms.shape
    steps = 2
    part = rows // steps
    return pl.pallas_call(
        finish_kernel,
        grid=(steps,),
        out_shape=jax.ShapeDtypeStruct((rows, width), residual.dtype),
        in_specs=[
            pl.BlockSpec((groups, part, width), lambda step: (0, step, 0)),
            pl.BlockSpec((part, width), lambda step: (step, 0)),
            pl.BlockSpec((1, width), lambda step: (0, 0)),
        ],
        out_specs=pl.BlockSpec((part, width), lambda step: (step, 0)),
        compiler_params=params(24),
        cost_estimate=pl.CostEstimate(flops=10 * groups * rows * width, bytes_accessed=2_000_000, transcendentals=0),
        name="finish",
    )(terms, residual, gate_scale.reshape(1, width))


def shards(queries, key_rows, value_rows, windows, residual, out_weight, gate_scale):
    packed, block = pack(windows, queries, key_rows, value_rows)
    first, second = swap_times(block, False), swap_times(block, True)
    asked = (packed, swap_pair(packed))
    *before, held_weight = attend(0, asked, block, out_weight=out_weight)
    before = attend(1, asked, first, before)
    (for_pair,) = attend(2, asked, second, before, (1,))
    for_middle = attend_middle(swap_middle(packed), block, first, second, for_pair)
    own, stats = attend(2, asked, second, before, (0,))
    from_pair = gate(swap_pair(for_pair))
    terms = project(own, stats, from_pair, swap_middle(for_middle), held_weight)
    terms = lax.all_to_all(terms, "head", 0, 0)
    return finish(terms, residual, gate_scale)


def solution(mesh):
    return jax.shard_map(
        shards,
        mesh=mesh,
        in_specs=(
            P("tile", "head"),
            P("tile", "head"),
            P("tile", "head"),
            P("tile", None),
            P("tile", "head"),
            P("head", None),
            P("head"),
        ),
        out_specs=P("tile", "head"),
        check_vma=False,
    )
```

```python
import functools

import jax
import jax.numpy as jnp
from jax import lax
from jax.experimental import pallas as pl
from jax.experimental.pallas import tpu as pltpu
from jax.sharding import PartitionSpec as P

HD = 128
HEIGHT_TILES = 4
SIDE = 16
LOG2E = 1.4426950408889634
MASKED = -1e30
MESH_AXES = ("tile", "head")
VMEM = pltpu.VMEM
SMEM = pltpu.SMEM


def params(megabytes):
    return pltpu.CompilerParams(vmem_limit_bytes=megabytes * 1024 * 1024)


def places():
    tiles = lax.axis_size("tile")
    return [(tile, *divmod(tile, HEIGHT_TILES), tiles // HEIGHT_TILES) for tile in range(tiles)]


def time_partner(time, height, later):
    odd = (height < HEIGHT_TILES // 2) != later
    return time + 1 if time % 2 == int(odd) else time - 1


def swap_times(block, later):
    route = []
    for tile, time, height, times in places():
        partner = time_partner(time, height, later)
        if 0 <= partner < times:
            route.append((tile, partner * HEIGHT_TILES + height))
    return lax.ppermute(block, "tile", route)


def swap_pair(block):
    return lax.ppermute(block, "tile", [(tile, tile ^ 1) for tile, *_ in places()])


def swap_middle(block):
    route = [(tile, tile + (1 if height == 1 else -1)) for tile, _, height, _ in places() if height in (1, 2)]
    return lax.ppermute(block, "tile", route)


def shift_columns(block, step):
    count = lax.axis_size("head")
    return lax.ppermute(block, "head", [(i, (i + 2 * step) % count) for i in range(count)])


def swap_depth(block):
    return lax.ppermute(block, "head", [(i, i ^ 1) for i in range(lax.axis_size("head"))])


def split_weight_kernel(weight_ref, *out_refs):
    width = out_refs[0].shape[1]
    mine = lax.axis_index("head") // 2
    for step, ref in enumerate(out_refs):
        start = pl.multiple_of(lax.rem(mine + step, len(out_refs)) * width, HD)
        ref[...] = weight_ref[:, pl.ds(start, width)]


def split_weight(out_weight):
    rows, features = out_weight.shape
    parts = lax.axis_size("head") // 2
    whole = pl.BlockSpec(memory_space=VMEM)
    return pl.pallas_call(
        split_weight_kernel,
        out_shape=(jax.ShapeDtypeStruct((rows, features // parts), out_weight.dtype),) * parts,
        in_specs=[whole],
        out_specs=(whole,) * parts,
        compiler_params=params(24),
        cost_estimate=pl.CostEstimate(flops=0, bytes_accessed=0, transcendentals=0),
        name="split_weight",
    )(out_weight)


def pack_kernel(windows_ref, q_ref, k_ref, v_ref, packed_ref, block_ref):
    rows = q_ref.shape[0]
    block_ref[:rows] = k_ref[...]
    block_ref[rows:] = v_ref[...]
    packed_ref[:rows] = q_ref[...]
    for axis in (0, 1):
        extent = windows_ref[0, axis].astype(jnp.float32)
        packed_ref[rows:, axis * HD : (axis + 1) * HD] = jnp.full((SIDE, HD), extent, jnp.float32).astype(packed_ref.dtype)
    packed_ref[rows:, 2 * HD :] = jnp.zeros((SIDE, q_ref.shape[1] - 2 * HD), packed_ref.dtype)


def pack(windows, queries, key_rows, value_rows):
    rows, width = queries.shape
    whole = pl.BlockSpec(memory_space=VMEM)
    return pl.pallas_call(
        pack_kernel,
        out_shape=(
            jax.ShapeDtypeStruct((rows + SIDE, width), queries.dtype),
            jax.ShapeDtypeStruct((2 * rows, width), queries.dtype),
        ),
        in_specs=[pl.BlockSpec(memory_space=SMEM)] + [whole] * 3,
        out_specs=(whole, whole),
        name="pack",
    )(windows, queries, key_rows, value_rows)


def column(values, index):
    return values[:, index : index + 1]


def split_float(value):
    high = value.astype(jnp.bfloat16).astype(jnp.float32)
    rest = value - high
    middle = rest.astype(jnp.bfloat16).astype(jnp.float32)
    return high, middle, (rest - middle).astype(jnp.bfloat16).astype(jnp.float32)


def wide_window(ref, rows, axis=0):
    return jnp.max(ref[rows:, axis * HD : (axis + 1) * HD].astype(jnp.float32)) > 0.5


def presence():
    tile = lax.axis_index("tile")
    time, height = tile // HEIGHT_TILES, tile % HEIGHT_TILES
    inner = (time > 0) & (time < lax.axis_size("tile") // HEIGHT_TILES - 1)
    lower = height < HEIGHT_TILES // 2
    return inner | ~lower, inner | lower


def raw_scores(query, keys):
    return lax.dot_general(query, keys, (((1,), (1,)), ((), ())), preferred_element_type=jnp.float32)


def put_message(ref, head, mix, stats, row):
    rows = mix.shape[0]
    low = head * HD
    line = lax.broadcasted_iota(jnp.int32, (8, rows), 0)
    ref[:rows, low : low + HD] = mix.astype(ref.dtype)
    side = jnp.zeros((8, rows), jnp.float32)
    for index, piece in enumerate(split_float(stats[row : row + 1]) + split_float(stats[row + 1 : row + 2])):
        side = jnp.where(line == index, piece, side)
    ref[rows:, low : low + HD] = jnp.concatenate([side[:, :HD], side[:, HD:]], axis=0).astype(ref.dtype)


def message_stats(ref, head, rows):
    side = ref[rows:, head * HD : (head + 1) * HD].astype(jnp.float32)
    side = jnp.concatenate([side[:8], side[8:]], axis=1)
    return side[0:1] + side[1:2] + side[2:3], side[3:4] + side[4:5] + side[5:6]


def message_columns(ref, head, rows):
    line = lax.broadcasted_iota(jnp.int32, (8, rows), 0)
    largest, total = message_stats(ref, head, rows)
    columns = jnp.transpose(jnp.where(line == 0, largest, jnp.where(line == 1, total, 0.0)))
    return [jnp.broadcast_to(column(columns, index), (rows, HD)) for index in (0, 1)]


def attend_kernel(stage, places, *refs):
    query_refs, block_ref, refs = refs[:2], refs[2], refs[3:]
    if stage > 0:
        old_mix_ref, old_stats_ref = refs[:2]
        refs = refs[2:]
    if stage == 1:
        refs = refs[-2:]
    if places == (0,):
        message_ref, refs = refs[0], refs[-2:]
    rows, width = block_ref.shape[0] // 2, block_ref.shape[1]
    scale = HD**-0.5 * LOG2E
    lane = lax.broadcasted_iota(jnp.int32, (rows, HD), 1)
    spread = lambda value: jnp.broadcast_to(value, (rows, HD))
    for place in places:
        ref = query_refs[place]
        bias = 0.0
        if stage > 0:
            bias = jnp.where(wide_window(ref, rows) & presence()[stage - 1], 0.0, MASKED)
        for head in range(width // HD):
            low = head * HD
            keys, values = block_ref[:rows, low : low + HD], block_ref[rows:, low : low + HD]
            part = raw_scores(ref[:rows, low : low + HD], keys)
            largest = spread(jnp.max(part, axis=1, keepdims=True)) * scale
            index = 2 * head + place
            if stage > 0:
                largest = jnp.maximum(largest + bias, old_stats_ref[2 * index])
            offset = jnp.concatenate([bias - largest] * (rows // HD), axis=1)
            weights = jnp.exp2(part * scale + offset)
            total = spread(jnp.sum(weights, axis=1, keepdims=True))
            mix = jnp.dot(weights.astype(values.dtype), values, preferred_element_type=jnp.float32)
            if stage > 0:
                shrink = jnp.exp2(old_stats_ref[2 * index] - largest)
                total += old_stats_ref[2 * index + 1] * shrink
                mix += old_mix_ref[index] * shrink
            if stage < 2:
                refs[0][index] = mix
                refs[1][2 * index] = largest
                refs[1][2 * index + 1] = total
                continue
            if place == 0:
                wide = wide_window(ref, rows, 1)
                their_largest, their_total = message_columns(message_ref, head, rows)
                peak = jnp.maximum(largest, jnp.where(wide, their_largest, MASKED))
                shrink, share = jnp.exp2(largest - peak), jnp.where(wide, jnp.exp2(their_largest - peak), 0.0)
                largest, total = peak, total * shrink + their_total * share
                mix = mix * shrink + message_ref[:rows, low : low + HD].astype(jnp.float32) * share
            stats = jnp.transpose(jnp.where(lane == 0, largest, jnp.where(lane == 1, total, 0.0)))[:8]
            if place == 0:
                refs[0][:, low : low + HD] = mix
                line = lax.broadcasted_iota(jnp.int32, stats.shape, 0)
                refs[1][head] = jnp.where(line == 2, jnp.where(wide, 1.0, 0.0), stats)
            else:
                put_message(refs[0], head, mix, stats, 0)


def attend(stage, queries, block, before=(), places=(0, 1), message=(), after=()):
    rows, width = block.shape[0] // 2, block.shape[1]
    heads = width // HD
    whole = pl.BlockSpec(memory_space=VMEM)
    flops = 4 * HD * len(places) * heads * rows * rows
    if stage < 2:
        out_shape = (
            jax.ShapeDtypeStruct((2 * heads, rows, HD), jnp.float32),
            jax.ShapeDtypeStruct((4 * heads, rows, HD), jnp.float32),
        )
    elif places == (0,):
        out_shape = (
            jax.ShapeDtypeStruct((rows, width), jnp.float32),
            jax.ShapeDtypeStruct((heads, 8, rows), jnp.float32),
        )
        flops = 3_500_000_000
    else:
        out_shape = (jax.ShapeDtypeStruct((rows + SIDE, width), jnp.bfloat16),)
    return pl.pallas_call(
        functools.partial(attend_kernel, stage, places),
        out_shape=out_shape,
        in_specs=[whole] * (3 + len(before) + len(message)) + [pl.BlockSpec(memory_space=pl.ANY)] * len(after),
        out_specs=(whole,) * len(out_shape),
        compiler_params=params(24),
        cost_estimate=pl.CostEstimate(flops=flops, bytes_accessed=2_000_000, transcendentals=len(places) * heads * rows * rows),
        name=("attend_own", "attend_first", "attend_second")[stage] + "_".join(map(str, places)),
    )(*queries, block, *before, *message, *after)


def middle_kernel(query_ref, own_ref, first_ref, second_ref, after_ref, out_ref):
    rows, width = own_ref.shape[0] // 2, own_ref.shape[1]
    scale = HD**-0.5 * LOG2E
    lane = lax.broadcasted_iota(jnp.int32, (rows, HD), 1)
    height = lax.axis_index("tile") % HEIGHT_TILES
    inside = (height > 0) & (height < HEIGHT_TILES - 1)

    @pl.when(inside)
    def compute():
        wide = wide_window(query_ref, rows)
        biases = [0.0] + [jnp.where(wide & present, 0.0, MASKED) for present in presence()]
        for head in range(width // HD):
            low = head * HD
            query = query_ref[:rows, low : low + HD]
            parts = [raw_scores(query, ref[:rows, low : low + HD]) for ref in (own_ref, first_ref, second_ref)]
            peaks = [jnp.max(part, axis=1, keepdims=True) * scale + bias for part, bias in zip(parts, biases)]
            largest = jnp.maximum(jnp.maximum(peaks[0], peaks[1]), peaks[2])
            weights = [jnp.exp2(part * scale + (bias - largest)) for part, bias in zip(parts, biases)]
            total = jnp.sum(weights[0] + weights[1] + weights[2], axis=1, keepdims=True)
            mix = jnp.zeros((rows, HD), jnp.float32)
            for weight, ref in zip(weights, (own_ref, first_ref, second_ref)):
                mix += jnp.dot(weight.astype(ref.dtype), ref[rows:, low : low + HD], preferred_element_type=jnp.float32)
            stats = jnp.where(lane == 0, largest, jnp.where(lane == 1, total, 0.0))
            put_message(out_ref, head, mix, jnp.transpose(stats)[:8], 0)

    @pl.when(jnp.logical_not(inside))
    def skip():
        out_ref[...] = jnp.zeros_like(out_ref)


def attend_middle(query, own, first, second, after):
    rows, width = own.shape[0] // 2, own.shape[1]
    heads = width // HD
    whole = pl.BlockSpec(memory_space=VMEM)
    return pl.pallas_call(
        middle_kernel,
        out_shape=jax.ShapeDtypeStruct((rows + SIDE, width), jnp.bfloat16),
        in_specs=[whole] * 4 + [pl.BlockSpec(memory_space=pl.ANY)],
        out_specs=whole,
        compiler_params=params(24),
        cost_estimate=pl.CostEstimate(flops=12 * heads * rows * rows * HD, bytes_accessed=2_000_000, transcendentals=3 * heads * rows * rows),
        name="attend_middle",
    )(query, own, first, second, after)


def merge_kernel(own_ref, stats_ref, middle_ref, out_ref):
    rows, width = own_ref.shape
    height = lax.axis_index("tile") % HEIGHT_TILES
    inside = jnp.where((height > 0) & (height < HEIGHT_TILES - 1), 1.0, 0.0)
    line = lax.broadcasted_iota(jnp.int32, (8, rows), 0)
    shares = jnp.zeros((8, rows), jnp.float32)
    for head in range(width // HD):
        stats = stats_ref[head]
        their_largest, their_total = message_stats(middle_ref, head, rows)
        valid = stats[2:3] * inside > 0.5
        peak = jnp.maximum(stats[0:1], jnp.where(valid, their_largest, MASKED))
        shrink = jnp.exp2(stats[0:1] - peak)
        share = jnp.where(valid, jnp.exp2(their_largest - peak), 0.0)
        whole = stats[1:2] * shrink + their_total * share
        shares = jnp.where(line == 2 * head, shrink / whole, shares)
        shares = jnp.where(line == 2 * head + 1, share / whole, shares)
    shares = jnp.transpose(shares)
    for head in range(width // HD):
        low = head * HD
        value = own_ref[:, low : low + HD] * column(shares, 2 * head)
        value += middle_ref[:rows, low : low + HD].astype(jnp.float32) * column(shares, 2 * head + 1)
        out_ref[:, low : low + HD] = value.astype(out_ref.dtype)


def merge(own, stats, middle):
    whole = pl.BlockSpec(memory_space=VMEM)
    return pl.pallas_call(
        merge_kernel,
        out_shape=jax.ShapeDtypeStruct(own.shape, jnp.bfloat16),
        in_specs=[whole] * 3,
        out_specs=whole,
        compiler_params=params(24),
        name="merge",
    )(own, stats, middle)


def project_kernel(*refs):
    parts = (len(refs) - 2) // 2
    attention_refs, weight_refs, (mine_ref, other_ref) = refs[:parts], refs[parts:-2], refs[-2:]
    width = mine_ref.shape[1]
    depth = lax.rem(lax.axis_index("head"), 2)
    for ref, place in ((other_ref, 1 - depth), (mine_ref, depth)):
        start = pl.multiple_of(place * width, HD)
        total = jnp.zeros(mine_ref.shape, jnp.float32)
        for attention_ref, weight_ref in zip(attention_refs, weight_refs):
            total += jnp.dot(attention_ref[...], weight_ref[:, pl.ds(start, width)], preferred_element_type=jnp.float32)
        ref[...] = total.astype(ref.dtype)


def project(attention, weights):
    shape = attention[0].shape
    whole = pl.BlockSpec(memory_space=VMEM)
    return pl.pallas_call(
        project_kernel,
        out_shape=(jax.ShapeDtypeStruct(shape, jnp.float32), jax.ShapeDtypeStruct(shape, jnp.bfloat16)),
        in_specs=[whole] * (len(attention) + len(weights)),
        out_specs=(whole, whole),
        compiler_params=params(24),
        name="project",
    )(*attention, *weights)


def finish_kernel(mine_ref, other_ref, residual_ref, gate_ref, out_ref):
    total = mine_ref[...] + other_ref[...].astype(jnp.float32)
    out_ref[...] = (residual_ref[...].astype(jnp.float32) + gate_ref[...] * total).astype(out_ref.dtype)


def finish(mine, other, residual, gate_scale):
    whole = pl.BlockSpec(memory_space=VMEM)
    return pl.pallas_call(
        finish_kernel,
        out_shape=jax.ShapeDtypeStruct(residual.shape, residual.dtype),
        in_specs=[whole] * 4,
        out_specs=whole,
        compiler_params=params(24),
        name="finish",
    )(mine, other, residual, gate_scale.reshape(1, -1))


def shards(queries, key_rows, value_rows, windows, residual, out_weight, gate_scale):
    packed, block = pack(windows, queries, key_rows, value_rows)
    first, second = swap_times(block, False), swap_times(block, True)
    asked = (packed, swap_pair(packed))
    weight, *to_send = split_weight(out_weight)
    steps = range(1, len(to_send) + 1)
    weights = [shift_columns(part, step) for step, part in zip(steps, to_send)]
    middle_asks = swap_middle(packed)
    before = attend(0, asked, block)
    before = attend(1, asked, first, before, after=(middle_asks,))
    (for_pair,) = attend(2, asked, second, before, (1,))
    for_middle = attend_middle(middle_asks, block, first, second, for_pair)
    own, stats = attend(2, asked, second, before, (0,), (swap_pair(for_pair),), weights)
    attention = merge(own, stats, swap_middle(for_middle))
    gathered = [shift_columns(attention, step) for step in steps]
    mine, other = project([attention, *gathered], [weight, *weights])
    return finish(mine, swap_depth(other), residual, gate_scale)


def solution(mesh):
    return jax.shard_map(
        shards,
        mesh=mesh,
        in_specs=(
            P("tile", "head"),
            P("tile", "head"),
            P("tile", "head"),
            P("tile", None),
            P("tile", "head"),
            P("head", None),
            P("head"),
        ),
        out_specs=P("tile", "head"),
        check_vma=False,
    )
```

```python
import functools

import jax
import jax.numpy as jnp
import numpy as np
from jax import lax
from jax.experimental import pallas as pl
from jax.experimental.pallas import tpu as pltpu
from jax.sharding import PartitionSpec as P

HD = 128
HEIGHT_TILES = 4
SIDE = 16
LOG2E = 1.4426950408889634
MASKED = -1e30
MESH_AXES = ("tile", "head")
VMEM = pltpu.VMEM
SMEM = pltpu.SMEM


def params(megabytes):
    return pltpu.CompilerParams(vmem_limit_bytes=megabytes * 1024 * 1024)


def places():
    tiles = lax.axis_size("tile")
    return [(tile, *divmod(tile, HEIGHT_TILES), tiles // HEIGHT_TILES) for tile in range(tiles)]


def time_partner(time, height, later):
    odd = (height < HEIGHT_TILES // 2) != later
    return time + 1 if time % 2 == int(odd) else time - 1


def swap_times(block, later):
    route = []
    for tile, time, height, times in places():
        partner = time_partner(time, height, later)
        if 0 <= partner < times:
            route.append((tile, partner * HEIGHT_TILES + height))
    return lax.ppermute(block, "tile", route)


def swap_pair(block):
    return lax.ppermute(block, "tile", [(tile, tile ^ 1) for tile, *_ in places()])


def swap_middle(block):
    route = [(tile, tile + (1 if height == 1 else -1)) for tile, _, height, _ in places() if height in (1, 2)]
    return lax.ppermute(block, "tile", route)


def swap_depth(block):
    return lax.ppermute(block, "depth", [(0, 1), (1, 0)])


def split_weight_kernel(weight_ref, out_ref):
    width = out_ref.shape[2]
    for part in range(out_ref.shape[0]):
        out_ref[part] = weight_ref[:, part * width : (part + 1) * width]


def split_weight(out_weight):
    rows, features = out_weight.shape
    parts = lax.axis_size("x")
    whole = pl.BlockSpec(memory_space=VMEM)
    return pl.pallas_call(
        split_weight_kernel,
        out_shape=jax.ShapeDtypeStruct((parts, rows, features // parts), out_weight.dtype),
        in_specs=[whole],
        out_specs=whole,
        compiler_params=params(24),
        cost_estimate=pl.CostEstimate(flops=0, bytes_accessed=0, transcendentals=0),
        name="split_weight",
    )(out_weight)


def pack_kernel(windows_ref, q_ref, k_ref, v_ref, packed_ref, block_ref):
    rows = q_ref.shape[0]
    block_ref[:rows] = k_ref[...]
    block_ref[rows:] = v_ref[...]
    packed_ref[:rows] = q_ref[...]
    for axis in (0, 1):
        extent = windows_ref[0, axis].astype(jnp.float32)
        packed_ref[rows:, axis * HD : (axis + 1) * HD] = jnp.full((SIDE, HD), extent, jnp.float32).astype(packed_ref.dtype)
    packed_ref[rows:, 2 * HD :] = jnp.zeros((SIDE, q_ref.shape[1] - 2 * HD), packed_ref.dtype)


def pack(windows, queries, key_rows, value_rows):
    rows, width = queries.shape
    whole = pl.BlockSpec(memory_space=VMEM)
    return pl.pallas_call(
        pack_kernel,
        out_shape=(
            jax.ShapeDtypeStruct((rows + SIDE, width), queries.dtype),
            jax.ShapeDtypeStruct((2 * rows, width), queries.dtype),
        ),
        in_specs=[pl.BlockSpec(memory_space=SMEM)] + [whole] * 3,
        out_specs=(whole, whole),
        name="pack",
    )(windows, queries, key_rows, value_rows)


def column(values, index):
    return values[:, index : index + 1]


def split_float(value):
    high = value.astype(jnp.bfloat16).astype(jnp.float32)
    rest = value - high
    middle = rest.astype(jnp.bfloat16).astype(jnp.float32)
    return high, middle, (rest - middle).astype(jnp.bfloat16).astype(jnp.float32)


def wide_window(ref, rows, axis=0):
    return jnp.max(ref[rows:, axis * HD : (axis + 1) * HD].astype(jnp.float32)) > 0.5


def presence():
    tile = lax.axis_index("tile")
    time, height = tile // HEIGHT_TILES, tile % HEIGHT_TILES
    inner = (time > 0) & (time < lax.axis_size("tile") // HEIGHT_TILES - 1)
    lower = height < HEIGHT_TILES // 2
    return inner | ~lower, inner | lower


def raw_scores(query, keys):
    return lax.dot_general(query, keys, (((1,), (1,)), ((), ())), preferred_element_type=jnp.float32)


def put_message(ref, head, mix, stats, row):
    rows = mix.shape[0]
    low = head * HD
    line = lax.broadcasted_iota(jnp.int32, (8, rows), 0)
    ref[:rows, low : low + HD] = mix.astype(ref.dtype)
    side = jnp.zeros((8, rows), jnp.float32)
    for index, piece in enumerate(split_float(stats[row : row + 1]) + split_float(stats[row + 1 : row + 2])):
        side = jnp.where(line == index, piece, side)
    ref[rows:, low : low + HD] = jnp.concatenate([side[:, :HD], side[:, HD:]], axis=0).astype(ref.dtype)


def message_stats(ref, head, rows):
    side = ref[rows:, head * HD : (head + 1) * HD].astype(jnp.float32)
    side = jnp.concatenate([side[:8], side[8:]], axis=1)
    return side[0:1] + side[1:2] + side[2:3], side[3:4] + side[4:5] + side[5:6]


def message_columns(ref, head, rows):
    line = lax.broadcasted_iota(jnp.int32, (8, rows), 0)
    largest, total = message_stats(ref, head, rows)
    columns = jnp.transpose(jnp.where(line == 0, largest, jnp.where(line == 1, total, 0.0)))
    return [jnp.broadcast_to(column(columns, index), (rows, HD)) for index in (0, 1)]


def attend_kernel(stage, places, *refs):
    query_refs, block_ref, refs = refs[:2], refs[2], refs[3:]
    if stage > 0:
        old_mix_ref, old_stats_ref = refs[:2]
        refs = refs[2:]
    if stage == 1:
        refs = refs[-2:]
    if places == (0,):
        message_ref, refs = refs[0], refs[-2:]
    rows, width = block_ref.shape[0] // 2, block_ref.shape[1]
    scale = HD**-0.5 * LOG2E
    lane = lax.broadcasted_iota(jnp.int32, (rows, HD), 1)
    spread = lambda value: jnp.broadcast_to(value, (rows, HD))
    for place in places:
        ref = query_refs[place]
        bias = 0.0
        if stage > 0:
            bias = jnp.where(wide_window(ref, rows) & presence()[stage - 1], 0.0, MASKED)
        for head in range(width // HD):
            low = head * HD
            keys, values = block_ref[:rows, low : low + HD], block_ref[rows:, low : low + HD]
            part = raw_scores(ref[:rows, low : low + HD], keys)
            largest = spread(jnp.max(part, axis=1, keepdims=True)) * scale
            index = 2 * head + place
            if stage > 0:
                largest = jnp.maximum(largest + bias, old_stats_ref[2 * index])
            offset = jnp.concatenate([bias - largest] * (rows // HD), axis=1)
            weights = jnp.exp2(part * scale + offset)
            total = spread(jnp.sum(weights, axis=1, keepdims=True))
            mix = jnp.dot(weights.astype(values.dtype), values, preferred_element_type=jnp.float32)
            if stage > 0:
                shrink = jnp.exp2(old_stats_ref[2 * index] - largest)
                total += old_stats_ref[2 * index + 1] * shrink
                mix += old_mix_ref[index] * shrink
            if stage < 2:
                refs[0][index] = mix
                refs[1][2 * index] = largest
                refs[1][2 * index + 1] = total
                continue
            if place == 0:
                wide = wide_window(ref, rows, 1)
                their_largest, their_total = message_columns(message_ref, head, rows)
                peak = jnp.maximum(largest, jnp.where(wide, their_largest, MASKED))
                shrink, share = jnp.exp2(largest - peak), jnp.where(wide, jnp.exp2(their_largest - peak), 0.0)
                largest, total = peak, total * shrink + their_total * share
                mix = mix * shrink + message_ref[:rows, low : low + HD].astype(jnp.float32) * share
            stats = jnp.transpose(jnp.where(lane == 0, largest, jnp.where(lane == 1, total, 0.0)))[:8]
            if place == 0:
                refs[0][:, low : low + HD] = mix
                line = lax.broadcasted_iota(jnp.int32, stats.shape, 0)
                refs[1][head] = jnp.where(line == 2, jnp.where(wide, 1.0, 0.0), stats)
            else:
                put_message(refs[0], head, mix, stats, 0)


def attend(stage, queries, block, before=(), places=(0, 1), message=(), after=()):
    rows, width = block.shape[0] // 2, block.shape[1]
    heads = width // HD
    whole = pl.BlockSpec(memory_space=VMEM)
    flops = 4 * HD * len(places) * heads * rows * rows
    if stage < 2:
        out_shape = (
            jax.ShapeDtypeStruct((2 * heads, rows, HD), jnp.float32),
            jax.ShapeDtypeStruct((4 * heads, rows, HD), jnp.float32),
        )
    elif places == (0,):
        out_shape = (
            jax.ShapeDtypeStruct((rows, width), jnp.float32),
            jax.ShapeDtypeStruct((heads, 8, rows), jnp.float32),
        )
        flops = 13_000_000_000
    else:
        out_shape = (jax.ShapeDtypeStruct((rows + SIDE, width), jnp.bfloat16),)
    return pl.pallas_call(
        functools.partial(attend_kernel, stage, places),
        out_shape=out_shape,
        in_specs=[whole] * (3 + len(before) + len(message)) + [pl.BlockSpec(memory_space=pl.ANY)] * len(after),
        out_specs=(whole,) * len(out_shape),
        compiler_params=params(24),
        cost_estimate=pl.CostEstimate(flops=flops, bytes_accessed=2_000_000, transcendentals=len(places) * heads * rows * rows),
        name=("attend_own", "attend_first", "attend_second")[stage] + "_".join(map(str, places)),
    )(*queries, block, *before, *message, *after)


def middle_kernel(query_ref, own_ref, first_ref, second_ref, after_ref, out_ref):
    rows, width = own_ref.shape[0] // 2, own_ref.shape[1]
    scale = HD**-0.5 * LOG2E
    lane = lax.broadcasted_iota(jnp.int32, (rows, HD), 1)
    height = lax.axis_index("tile") % HEIGHT_TILES
    inside = (height > 0) & (height < HEIGHT_TILES - 1)

    @pl.when(inside)
    def compute():
        wide = wide_window(query_ref, rows)
        biases = [0.0] + [jnp.where(wide & present, 0.0, MASKED) for present in presence()]
        for head in range(width // HD):
            low = head * HD
            query = query_ref[:rows, low : low + HD]
            parts = [raw_scores(query, ref[:rows, low : low + HD]) for ref in (own_ref, first_ref, second_ref)]
            peaks = [jnp.max(part, axis=1, keepdims=True) * scale + bias for part, bias in zip(parts, biases)]
            largest = jnp.maximum(jnp.maximum(peaks[0], peaks[1]), peaks[2])
            weights = [jnp.exp2(part * scale + (bias - largest)) for part, bias in zip(parts, biases)]
            total = jnp.sum(weights[0] + weights[1] + weights[2], axis=1, keepdims=True)
            mix = jnp.zeros((rows, HD), jnp.float32)
            for weight, ref in zip(weights, (own_ref, first_ref, second_ref)):
                mix += jnp.dot(weight.astype(ref.dtype), ref[rows:, low : low + HD], preferred_element_type=jnp.float32)
            stats = jnp.where(lane == 0, largest, jnp.where(lane == 1, total, 0.0))
            put_message(out_ref, head, mix, jnp.transpose(stats)[:8], 0)

    @pl.when(jnp.logical_not(inside))
    def skip():
        out_ref[...] = jnp.zeros_like(out_ref)


def attend_middle(query, own, first, second, after):
    rows, width = own.shape[0] // 2, own.shape[1]
    heads = width // HD
    whole = pl.BlockSpec(memory_space=VMEM)
    return pl.pallas_call(
        middle_kernel,
        out_shape=jax.ShapeDtypeStruct((rows + SIDE, width), jnp.bfloat16),
        in_specs=[whole] * 4 + [pl.BlockSpec(memory_space=pl.ANY)],
        out_specs=whole,
        compiler_params=params(24),
        cost_estimate=pl.CostEstimate(flops=12 * heads * rows * rows * HD, bytes_accessed=2_000_000, transcendentals=3 * heads * rows * rows),
        name="attend_middle",
    )(query, own, first, second, after)


def merge_kernel(own_ref, stats_ref, middle_ref, after_ref, out_ref):
    rows, width = own_ref.shape
    height = lax.axis_index("tile") % HEIGHT_TILES
    inside = jnp.where((height > 0) & (height < HEIGHT_TILES - 1), 1.0, 0.0)
    line = lax.broadcasted_iota(jnp.int32, (8, rows), 0)
    shares = jnp.zeros((8, rows), jnp.float32)
    for head in range(width // HD):
        stats = stats_ref[head]
        their_largest, their_total = message_stats(middle_ref, head, rows)
        valid = stats[2:3] * inside > 0.5
        peak = jnp.maximum(stats[0:1], jnp.where(valid, their_largest, MASKED))
        shrink = jnp.exp2(stats[0:1] - peak)
        share = jnp.where(valid, jnp.exp2(their_largest - peak), 0.0)
        whole = stats[1:2] * shrink + their_total * share
        shares = jnp.where(line == 2 * head, shrink / whole, shares)
        shares = jnp.where(line == 2 * head + 1, share / whole, shares)
    shares = jnp.transpose(shares)
    for head in range(width // HD):
        low = head * HD
        value = own_ref[:, low : low + HD] * column(shares, 2 * head)
        value += middle_ref[:rows, low : low + HD].astype(jnp.float32) * column(shares, 2 * head + 1)
        for part in range(out_ref.shape[0]):
            out_ref[part, :, low : low + HD] = value.astype(out_ref.dtype)


def merge(own, stats, middle, after):
    whole = pl.BlockSpec(memory_space=VMEM)
    return pl.pallas_call(
        merge_kernel,
        out_shape=jax.ShapeDtypeStruct((lax.axis_size("x"), *own.shape), jnp.bfloat16),
        in_specs=[whole] * 3 + [pl.BlockSpec(memory_space=pl.ANY)],
        out_specs=whole,
        compiler_params=params(24),
        name="merge",
    )(own, stats, middle, after)


def project_kernel(attention_ref, weight_ref, mine_ref, other_ref):
    width = mine_ref.shape[1]
    depth = lax.axis_index("depth")
    for ref, place in ((other_ref, 1 - depth), (mine_ref, depth)):
        start = pl.multiple_of(place * width, HD)
        total = jnp.zeros(mine_ref.shape, jnp.float32)
        for part in range(attention_ref.shape[0]):
            total += jnp.dot(attention_ref[part], weight_ref[part, :, pl.ds(start, width)], preferred_element_type=jnp.float32)
        ref[...] = total.astype(ref.dtype)


def project(attention, weight):
    shape = attention.shape[1:]
    whole = pl.BlockSpec(memory_space=VMEM)
    return pl.pallas_call(
        project_kernel,
        out_shape=(jax.ShapeDtypeStruct(shape, jnp.float32), jax.ShapeDtypeStruct(shape, jnp.bfloat16)),
        in_specs=[whole] * 2,
        out_specs=(whole, whole),
        compiler_params=params(24),
        name="project",
    )(attention, weight)


def finish_kernel(mine_ref, other_ref, residual_ref, gate_ref, out_ref):
    total = mine_ref[...] + other_ref[...].astype(jnp.float32)
    out_ref[...] = (residual_ref[...].astype(jnp.float32) + gate_ref[...] * total).astype(out_ref.dtype)


def finish(mine, other, residual, gate_scale):
    whole = pl.BlockSpec(memory_space=VMEM)
    return pl.pallas_call(
        finish_kernel,
        out_shape=jax.ShapeDtypeStruct(residual.shape, residual.dtype),
        in_specs=[whole] * 4,
        out_specs=whole,
        compiler_params=params(24),
        name="finish",
    )(mine, other, residual, gate_scale.reshape(1, -1))


def shards(queries, key_rows, value_rows, windows, residual, out_weight, gate_scale):
    packed, block = pack(windows, queries, key_rows, value_rows)
    first, second = swap_times(block, False), swap_times(block, True)
    asked = (packed, swap_pair(packed))
    middle_asks = swap_middle(packed)
    weight = lax.all_to_all(split_weight(out_weight), "x", 0, 0)
    before = attend(0, asked, block)
    before = attend(1, asked, first, before)
    (for_pair,) = attend(2, asked, second, before, (1,))
    for_middle = attend_middle(middle_asks, block, first, second, for_pair)
    own, stats = attend(2, asked, second, before, (0,), (swap_pair(for_pair),))
    attention = merge(own, stats, swap_middle(for_middle), weight)
    mine, other = project(lax.all_to_all(attention, "x", 0, 0), weight)
    return finish(mine, swap_depth(other), residual, gate_scale)


def solution(mesh):
    devices = np.asarray(mesh.devices)
    tiles, heads = devices.shape
    split = jax.sharding.Mesh(devices.reshape(tiles, heads // 2, 2), ("tile", "x", "depth"))
    head = ("x", "depth")
    return jax.shard_map(
        shards,
        mesh=split,
        in_specs=(
            P("tile", head),
            P("tile", head),
            P("tile", head),
            P("tile", None),
            P("tile", head),
            P(head, None),
            P(head),
        ),
        out_specs=P("tile", head),
        check_vma=False,
    )
```

```python
import functools

import jax
import jax.numpy as jnp
from jax import lax
from jax.experimental import pallas as pl
from jax.experimental.pallas import tpu as pltpu
from jax.sharding import PartitionSpec as P

HD = 128
HEIGHT_TILES = 4
SIDE = 16
LOG2E = 1.4426950408889634
MASKED = -1e30
MESH_AXES = ("tile", "head")
VMEM = pltpu.VMEM
SMEM = pltpu.SMEM


def params(megabytes):
    return pltpu.CompilerParams(vmem_limit_bytes=megabytes * 1024 * 1024)


def places():
    tiles = lax.axis_size("tile")
    return [(tile, *divmod(tile, HEIGHT_TILES), tiles // HEIGHT_TILES) for tile in range(tiles)]


def swap_times(block, later):
    route = []
    for tile, time, height, times in places():
        partner = time + 1 if time % 2 == int(not later) else time - 1
        if 0 <= partner < times:
            route.append((tile, partner * HEIGHT_TILES + height))
    return lax.ppermute(block, "tile", route)


def swap_pair(block):
    return lax.ppermute(block, "tile", [(tile, tile ^ 1) for tile, *_ in places()])


def swap_middle(block):
    route = [(tile, tile + (1 if height == 1 else -1)) for tile, _, height, _ in places() if height in (1, 2)]
    return lax.ppermute(block, "tile", route)


def pack_kernel(windows_ref, q_ref, k_ref, v_ref, packed_ref, block_ref):
    rows = q_ref.shape[0]
    block_ref[:rows] = k_ref[...]
    block_ref[rows:] = v_ref[...]
    packed_ref[:rows] = q_ref[...]
    for axis in (0, 1):
        extent = windows_ref[0, axis].astype(jnp.float32)
        packed_ref[rows:, axis * HD : (axis + 1) * HD] = jnp.full((SIDE, HD), extent, jnp.float32).astype(packed_ref.dtype)
    packed_ref[rows:, 2 * HD :] = jnp.zeros((SIDE, q_ref.shape[1] - 2 * HD), packed_ref.dtype)


def pack(windows, queries, key_rows, value_rows):
    rows, width = queries.shape
    whole = pl.BlockSpec(memory_space=VMEM)
    return pl.pallas_call(
        pack_kernel,
        out_shape=(
            jax.ShapeDtypeStruct((rows + SIDE, width), queries.dtype),
            jax.ShapeDtypeStruct((2 * rows, width), queries.dtype),
        ),
        in_specs=[pl.BlockSpec(memory_space=SMEM)] + [whole] * 3,
        out_specs=(whole, whole),
        name="pack",
    )(windows, queries, key_rows, value_rows)


def column(values, index):
    return values[:, index : index + 1]


def split_float(value):
    high = value.astype(jnp.bfloat16).astype(jnp.float32)
    rest = value - high
    middle = rest.astype(jnp.bfloat16).astype(jnp.float32)
    return high, middle, (rest - middle).astype(jnp.bfloat16).astype(jnp.float32)


def wide_window(ref, rows, axis=0):
    return jnp.max(ref[rows:, axis * HD : (axis + 1) * HD].astype(jnp.float32)) > 0.5


def has_first():
    time = lax.axis_index("tile") // HEIGHT_TILES
    return (time > 0) & (time < lax.axis_size("tile") // HEIGHT_TILES - 1)


def block_bias(wide, stage):
    return jnp.where(wide & has_first() if stage == 1 else wide, 0.0, MASKED)


def raw_scores(query, keys):
    return lax.dot_general(query, keys, (((1,), (1,)), ((), ())), preferred_element_type=jnp.float32)


def put_message(ref, head, mix, stats, row):
    rows = mix.shape[0]
    low = head * HD
    line = lax.broadcasted_iota(jnp.int32, (8, rows), 0)
    ref[:rows, low : low + HD] = mix.astype(ref.dtype)
    side = jnp.zeros((8, rows), jnp.float32)
    for index, piece in enumerate(split_float(stats[row : row + 1]) + split_float(stats[row + 1 : row + 2])):
        side = jnp.where(line == index, piece, side)
    ref[rows:, low : low + HD] = jnp.concatenate([side[:, :HD], side[:, HD:]], axis=0).astype(ref.dtype)


def message_stats(ref, head, rows):
    side = ref[rows:, head * HD : (head + 1) * HD].astype(jnp.float32)
    side = jnp.concatenate([side[:8], side[8:]], axis=1)
    return side[0:1] + side[1:2] + side[2:3], side[3:4] + side[4:5] + side[5:6]


def message_columns(ref, head, rows):
    line = lax.broadcasted_iota(jnp.int32, (8, rows), 0)
    largest, total = message_stats(ref, head, rows)
    columns = jnp.transpose(jnp.where(line == 0, largest, jnp.where(line == 1, total, 0.0)))
    return [jnp.broadcast_to(column(columns, index), (rows, HD)) for index in (0, 1)]


def attend_kernel(stage, places, *refs):
    query_refs, block_ref, refs = refs[:2], refs[2], refs[3:]
    if stage == 0:
        weight_ref, refs, held_ref, sem = refs[0], refs[1:3], refs[3], refs[4]
        copy = pltpu.make_async_copy(weight_ref, held_ref, sem)
        copy.start()
    if stage > 0:
        old_mix_ref, old_stats_ref = refs[:2]
        refs = refs[2:]
    if places == (0,):
        message_ref, refs = refs[0], refs[-2:]
    rows, width = block_ref.shape[0] // 2, block_ref.shape[1]
    scale = HD**-0.5 * LOG2E
    lane = lax.broadcasted_iota(jnp.int32, (rows, HD), 1)
    spread = lambda value: jnp.broadcast_to(value, (rows, HD))
    for place in places:
        ref = query_refs[place]
        bias = 0.0
        if stage > 0:
            bias = block_bias(wide_window(ref, rows), stage)
        for head in range(width // HD):
            low = head * HD
            keys, values = block_ref[:rows, low : low + HD], block_ref[rows:, low : low + HD]
            part = raw_scores(ref[:rows, low : low + HD], keys)
            largest = spread(jnp.max(part, axis=1, keepdims=True)) * scale
            index = 2 * head + place
            if stage > 0:
                largest = jnp.maximum(largest + bias, old_stats_ref[2 * index])
            offset = jnp.concatenate([bias - largest] * (rows // HD), axis=1)
            weights = jnp.exp2(part * scale + offset)
            total = spread(jnp.sum(weights, axis=1, keepdims=True))
            mix = jnp.dot(weights.astype(values.dtype), values, preferred_element_type=jnp.float32)
            if stage > 0:
                shrink = jnp.exp2(old_stats_ref[2 * index] - largest)
                total += old_stats_ref[2 * index + 1] * shrink
                mix += old_mix_ref[index] * shrink
            if stage < 2:
                refs[0][index] = mix
                refs[1][2 * index] = largest
                refs[1][2 * index + 1] = total
                continue
            if place == 0:
                wide = wide_window(ref, rows, 1)
                their_largest, their_total = message_columns(message_ref, head, rows)
                peak = jnp.maximum(largest, jnp.where(wide, their_largest, MASKED))
                shrink, share = jnp.exp2(largest - peak), jnp.where(wide, jnp.exp2(their_largest - peak), 0.0)
                largest, total = peak, total * shrink + their_total * share
                mix = mix * shrink + message_ref[:rows, low : low + HD].astype(jnp.float32) * share
            stats = jnp.transpose(jnp.where(lane == 0, largest, jnp.where(lane == 1, total, 0.0)))[:8]
            if place == 0:
                refs[0][:, low : low + HD] = mix
                line = lax.broadcasted_iota(jnp.int32, stats.shape, 0)
                refs[1][head] = jnp.where(line == 2, jnp.where(wide, 1.0, 0.0), stats)
            else:
                put_message(refs[0], head, mix, stats, 0)
    if stage == 0:
        copy.wait()


def attend(stage, queries, block, before=(), places=(0, 1), message=(), out_weight=None):
    rows, width = block.shape[0] // 2, block.shape[1]
    heads = width // HD
    whole = pl.BlockSpec(memory_space=VMEM)
    flops = 4 * HD * len(places) * heads * rows * rows
    if stage < 2:
        out_shape = (
            jax.ShapeDtypeStruct((2 * heads, rows, HD), jnp.float32),
            jax.ShapeDtypeStruct((4 * heads, rows, HD), jnp.float32),
        )
    elif places == (0,):
        out_shape = (
            jax.ShapeDtypeStruct((rows, width), jnp.float32),
            jax.ShapeDtypeStruct((heads, 8, rows), jnp.float32),
        )
        flops = 3_500_000_000
    else:
        out_shape = (jax.ShapeDtypeStruct((rows + SIDE, width), jnp.bfloat16),)
    extra, extra_specs, scratch = (), [], []
    if stage == 0:
        extra, extra_specs = (out_weight,), [pl.BlockSpec(memory_space=pl.ANY)]
        out_shape += (jax.ShapeDtypeStruct(out_weight.shape, out_weight.dtype),)
        scratch = [pltpu.SemaphoreType.DMA]
    return pl.pallas_call(
        functools.partial(attend_kernel, stage, places),
        out_shape=out_shape,
        in_specs=[whole] * 3 + extra_specs + [whole] * (len(before) + len(message)),
        out_specs=(whole,) * len(out_shape),
        scratch_shapes=scratch,
        compiler_params=params(24),
        cost_estimate=pl.CostEstimate(flops=flops, bytes_accessed=2_000_000, transcendentals=len(places) * heads * rows * rows),
        name=("attend_own", "attend_first", "attend_second")[stage] + "_".join(map(str, places)),
    )(*queries, block, *extra, *before, *message)


def middle_kernel(query_ref, own_ref, first_ref, second_ref, after_ref, out_ref):
    rows, width = own_ref.shape[0] // 2, own_ref.shape[1]
    scale = HD**-0.5 * LOG2E
    lane = lax.broadcasted_iota(jnp.int32, (rows, HD), 1)
    height = lax.axis_index("tile") % HEIGHT_TILES
    inside = (height > 0) & (height < HEIGHT_TILES - 1)

    @pl.when(inside)
    def compute():
        wide = wide_window(query_ref, rows)
        biases = [0.0] + [block_bias(wide, stage) for stage in (1, 2)]
        for head in range(width // HD):
            low = head * HD
            query = query_ref[:rows, low : low + HD]
            parts = [raw_scores(query, ref[:rows, low : low + HD]) for ref in (own_ref, first_ref, second_ref)]
            peaks = [jnp.max(part, axis=1, keepdims=True) * scale + bias for part, bias in zip(parts, biases)]
            largest = jnp.maximum(jnp.maximum(peaks[0], peaks[1]), peaks[2])
            weights = [jnp.exp2(part * scale + (bias - largest)) for part, bias in zip(parts, biases)]
            total = jnp.sum(weights[0] + weights[1] + weights[2], axis=1, keepdims=True)
            mix = jnp.zeros((rows, HD), jnp.float32)
            for weight, ref in zip(weights, (own_ref, first_ref, second_ref)):
                mix += jnp.dot(weight.astype(ref.dtype), ref[rows:, low : low + HD], preferred_element_type=jnp.float32)
            stats = jnp.where(lane == 0, largest, jnp.where(lane == 1, total, 0.0))
            put_message(out_ref, head, mix, jnp.transpose(stats)[:8], 0)

    @pl.when(jnp.logical_not(inside))
    def skip():
        out_ref[...] = jnp.zeros_like(out_ref)


def attend_middle(query, own, first, second, after):
    rows, width = own.shape[0] // 2, own.shape[1]
    heads = width // HD
    whole = pl.BlockSpec(memory_space=VMEM)
    return pl.pallas_call(
        middle_kernel,
        out_shape=jax.ShapeDtypeStruct((rows + SIDE, width), jnp.bfloat16),
        in_specs=[whole] * 4 + [pl.BlockSpec(memory_space=pl.ANY)],
        out_specs=whole,
        compiler_params=params(24),
        cost_estimate=pl.CostEstimate(flops=12 * heads * rows * rows * HD, bytes_accessed=2_000_000, transcendentals=3 * heads * rows * rows),
        name="attend_middle",
    )(query, own, first, second, after)


def project_kernel(own_ref, stats_ref, middle_ref, weight_ref, out_ref):
    rows, width = own_ref.shape
    heads = width // HD
    height = lax.axis_index("tile") % HEIGHT_TILES
    inside = jnp.where((height > 0) & (height < HEIGHT_TILES - 1), 1.0, 0.0)
    line = lax.broadcasted_iota(jnp.int32, (8, rows), 0)
    shares = jnp.zeros((8, rows), jnp.float32)
    for head in range(heads):
        stats = stats_ref[head]
        their_largest, their_total = message_stats(middle_ref, head, rows)
        valid = stats[2:3] * inside > 0.5
        peak = jnp.maximum(stats[0:1], jnp.where(valid, their_largest, MASKED))
        shrink = jnp.exp2(stats[0:1] - peak)
        share = jnp.where(valid, jnp.exp2(their_largest - peak), 0.0)
        whole = stats[1:2] * shrink + their_total * share
        shares = jnp.where(line == 2 * head, shrink / whole, shares)
        shares = jnp.where(line == 2 * head + 1, share / whole, shares)
    shares = jnp.transpose(shares)
    merged = []
    for head in range(heads):
        low = head * HD
        value = own_ref[:, low : low + HD] * column(shares, 2 * head)
        value += middle_ref[:rows, low : low + HD].astype(jnp.float32) * column(shares, 2 * head + 1)
        merged.append(value.astype(jnp.bfloat16))
    attention = jnp.concatenate(merged, axis=1)
    for group in range(out_ref.shape[0]):
        out_ref[group] = jnp.dot(
            attention, weight_ref[:, group * width : (group + 1) * width], preferred_element_type=jnp.float32
        ).astype(out_ref.dtype)


def project(own, stats, middle, out_weight):
    rows, width = own.shape
    features = out_weight.shape[1]
    whole = pl.BlockSpec(memory_space=VMEM)
    return pl.pallas_call(
        project_kernel,
        out_shape=jax.ShapeDtypeStruct((features // width, rows, width), jnp.bfloat16),
        in_specs=[whole] * 4,
        out_specs=whole,
        compiler_params=params(24),
        cost_estimate=pl.CostEstimate(flops=2 * rows * width * features, bytes_accessed=5_000_000, transcendentals=0),
        name="project",
    )(own, stats, middle, out_weight)


def finish_kernel(terms_ref, residual_ref, gate_ref, out_ref):
    total = jnp.sum(terms_ref[...].astype(jnp.float32), axis=0)
    out_ref[...] = (residual_ref[...].astype(jnp.float32) + gate_ref[...] * total).astype(out_ref.dtype)


def finish(terms, residual, gate_scale):
    whole = pl.BlockSpec(memory_space=VMEM)
    return pl.pallas_call(
        finish_kernel,
        out_shape=jax.ShapeDtypeStruct(residual.shape, residual.dtype),
        in_specs=[whole] * 3,
        out_specs=whole,
        compiler_params=params(24),
        cost_estimate=pl.CostEstimate(flops=10 * terms.size, bytes_accessed=2_000_000, transcendentals=0),
        name="finish",
    )(terms, residual, gate_scale.reshape(1, -1))


def shards(queries, key_rows, value_rows, windows, residual, out_weight, gate_scale):
    packed, block = pack(windows, queries, key_rows, value_rows)
    first, second = swap_times(block, False), swap_times(block, True)
    asked = (packed, swap_pair(packed))
    *before, held_weight = attend(0, asked, block, out_weight=out_weight)
    before = attend(1, asked, first, before)
    (for_pair,) = attend(2, asked, second, before, (1,))
    for_middle = attend_middle(swap_middle(packed), block, first, second, for_pair)
    own, stats = attend(2, asked, second, before, (0,), (swap_pair(for_pair),))
    terms = project(own, stats, swap_middle(for_middle), held_weight)
    terms = lax.all_to_all(terms, "head", 0, 0)
    return finish(terms, residual, gate_scale)


def solution(mesh):
    return jax.shard_map(
        shards,
        mesh=mesh,
        in_specs=(
            P("tile", "head"),
            P("tile", "head"),
            P("tile", "head"),
            P("tile", None),
            P("tile", "head"),
            P("head", None),
            P("head"),
        ),
        out_specs=P("tile", "head"),
        check_vma=False,
    )
```

```python
import functools

import jax
import jax.numpy as jnp
from jax import lax
from jax.experimental import pallas as pl
from jax.experimental.pallas import tpu as pltpu
from jax.sharding import PartitionSpec as P

HD = 128
HEIGHT_TILES = 4
SIDE = 16
LOG2E = 1.4426950408889634
MASKED = -1e30
LAST_FLOPS = 3_500_000_000
HERE_FLOPS = 2_000_000_000
MESH_AXES = ("tile", "head")
VMEM = pltpu.VMEM
SMEM = pltpu.SMEM


def params(megabytes):
    return pltpu.CompilerParams(vmem_limit_bytes=megabytes * 1024 * 1024)


def places():
    tiles = lax.axis_size("tile")
    return [(tile, *divmod(tile, HEIGHT_TILES), tiles // HEIGHT_TILES) for tile in range(tiles)]


def swap_times(block, later):
    route = []
    for tile, time, height, times in places():
        partner = time + 1 if time % 2 == int(not later) else time - 1
        if 0 <= partner < times:
            route.append((tile, partner * HEIGHT_TILES + height))
    return lax.ppermute(block, "tile", route)


def swap_pair(block):
    return lax.ppermute(block, "tile", [(tile, tile ^ 1) for tile, *_ in places()])


def swap_middle(block):
    route = [(tile, tile + (1 if height == 1 else -1)) for tile, _, height, _ in places() if height in (1, 2)]
    return lax.ppermute(block, "tile", route)


def pack_kernel(windows_ref, q_ref, packed_ref):
    rows = q_ref.shape[0]
    packed_ref[:rows] = q_ref[...]
    for axis in (0, 1):
        extent = windows_ref[0, axis].astype(jnp.float32)
        packed_ref[rows:, axis * HD : (axis + 1) * HD] = jnp.full((SIDE, HD), extent, jnp.float32).astype(packed_ref.dtype)
    packed_ref[rows:, 2 * HD :] = jnp.zeros((SIDE, q_ref.shape[1] - 2 * HD), packed_ref.dtype)


def pack(windows, queries):
    rows, width = queries.shape
    whole = pl.BlockSpec(memory_space=VMEM)
    return pl.pallas_call(
        pack_kernel,
        out_shape=jax.ShapeDtypeStruct((rows + SIDE, width), queries.dtype),
        in_specs=[pl.BlockSpec(memory_space=SMEM), whole],
        out_specs=whole,
        compiler_params=params(8),
        name="pack",
    )(windows, queries)


def column(values, index):
    return values[:, index : index + 1]


def split_float(value):
    high = value.astype(jnp.bfloat16).astype(jnp.float32)
    rest = value - high
    middle = rest.astype(jnp.bfloat16).astype(jnp.float32)
    return high, middle, (rest - middle).astype(jnp.bfloat16).astype(jnp.float32)


def wide_window(ref, rows, axis=0):
    return jnp.max(ref[rows:, axis * HD : (axis + 1) * HD].astype(jnp.float32)) > 0.5


def has_first():
    time = lax.axis_index("tile") // HEIGHT_TILES
    return (time > 0) & (time < lax.axis_size("tile") // HEIGHT_TILES - 1)


def block_bias(wide, stage):
    return jnp.where(wide & has_first() if stage == 1 else wide, 0.0, MASKED)


def raw_scores(query, keys):
    return lax.dot_general(query, keys, (((1,), (1,)), ((), ())), preferred_element_type=jnp.float32)


def put_message(ref, head, mix, stats, row):
    rows = mix.shape[0]
    low = head * HD
    line = lax.broadcasted_iota(jnp.int32, (8, rows), 0)
    ref[:rows, low : low + HD] = mix.astype(ref.dtype)
    side = jnp.zeros((8, rows), jnp.float32)
    for index, piece in enumerate(split_float(stats[row : row + 1]) + split_float(stats[row + 1 : row + 2])):
        side = jnp.where(line == index, piece, side)
    ref[rows:, low : low + HD] = jnp.concatenate([side[:, :HD], side[:, HD:]], axis=0).astype(ref.dtype)


def message_stats(ref, head, rows):
    side = ref[rows:, head * HD : (head + 1) * HD].astype(jnp.float32)
    side = jnp.concatenate([side[:8], side[8:]], axis=1)
    return side[0:1] + side[1:2] + side[2:3], side[3:4] + side[4:5] + side[5:6]


def message_columns(ref, head, rows):
    line = lax.broadcasted_iota(jnp.int32, (8, rows), 0)
    largest, total = message_stats(ref, head, rows)
    columns = jnp.transpose(jnp.where(line == 0, largest, jnp.where(line == 1, total, 0.0)))
    return [jnp.broadcast_to(column(columns, index), (rows, HD)) for index in (0, 1)]


def attend(query, blocks, biases, low, old=None):
    rows = blocks[0][0].shape[0]
    scale = HD**-0.5 * LOG2E
    spread = lambda value: jnp.broadcast_to(value, (rows, HD))
    parts = [raw_scores(query, keys[:, low : low + HD]) for keys, _ in blocks]
    largest = None if old is None else old[0]
    for part, bias in zip(parts, biases):
        peak = spread(jnp.max(part, axis=1, keepdims=True)) * scale + bias
        largest = peak if largest is None else jnp.maximum(largest, peak)
    summed, mix = None, None
    for part, bias, (_, values) in zip(parts, biases, blocks):
        offset = jnp.concatenate([bias - largest] * (rows // HD), axis=1)
        weights = jnp.exp2(part * scale + offset)
        product = jnp.dot(weights.astype(values.dtype), values[:, low : low + HD], preferred_element_type=jnp.float32)
        summed = weights if summed is None else summed + weights
        mix = product if mix is None else mix + product
    total = spread(jnp.sum(summed, axis=1, keepdims=True))
    if old is not None:
        shrink = jnp.exp2(old[0] - largest)
        total, mix = total + old[1] * shrink, mix + old[2] * shrink
    return largest, total, mix


def row_stats(largest, total):
    lane = lax.broadcasted_iota(jnp.int32, largest.shape, 1)
    return jnp.transpose(jnp.where(lane == 0, largest, jnp.where(lane == 1, total, 0.0)))[:8]


def own_kernel(query_ref, key_ref, value_ref, weight_ref, mix_ref, stats_ref, held_ref, sem):
    copy = pltpu.make_async_copy(weight_ref, held_ref, sem)
    copy.start()
    rows, width = key_ref.shape
    for head in range(width // HD):
        low = head * HD
        largest, total, mix = attend(query_ref[:rows, low : low + HD], [(key_ref, value_ref)], [0.0], low)
        mix_ref[head], stats_ref[2 * head], stats_ref[2 * head + 1] = mix, largest, total
    copy.wait()


def attend_own(queries, block, out_weight):
    rows, width = block[0].shape
    heads = width // HD
    whole = pl.BlockSpec(memory_space=VMEM)
    return pl.pallas_call(
        own_kernel,
        out_shape=(
            jax.ShapeDtypeStruct((heads, rows, HD), jnp.float32),
            jax.ShapeDtypeStruct((2 * heads, rows, HD), jnp.float32),
            jax.ShapeDtypeStruct(out_weight.shape, out_weight.dtype),
        ),
        in_specs=[whole] * 3 + [pl.BlockSpec(memory_space=pl.ANY)],
        out_specs=(whole,) * 3,
        scratch_shapes=[pltpu.SemaphoreType.DMA],
        compiler_params=params(24),
        cost_estimate=pl.CostEstimate(flops=0, bytes_accessed=0, transcendentals=0),
        name="attend_own",
    )(queries, *block, out_weight)


def neighbour_kernel(middle, query_ref, *refs):
    blocks = [(refs[2 * i], refs[2 * i + 1]) for i in range(3)]
    out_ref = refs[-1]
    rows, width = blocks[0][0].shape
    height = lax.axis_index("tile") % HEIGHT_TILES

    def compute():
        wide = wide_window(query_ref, rows)
        biases = [0.0] + [block_bias(wide, stage) for stage in (1, 2)]
        for head in range(width // HD):
            low = head * HD
            largest, total, mix = attend(query_ref[:rows, low : low + HD], blocks, biases, low)
            put_message(out_ref, head, mix, row_stats(largest, total), 0)

    if not middle:
        compute()
        return
    inside = (height > 0) & (height < HEIGHT_TILES - 1)
    pl.when(inside)(compute)

    @pl.when(jnp.logical_not(inside))
    def skip():
        out_ref[...] = jnp.zeros_like(out_ref)


def attend_neighbour(middle, query, blocks, after=()):
    rows, width = blocks[0][0].shape
    whole = pl.BlockSpec(memory_space=VMEM)
    cost = 3 * (width // HD) * rows * rows
    return pl.pallas_call(
        functools.partial(neighbour_kernel, middle),
        out_shape=jax.ShapeDtypeStruct((rows + SIDE, width), jnp.bfloat16),
        in_specs=[whole] * 7 + [pl.BlockSpec(memory_space=pl.ANY)] * len(after),
        out_specs=whole,
        compiler_params=params(24),
        cost_estimate=pl.CostEstimate(flops=4 * HD * cost, bytes_accessed=2_000_000, transcendentals=cost),
        name="attend_middle" if middle else "attend_pair",
    )(query, *[array for block in blocks for array in block], *after)


def here_kernel(*refs):
    refs[-1][...] = jnp.zeros_like(refs[-1])


def all_here(arrays):
    return pl.pallas_call(
        here_kernel,
        out_shape=jax.ShapeDtypeStruct((8, HD), jnp.float32),
        in_specs=[pl.BlockSpec(memory_space=pl.ANY)] * len(arrays),
        out_specs=pl.BlockSpec(memory_space=VMEM),
        compiler_params=params(4),
        cost_estimate=pl.CostEstimate(flops=HERE_FLOPS, bytes_accessed=0, transcendentals=0),
        name="all_here",
    )(*arrays)


def last_kernel(query_ref, k1_ref, v1_ref, k2_ref, v2_ref, old_mix_ref, old_stats_ref, message_ref, mix_ref, stats_ref):
    rows, width = k1_ref.shape
    wide = wide_window(query_ref, rows, 1)
    biases = [block_bias(wide_window(query_ref, rows), stage) for stage in (1, 2)]
    for head in range(width // HD):
        low = head * HD
        old = (old_stats_ref[2 * head], old_stats_ref[2 * head + 1], old_mix_ref[head])
        blocks = [(k1_ref, v1_ref), (k2_ref, v2_ref)]
        largest, total, mix = attend(query_ref[:rows, low : low + HD], blocks, biases, low, old)
        their_largest, their_total = message_columns(message_ref, head, rows)
        peak = jnp.maximum(largest, jnp.where(wide, their_largest, MASKED))
        shrink, share = jnp.exp2(largest - peak), jnp.where(wide, jnp.exp2(their_largest - peak), 0.0)
        stats = row_stats(peak, total * shrink + their_total * share)
        mix_ref[:, low : low + HD] = mix * shrink + message_ref[:rows, low : low + HD].astype(jnp.float32) * share
        line = lax.broadcasted_iota(jnp.int32, stats.shape, 0)
        stats_ref[head] = jnp.where(line == 2, jnp.where(wide, 1.0, 0.0), stats)


def attend_last(queries, first, second, mix, stats, message):
    rows, width = first[0].shape
    whole = pl.BlockSpec(memory_space=VMEM)
    return pl.pallas_call(
        last_kernel,
        out_shape=(
            jax.ShapeDtypeStruct((rows, width), jnp.float32),
            jax.ShapeDtypeStruct((width // HD, 8, rows), jnp.float32),
        ),
        in_specs=[whole] * 8,
        out_specs=(whole, whole),
        compiler_params=params(24),
        cost_estimate=pl.CostEstimate(flops=LAST_FLOPS, bytes_accessed=2_000_000, transcendentals=0),
        name="attend_last",
    )(queries, *first, *second, mix, stats, message)


def project_kernel(own_ref, stats_ref, middle_ref, weight_ref, out_ref):
    rows, width = own_ref.shape
    heads = width // HD
    height = lax.axis_index("tile") % HEIGHT_TILES
    inside = jnp.where((height > 0) & (height < HEIGHT_TILES - 1), 1.0, 0.0)
    line = lax.broadcasted_iota(jnp.int32, (8, rows), 0)
    shares = jnp.zeros((8, rows), jnp.float32)
    for head in range(heads):
        stats = stats_ref[head]
        their_largest, their_total = message_stats(middle_ref, head, rows)
        valid = stats[2:3] * inside > 0.5
        peak = jnp.maximum(stats[0:1], jnp.where(valid, their_largest, MASKED))
        shrink = jnp.exp2(stats[0:1] - peak)
        share = jnp.where(valid, jnp.exp2(their_largest - peak), 0.0)
        whole = stats[1:2] * shrink + their_total * share
        shares = jnp.where(line == 2 * head, shrink / whole, shares)
        shares = jnp.where(line == 2 * head + 1, share / whole, shares)
    shares = jnp.transpose(shares)
    merged = []
    for head in range(heads):
        low = head * HD
        value = own_ref[:, low : low + HD] * column(shares, 2 * head)
        value += middle_ref[:rows, low : low + HD].astype(jnp.float32) * column(shares, 2 * head + 1)
        merged.append(value.astype(jnp.bfloat16))
    attention = jnp.concatenate(merged, axis=1)
    for group in range(out_ref.shape[0]):
        out_ref[group] = jnp.dot(
            attention, weight_ref[:, group * width : (group + 1) * width], preferred_element_type=jnp.float32
        ).astype(out_ref.dtype)


def project(own, stats, middle, out_weight):
    rows, width = own.shape
    features = out_weight.shape[1]
    whole = pl.BlockSpec(memory_space=VMEM)
    return pl.pallas_call(
        project_kernel,
        out_shape=jax.ShapeDtypeStruct((features // width, rows, width), jnp.bfloat16),
        in_specs=[whole] * 4,
        out_specs=whole,
        compiler_params=params(24),
        cost_estimate=pl.CostEstimate(flops=2 * rows * width * features, bytes_accessed=5_000_000, transcendentals=0),
        name="project",
    )(own, stats, middle, out_weight)


def finish_kernel(terms_ref, residual_ref, gate_ref, out_ref):
    total = jnp.sum(terms_ref[...].astype(jnp.float32), axis=0)
    out_ref[...] = (residual_ref[...].astype(jnp.float32) + gate_ref[...] * total).astype(out_ref.dtype)


def finish(terms, residual, gate_scale):
    whole = pl.BlockSpec(memory_space=VMEM)
    return pl.pallas_call(
        finish_kernel,
        out_shape=jax.ShapeDtypeStruct(residual.shape, residual.dtype),
        in_specs=[whole] * 3,
        out_specs=whole,
        compiler_params=params(24),
        cost_estimate=pl.CostEstimate(flops=10 * terms.size, bytes_accessed=2_000_000, transcendentals=0),
        name="finish",
    )(terms, residual, gate_scale.reshape(1, -1))


def shards(queries, key_rows, value_rows, windows, residual, out_weight, gate_scale):
    own_block = (key_rows, value_rows)
    first, second = [[swap_times(array, later) for array in own_block] for later in (False, True)]
    packed = pack(windows, queries)
    blocks = (own_block, first, second)
    mix, stats, held_weight = attend_own(packed, own_block, out_weight)
    asked = swap_pair(packed), swap_middle(packed)
    for_pair = attend_neighbour(False, asked[0], blocks, (stats, all_here(first + second), asked[1]))
    for_middle = attend_neighbour(True, asked[1], blocks, (for_pair,))
    mix, stats = attend_last(packed, first, second, mix, stats, swap_pair(for_pair))
    terms = project(mix, stats, swap_middle(for_middle), held_weight)
    terms = lax.all_to_all(terms, "head", 0, 0)
    return finish(terms, residual, gate_scale)


def solution(mesh):
    return jax.shard_map(
        shards,
        mesh=mesh,
        in_specs=(
            P("tile", "head"),
            P("tile", "head"),
            P("tile", "head"),
            P("tile", None),
            P("tile", "head"),
            P("head", None),
            P("head"),
        ),
        out_specs=P("tile", "head"),
        check_vma=False,
    )
```

```python
import functools

import jax
import jax.numpy as jnp
from jax import lax
from jax.experimental import pallas as pl
from jax.experimental.pallas import tpu as pltpu
from jax.sharding import PartitionSpec as P

HD = 128
HEIGHT_TILES = 4
SIDE = 16
LOG2E = 1.4426950408889634
MASKED = -1e30
LAST_FLOPS = 400_000_000
MESH_AXES = ("tile", "head")
VMEM = pltpu.VMEM
SMEM = pltpu.SMEM


def params(megabytes):
    return pltpu.CompilerParams(vmem_limit_bytes=megabytes * 1024 * 1024)


def places():
    tiles = lax.axis_size("tile")
    return [(tile, *divmod(tile, HEIGHT_TILES), tiles // HEIGHT_TILES) for tile in range(tiles)]


def swap_times(block, later):
    route = []
    for tile, time, height, times in places():
        partner = time + 1 if time % 2 == int(not later) else time - 1
        if 0 <= partner < times:
            route.append((tile, partner * HEIGHT_TILES + height))
    return lax.ppermute(block, "tile", route)


def swap_pair(block):
    return lax.ppermute(block, "tile", [(tile, tile ^ 1) for tile, *_ in places()])


def swap_middle(block):
    route = [(tile, tile + (1 if height == 1 else -1)) for tile, _, height, _ in places() if height in (1, 2)]
    return lax.ppermute(block, "tile", route)


def pack_kernel(windows_ref, q_ref, k_ref, v_ref, packed_ref, block_ref):
    rows = q_ref.shape[0]
    block_ref[:rows] = k_ref[...]
    block_ref[rows:] = v_ref[...]
    packed_ref[:rows] = q_ref[...]
    for axis in (0, 1):
        extent = windows_ref[0, axis].astype(jnp.float32)
        packed_ref[rows:, axis * HD : (axis + 1) * HD] = jnp.full((SIDE, HD), extent, jnp.float32).astype(packed_ref.dtype)
    packed_ref[rows:, 2 * HD :] = jnp.zeros((SIDE, q_ref.shape[1] - 2 * HD), packed_ref.dtype)


def pack(windows, queries, key_rows, value_rows):
    rows, width = queries.shape
    whole = pl.BlockSpec(memory_space=VMEM)
    return pl.pallas_call(
        pack_kernel,
        out_shape=(
            jax.ShapeDtypeStruct((rows + SIDE, width), queries.dtype),
            jax.ShapeDtypeStruct((2 * rows, width), queries.dtype),
        ),
        in_specs=[pl.BlockSpec(memory_space=SMEM)] + [whole] * 3,
        out_specs=(whole, whole),
        name="pack",
    )(windows, queries, key_rows, value_rows)


def column(values, index):
    return values[:, index : index + 1]


def split_float(value):
    high = value.astype(jnp.bfloat16).astype(jnp.float32)
    rest = value - high
    middle = rest.astype(jnp.bfloat16).astype(jnp.float32)
    return high, middle, (rest - middle).astype(jnp.bfloat16).astype(jnp.float32)


def wide_window(ref, rows, axis=0):
    return jnp.max(ref[rows:, axis * HD : (axis + 1) * HD].astype(jnp.float32)) > 0.5


def has_first():
    time = lax.axis_index("tile") // HEIGHT_TILES
    return (time > 0) & (time < lax.axis_size("tile") // HEIGHT_TILES - 1)


def block_bias(wide, stage):
    return jnp.where(wide & has_first() if stage == 1 else wide, 0.0, MASKED)


def raw_scores(query, keys):
    return lax.dot_general(query, keys, (((1,), (1,)), ((), ())), preferred_element_type=jnp.float32)


def put_message(ref, head, mix, stats, row):
    rows = mix.shape[0]
    low = head * HD
    line = lax.broadcasted_iota(jnp.int32, (8, rows), 0)
    ref[:rows, low : low + HD] = mix.astype(ref.dtype)
    side = jnp.zeros((8, rows), jnp.float32)
    for index, piece in enumerate(split_float(stats[row : row + 1]) + split_float(stats[row + 1 : row + 2])):
        side = jnp.where(line == index, piece, side)
    ref[rows:, low : low + HD] = jnp.concatenate([side[:, :HD], side[:, HD:]], axis=0).astype(ref.dtype)


def message_stats(ref, head, rows):
    side = ref[rows:, head * HD : (head + 1) * HD].astype(jnp.float32)
    side = jnp.concatenate([side[:8], side[8:]], axis=1)
    return side[0:1] + side[1:2] + side[2:3], side[3:4] + side[4:5] + side[5:6]


def message_columns(ref, head, rows):
    line = lax.broadcasted_iota(jnp.int32, (8, rows), 0)
    largest, total = message_stats(ref, head, rows)
    columns = jnp.transpose(jnp.where(line == 0, largest, jnp.where(line == 1, total, 0.0)))
    return [jnp.broadcast_to(column(columns, index), (rows, HD)) for index in (0, 1)]


def attend(query, blocks, biases, low, old=None):
    rows = blocks[0].shape[0] // 2
    scale = HD**-0.5 * LOG2E
    spread = lambda value: jnp.broadcast_to(value, (rows, HD))
    parts = [raw_scores(query, block[:rows, low : low + HD]) for block in blocks]
    largest = None if old is None else old[0]
    for part, bias in zip(parts, biases):
        peak = spread(jnp.max(part, axis=1, keepdims=True)) * scale + bias
        largest = peak if largest is None else jnp.maximum(largest, peak)
    summed, mix = None, None
    for part, bias, block in zip(parts, biases, blocks):
        offset = jnp.concatenate([bias - largest] * (rows // HD), axis=1)
        weights = jnp.exp2(part * scale + offset)
        product = jnp.dot(weights.astype(block.dtype), block[rows:, low : low + HD], preferred_element_type=jnp.float32)
        summed = weights if summed is None else summed + weights
        mix = product if mix is None else mix + product
    total = spread(jnp.sum(summed, axis=1, keepdims=True))
    if old is not None:
        shrink = jnp.exp2(old[0] - largest)
        total, mix = total + old[1] * shrink, mix + old[2] * shrink
    return largest, total, mix


def row_stats(largest, total):
    lane = lax.broadcasted_iota(jnp.int32, largest.shape, 1)
    return jnp.transpose(jnp.where(lane == 0, largest, jnp.where(lane == 1, total, 0.0)))[:8]


def block_biases(query_ref, rows):
    wide = wide_window(query_ref, rows)
    return [block_bias(wide, stage) for stage in (1, 2)]


def own_kernel(query_ref, pair_ref, block_ref, weight_ref, mix_ref, stats_ref, held_ref, sem):
    copy = pltpu.make_async_copy(weight_ref, held_ref, sem)
    copy.start()
    rows, width = block_ref.shape[0] // 2, block_ref.shape[1]
    for place, ref in enumerate((query_ref, pair_ref)):
        for head in range(width // HD):
            low, index = head * HD, 2 * head + place
            largest, total, mix = attend(ref[:rows, low : low + HD], [block_ref], [0.0], low)
            mix_ref[index], stats_ref[2 * index], stats_ref[2 * index + 1] = mix, largest, total
    copy.wait()


def attend_own(queries, pair, block, out_weight):
    rows, width = block.shape[0] // 2, block.shape[1]
    heads = width // HD
    whole = pl.BlockSpec(memory_space=VMEM)
    return pl.pallas_call(
        own_kernel,
        out_shape=(
            jax.ShapeDtypeStruct((2 * heads, rows, HD), jnp.float32),
            jax.ShapeDtypeStruct((4 * heads, rows, HD), jnp.float32),
            jax.ShapeDtypeStruct(out_weight.shape, out_weight.dtype),
        ),
        in_specs=[whole] * 3 + [pl.BlockSpec(memory_space=pl.ANY)],
        out_specs=(whole,) * 3,
        scratch_shapes=[pltpu.SemaphoreType.DMA],
        compiler_params=params(24),
        cost_estimate=pl.CostEstimate(flops=0, bytes_accessed=0, transcendentals=0),
        name="attend_own",
    )(queries, pair, block, out_weight)


def old_parts(mix_ref, stats_ref, head, place):
    index = 2 * head + place
    return stats_ref[2 * index], stats_ref[2 * index + 1], mix_ref[index]


def neighbours_kernel(pair_ref, middle_ref, own_ref, first_ref, second_ref, mix_ref, stats_ref, for_pair_ref, for_middle_ref):
    rows, width = own_ref.shape[0] // 2, own_ref.shape[1]
    height = lax.axis_index("tile") % HEIGHT_TILES
    inside = (height > 0) & (height < HEIGHT_TILES - 1)
    biases = block_biases(pair_ref, rows)
    for head in range(width // HD):
        low = head * HD
        old = old_parts(mix_ref, stats_ref, head, 1)
        largest, total, mix = attend(pair_ref[:rows, low : low + HD], [first_ref, second_ref], biases, low, old)
        put_message(for_pair_ref, head, mix, row_stats(largest, total), 0)

    @pl.when(inside)
    def compute():
        biases = [0.0] + block_biases(middle_ref, rows)
        blocks = [own_ref, first_ref, second_ref]
        for head in range(width // HD):
            low = head * HD
            largest, total, mix = attend(middle_ref[:rows, low : low + HD], blocks, biases, low)
            put_message(for_middle_ref, head, mix, row_stats(largest, total), 0)

    @pl.when(jnp.logical_not(inside))
    def skip():
        for_middle_ref[...] = jnp.zeros_like(for_middle_ref)


def attend_neighbours(pair, middle, own, first, second, mix, stats):
    whole = pl.BlockSpec(memory_space=VMEM)
    shape = jax.ShapeDtypeStruct(pair.shape, jnp.bfloat16)
    return pl.pallas_call(
        neighbours_kernel,
        out_shape=(shape, shape),
        in_specs=[whole] * 7,
        out_specs=(whole, whole),
        compiler_params=params(24),
        cost_estimate=pl.CostEstimate(flops=1_000_000_000, bytes_accessed=2_000_000, transcendentals=0),
        name="attend_neighbours",
    )(pair, middle, own, first, second, mix, stats)


def last_kernel(query_ref, first_ref, second_ref, old_mix_ref, old_stats_ref, message_ref, mix_ref, stats_ref):
    rows, width = first_ref.shape[0] // 2, first_ref.shape[1]
    wide = wide_window(query_ref, rows, 1)
    biases = block_biases(query_ref, rows)
    for head in range(width // HD):
        low = head * HD
        old = old_parts(old_mix_ref, old_stats_ref, head, 0)
        largest, total, mix = attend(query_ref[:rows, low : low + HD], [first_ref, second_ref], biases, low, old)
        their_largest, their_total = message_columns(message_ref, head, rows)
        peak = jnp.maximum(largest, jnp.where(wide, their_largest, MASKED))
        shrink, share = jnp.exp2(largest - peak), jnp.where(wide, jnp.exp2(their_largest - peak), 0.0)
        stats = row_stats(peak, total * shrink + their_total * share)
        mix_ref[:, low : low + HD] = mix * shrink + message_ref[:rows, low : low + HD].astype(jnp.float32) * share
        line = lax.broadcasted_iota(jnp.int32, stats.shape, 0)
        stats_ref[head] = jnp.where(line == 2, jnp.where(wide, 1.0, 0.0), stats)


def attend_last(queries, first, second, mix, stats, message):
    rows, width = first.shape[0] // 2, first.shape[1]
    whole = pl.BlockSpec(memory_space=VMEM)
    return pl.pallas_call(
        last_kernel,
        out_shape=(
            jax.ShapeDtypeStruct((rows, width), jnp.float32),
            jax.ShapeDtypeStruct((width // HD, 8, rows), jnp.float32),
        ),
        in_specs=[whole] * 6,
        out_specs=(whole, whole),
        compiler_params=params(24),
        cost_estimate=pl.CostEstimate(flops=LAST_FLOPS, bytes_accessed=2_000_000, transcendentals=0),
        name="attend_last",
    )(queries, first, second, mix, stats, message)


def project_kernel(own_ref, stats_ref, middle_ref, weight_ref, out_ref, held_ref, sems):
    rows, width = own_ref.shape
    heads = width // HD
    height = lax.axis_index("tile") % HEIGHT_TILES
    inside = jnp.where((height > 0) & (height < HEIGHT_TILES - 1), 1.0, 0.0)
    line = lax.broadcasted_iota(jnp.int32, (8, rows), 0)
    shares = jnp.zeros((8, rows), jnp.float32)
    for head in range(heads):
        stats = stats_ref[head]
        their_largest, their_total = message_stats(middle_ref, head, rows)
        valid = stats[2:3] * inside > 0.5
        peak = jnp.maximum(stats[0:1], jnp.where(valid, their_largest, MASKED))
        shrink = jnp.exp2(stats[0:1] - peak)
        share = jnp.where(valid, jnp.exp2(their_largest - peak), 0.0)
        whole = stats[1:2] * shrink + their_total * share
        shares = jnp.where(line == 2 * head, shrink / whole, shares)
        shares = jnp.where(line == 2 * head + 1, share / whole, shares)
    shares = jnp.transpose(shares)
    merged = []
    for head in range(heads):
        low = head * HD
        value = own_ref[:, low : low + HD] * column(shares, 2 * head)
        value += middle_ref[:rows, low : low + HD].astype(jnp.float32) * column(shares, 2 * head + 1)
        merged.append(value.astype(jnp.bfloat16))
    attention = jnp.concatenate(merged, axis=1)
    copies = []
    for group in range(out_ref.shape[0]):
        held_ref[group] = jnp.dot(
            attention, weight_ref[:, group * width : (group + 1) * width], preferred_element_type=jnp.float32
        ).astype(held_ref.dtype)
        copies.append(pltpu.make_async_copy(held_ref.at[group], out_ref.at[group], sems.at[group]))
        copies[-1].start()
    for copy in copies:
        copy.wait()


def project(own, stats, middle, out_weight):
    rows, width = own.shape
    groups = out_weight.shape[1] // width
    whole = pl.BlockSpec(memory_space=VMEM)
    shape = (groups, rows, width)
    return pl.pallas_call(
        project_kernel,
        out_shape=jax.ShapeDtypeStruct(shape, jnp.bfloat16),
        in_specs=[whole] * 4,
        out_specs=pl.BlockSpec(memory_space=pl.ANY),
        scratch_shapes=[pltpu.VMEM(shape, jnp.bfloat16), pltpu.SemaphoreType.DMA((groups,))],
        compiler_params=params(24),
        cost_estimate=pl.CostEstimate(flops=2 * groups * rows * width * width, bytes_accessed=5_000_000, transcendentals=0),
        name="project",
    )(own, stats, middle, out_weight)


def finish_kernel(terms_ref, residual_ref, gate_ref, out_ref):
    total = jnp.sum(terms_ref[...].astype(jnp.float32), axis=0)
    out_ref[...] = (residual_ref[...].astype(jnp.float32) + gate_ref[...] * total).astype(out_ref.dtype)


def finish(terms, residual, gate_scale):
    whole = pl.BlockSpec(memory_space=VMEM)
    return pl.pallas_call(
        finish_kernel,
        out_shape=jax.ShapeDtypeStruct(residual.shape, residual.dtype),
        in_specs=[whole] * 3,
        out_specs=whole,
        compiler_params=params(24),
        cost_estimate=pl.CostEstimate(flops=10 * terms.size, bytes_accessed=2_000_000, transcendentals=0),
        name="finish",
    )(terms, residual, gate_scale.reshape(1, -1))


def shards(queries, key_rows, value_rows, windows, residual, out_weight, gate_scale):
    packed, block = pack(windows, queries, key_rows, value_rows)
    first, second = swap_times(block, False), swap_times(block, True)
    pair_asks, middle_asks = swap_pair(packed), swap_middle(packed)
    mix, stats, held_weight = attend_own(packed, pair_asks, block, out_weight)
    for_pair, for_middle = attend_neighbours(pair_asks, middle_asks, block, first, second, mix, stats)
    mix, stats = attend_last(packed, first, second, mix, stats, swap_pair(for_pair))
    terms = project(mix, stats, swap_middle(for_middle), held_weight)
    terms = lax.all_to_all(terms, "head", 0, 0)
    return finish(terms, residual, gate_scale)


def solution(mesh):
    return jax.shard_map(
        shards,
        mesh=mesh,
        in_specs=(
            P("tile", "head"),
            P("tile", "head"),
            P("tile", "head"),
            P("tile", None),
            P("tile", "head"),
            P("head", None),
            P("head"),
        ),
        out_specs=P("tile", "head"),
        check_vma=False,
    )
```

```python
import functools

import jax
import jax.numpy as jnp
from jax import lax
from jax.experimental import pallas as pl
from jax.experimental.pallas import tpu as pltpu
from jax.sharding import PartitionSpec as P

HD = 128
HEIGHT_TILES = 4
SIDE = 16
LOG2E = 1.4426950408889634
MASKED = -1e30
LAST_FLOPS = 400_000_000
MESH_AXES = ("tile", "head")
VMEM = pltpu.VMEM
SMEM = pltpu.SMEM


def params(megabytes):
    return pltpu.CompilerParams(vmem_limit_bytes=megabytes * 1024 * 1024)


def places():
    tiles = lax.axis_size("tile")
    return [(tile, *divmod(tile, HEIGHT_TILES), tiles // HEIGHT_TILES) for tile in range(tiles)]


def swap_times(block, later):
    route = []
    for tile, time, height, times in places():
        partner = time + 1 if time % 2 == int(not later) else time - 1
        if 0 <= partner < times:
            route.append((tile, partner * HEIGHT_TILES + height))
    return lax.ppermute(block, "tile", route)


def swap_pair(block):
    return lax.ppermute(block, "tile", [(tile, tile ^ 1) for tile, *_ in places()])


def swap_middle(block):
    route = [(tile, tile + (1 if height == 1 else -1)) for tile, _, height, _ in places() if height in (1, 2)]
    return lax.ppermute(block, "tile", route)


def pack_kernel(windows_ref, q_ref, k_ref, v_ref, packed_ref, block_ref):
    rows = q_ref.shape[0]
    block_ref[:rows] = k_ref[...]
    block_ref[rows:] = v_ref[...]
    packed_ref[:rows] = q_ref[...]
    for axis in (0, 1):
        extent = windows_ref[0, axis].astype(jnp.float32)
        packed_ref[rows:, axis * HD : (axis + 1) * HD] = jnp.full((SIDE, HD), extent, jnp.float32).astype(packed_ref.dtype)
    packed_ref[rows:, 2 * HD :] = jnp.zeros((SIDE, q_ref.shape[1] - 2 * HD), packed_ref.dtype)


def pack(windows, queries, key_rows, value_rows):
    rows, width = queries.shape
    whole = pl.BlockSpec(memory_space=VMEM)
    return pl.pallas_call(
        pack_kernel,
        out_shape=(
            jax.ShapeDtypeStruct((rows + SIDE, width), queries.dtype),
            jax.ShapeDtypeStruct((2 * rows, width), queries.dtype),
        ),
        in_specs=[pl.BlockSpec(memory_space=SMEM)] + [whole] * 3,
        out_specs=(whole, whole),
        name="pack",
    )(windows, queries, key_rows, value_rows)


def column(values, index):
    return values[:, index : index + 1]


def split_float(value):
    high = value.astype(jnp.bfloat16).astype(jnp.float32)
    rest = value - high
    middle = rest.astype(jnp.bfloat16).astype(jnp.float32)
    return high, middle, (rest - middle).astype(jnp.bfloat16).astype(jnp.float32)


def wide_window(ref, rows, axis=0):
    return jnp.max(ref[rows:, axis * HD : (axis + 1) * HD].astype(jnp.float32)) > 0.5


def has_first():
    time = lax.axis_index("tile") // HEIGHT_TILES
    return (time > 0) & (time < lax.axis_size("tile") // HEIGHT_TILES - 1)


def block_bias(wide, stage):
    return jnp.where(wide & has_first() if stage == 1 else wide, 0.0, MASKED)


def raw_scores(query, keys):
    return lax.dot_general(query, keys, (((1,), (1,)), ((), ())), preferred_element_type=jnp.float32)


def put_message(ref, head, mix, stats, row):
    rows = mix.shape[0]
    low = head * HD
    line = lax.broadcasted_iota(jnp.int32, (8, rows), 0)
    ref[:rows, low : low + HD] = mix.astype(ref.dtype)
    side = jnp.zeros((8, rows), jnp.float32)
    for index, piece in enumerate(split_float(stats[row : row + 1]) + split_float(stats[row + 1 : row + 2])):
        side = jnp.where(line == index, piece, side)
    ref[rows:, low : low + HD] = jnp.concatenate([side[:, :HD], side[:, HD:]], axis=0).astype(ref.dtype)


def message_stats(ref, head, rows):
    side = ref[rows:, head * HD : (head + 1) * HD].astype(jnp.float32)
    side = jnp.concatenate([side[:8], side[8:]], axis=1)
    return side[0:1] + side[1:2] + side[2:3], side[3:4] + side[4:5] + side[5:6]


def message_columns(ref, head, rows):
    line = lax.broadcasted_iota(jnp.int32, (8, rows), 0)
    largest, total = message_stats(ref, head, rows)
    columns = jnp.transpose(jnp.where(line == 0, largest, jnp.where(line == 1, total, 0.0)))
    return [jnp.broadcast_to(column(columns, index), (rows, HD)) for index in (0, 1)]


def attend(query, blocks, biases, low, old=None):
    rows = blocks[0].shape[0] // 2
    scale = HD**-0.5 * LOG2E
    spread = lambda value: jnp.broadcast_to(value, (rows, HD))
    parts = [raw_scores(query, block[:rows, low : low + HD]) for block in blocks]
    largest = None if old is None else old[0]
    for part, bias in zip(parts, biases):
        peak = spread(jnp.max(part, axis=1, keepdims=True)) * scale + bias
        largest = peak if largest is None else jnp.maximum(largest, peak)
    summed, mix = None, None
    for part, bias, block in zip(parts, biases, blocks):
        offset = jnp.concatenate([bias - largest] * (rows // HD), axis=1)
        weights = jnp.exp2(part * scale + offset)
        product = jnp.dot(weights.astype(block.dtype), block[rows:, low : low + HD], preferred_element_type=jnp.float32)
        summed = weights if summed is None else summed + weights
        mix = product if mix is None else mix + product
    total = spread(jnp.sum(summed, axis=1, keepdims=True))
    if old is not None:
        shrink = jnp.exp2(old[0] - largest)
        total, mix = total + old[1] * shrink, mix + old[2] * shrink
    return largest, total, mix


def row_stats(largest, total):
    lane = lax.broadcasted_iota(jnp.int32, largest.shape, 1)
    return jnp.transpose(jnp.where(lane == 0, largest, jnp.where(lane == 1, total, 0.0)))[:8]


def block_biases(query_ref, rows):
    wide = wide_window(query_ref, rows)
    return [block_bias(wide, stage) for stage in (1, 2)]


def own_kernel(query_ref, pair_ref, block_ref, weight_ref, mix_ref, stats_ref, held_ref, sem):
    copy = pltpu.make_async_copy(weight_ref, held_ref, sem)
    copy.start()
    rows, width = block_ref.shape[0] // 2, block_ref.shape[1]
    for place, ref in enumerate((query_ref, pair_ref)):
        for head in range(width // HD):
            low, index = head * HD, 2 * head + place
            largest, total, mix = attend(ref[:rows, low : low + HD], [block_ref], [0.0], low)
            mix_ref[index], stats_ref[2 * index], stats_ref[2 * index + 1] = mix, largest, total
    copy.wait()


def attend_own(queries, pair, block, out_weight):
    rows, width = block.shape[0] // 2, block.shape[1]
    heads = width // HD
    whole = pl.BlockSpec(memory_space=VMEM)
    return pl.pallas_call(
        own_kernel,
        out_shape=(
            jax.ShapeDtypeStruct((2 * heads, rows, HD), jnp.float32),
            jax.ShapeDtypeStruct((4 * heads, rows, HD), jnp.float32),
            jax.ShapeDtypeStruct(out_weight.shape, out_weight.dtype),
        ),
        in_specs=[whole] * 3 + [pl.BlockSpec(memory_space=pl.ANY)],
        out_specs=(whole,) * 3,
        scratch_shapes=[pltpu.SemaphoreType.DMA],
        compiler_params=params(24),
        cost_estimate=pl.CostEstimate(flops=0, bytes_accessed=0, transcendentals=0),
        name="attend_own",
    )(queries, pair, block, out_weight)


def old_parts(mix_ref, stats_ref, head, place):
    index = 2 * head + place
    return stats_ref[2 * index], stats_ref[2 * index + 1], mix_ref[index]


def pair_kernel(query_ref, first_ref, second_ref, mix_ref, stats_ref, out_ref):
    rows, width = first_ref.shape[0] // 2, first_ref.shape[1]
    biases = block_biases(query_ref, rows)
    for head in range(width // HD):
        low = head * HD
        old = old_parts(mix_ref, stats_ref, head, 1)
        largest, total, mix = attend(query_ref[:rows, low : low + HD], [first_ref, second_ref], biases, low, old)
        put_message(out_ref, head, mix, row_stats(largest, total), 0)


def attend_pair(query, first, second, mix, stats):
    whole = pl.BlockSpec(memory_space=VMEM)
    return pl.pallas_call(
        pair_kernel,
        out_shape=jax.ShapeDtypeStruct(query.shape, jnp.bfloat16),
        in_specs=[whole] * 5,
        out_specs=whole,
        compiler_params=params(24),
        cost_estimate=pl.CostEstimate(flops=400_000_000, bytes_accessed=2_000_000, transcendentals=0),
        name="attend_pair",
    )(query, first, second, mix, stats)


def middle_kernel(query_ref, own_ref, first_ref, second_ref, after_ref, out_ref):
    rows, width = own_ref.shape[0] // 2, own_ref.shape[1]
    height = lax.axis_index("tile") % HEIGHT_TILES
    inside = (height > 0) & (height < HEIGHT_TILES - 1)

    @pl.when(inside)
    def compute():
        biases = [0.0] + block_biases(query_ref, rows)
        blocks = [own_ref, first_ref, second_ref]
        for head in range(width // HD):
            low = head * HD
            largest, total, mix = attend(query_ref[:rows, low : low + HD], blocks, biases, low)
            put_message(out_ref, head, mix, row_stats(largest, total), 0)

    @pl.when(jnp.logical_not(inside))
    def skip():
        out_ref[...] = jnp.zeros_like(out_ref)


def attend_middle(query, own, first, second, after):
    whole = pl.BlockSpec(memory_space=VMEM)
    return pl.pallas_call(
        middle_kernel,
        out_shape=jax.ShapeDtypeStruct(query.shape, jnp.bfloat16),
        in_specs=[whole] * 4 + [pl.BlockSpec(memory_space=pl.ANY)],
        out_specs=whole,
        compiler_params=params(24),
        cost_estimate=pl.CostEstimate(flops=600_000_000, bytes_accessed=2_000_000, transcendentals=0),
        name="attend_middle",
    )(query, own, first, second, after)


def last_kernel(query_ref, first_ref, second_ref, old_mix_ref, old_stats_ref, message_ref, mix_ref, stats_ref):
    rows, width = first_ref.shape[0] // 2, first_ref.shape[1]
    wide = wide_window(query_ref, rows, 1)
    biases = block_biases(query_ref, rows)
    for head in range(width // HD):
        low = head * HD
        old = old_parts(old_mix_ref, old_stats_ref, head, 0)
        largest, total, mix = attend(query_ref[:rows, low : low + HD], [first_ref, second_ref], biases, low, old)
        their_largest, their_total = message_columns(message_ref, head, rows)
        peak = jnp.maximum(largest, jnp.where(wide, their_largest, MASKED))
        shrink, share = jnp.exp2(largest - peak), jnp.where(wide, jnp.exp2(their_largest - peak), 0.0)
        stats = row_stats(peak, total * shrink + their_total * share)
        mix_ref[:, low : low + HD] = mix * shrink + message_ref[:rows, low : low + HD].astype(jnp.float32) * share
        line = lax.broadcasted_iota(jnp.int32, stats.shape, 0)
        stats_ref[head] = jnp.where(line == 2, jnp.where(wide, 1.0, 0.0), stats)


def attend_last(queries, first, second, mix, stats, message):
    rows, width = first.shape[0] // 2, first.shape[1]
    whole = pl.BlockSpec(memory_space=VMEM)
    return pl.pallas_call(
        last_kernel,
        out_shape=(
            jax.ShapeDtypeStruct((rows, width), jnp.float32),
            jax.ShapeDtypeStruct((width // HD, 8, rows), jnp.float32),
        ),
        in_specs=[whole] * 6,
        out_specs=(whole, whole),
        compiler_params=params(24),
        cost_estimate=pl.CostEstimate(flops=LAST_FLOPS, bytes_accessed=2_000_000, transcendentals=0),
        name="attend_last",
    )(queries, first, second, mix, stats, message)


def project_kernel(own_ref, stats_ref, middle_ref, weight_ref, out_ref, held_ref, sems):
    rows, width = own_ref.shape
    heads = width // HD
    height = lax.axis_index("tile") % HEIGHT_TILES
    inside = jnp.where((height > 0) & (height < HEIGHT_TILES - 1), 1.0, 0.0)
    line = lax.broadcasted_iota(jnp.int32, (8, rows), 0)
    shares = jnp.zeros((8, rows), jnp.float32)
    for head in range(heads):
        stats = stats_ref[head]
        their_largest, their_total = message_stats(middle_ref, head, rows)
        valid = stats[2:3] * inside > 0.5
        peak = jnp.maximum(stats[0:1], jnp.where(valid, their_largest, MASKED))
        shrink = jnp.exp2(stats[0:1] - peak)
        share = jnp.where(valid, jnp.exp2(their_largest - peak), 0.0)
        whole = stats[1:2] * shrink + their_total * share
        shares = jnp.where(line == 2 * head, shrink / whole, shares)
        shares = jnp.where(line == 2 * head + 1, share / whole, shares)
    shares = jnp.transpose(shares)
    merged = []
    for head in range(heads):
        low = head * HD
        value = own_ref[:, low : low + HD] * column(shares, 2 * head)
        value += middle_ref[:rows, low : low + HD].astype(jnp.float32) * column(shares, 2 * head + 1)
        merged.append(value.astype(jnp.bfloat16))
    attention = jnp.concatenate(merged, axis=1)
    copies = []
    for group in range(out_ref.shape[0]):
        held_ref[group] = jnp.dot(
            attention, weight_ref[:, group * width : (group + 1) * width], preferred_element_type=jnp.float32
        ).astype(held_ref.dtype)
        copies.append(pltpu.make_async_copy(held_ref.at[group], out_ref.at[group], sems.at[group]))
        copies[-1].start()
    for copy in copies:
        copy.wait()


def project(own, stats, middle, out_weight):
    rows, width = own.shape
    groups = out_weight.shape[1] // width
    whole = pl.BlockSpec(memory_space=VMEM)
    shape = (groups, rows, width)
    return pl.pallas_call(
        project_kernel,
        out_shape=jax.ShapeDtypeStruct(shape, jnp.bfloat16),
        in_specs=[whole] * 4,
        out_specs=pl.BlockSpec(memory_space=pl.ANY),
        scratch_shapes=[pltpu.VMEM(shape, jnp.bfloat16), pltpu.SemaphoreType.DMA((groups,))],
        compiler_params=params(24),
        cost_estimate=pl.CostEstimate(flops=2 * groups * rows * width * width, bytes_accessed=5_000_000, transcendentals=0),
        name="project",
    )(own, stats, middle, out_weight)


def finish_kernel(terms_ref, residual_ref, gate_ref, out_ref):
    total = jnp.sum(terms_ref[...].astype(jnp.float32), axis=0)
    out_ref[...] = (residual_ref[...].astype(jnp.float32) + gate_ref[...] * total).astype(out_ref.dtype)


def finish(terms, residual, gate_scale):
    whole = pl.BlockSpec(memory_space=VMEM)
    return pl.pallas_call(
        finish_kernel,
        out_shape=jax.ShapeDtypeStruct(residual.shape, residual.dtype),
        in_specs=[whole] * 3,
        out_specs=whole,
        compiler_params=params(24),
        cost_estimate=pl.CostEstimate(flops=10 * terms.size, bytes_accessed=2_000_000, transcendentals=0),
        name="finish",
    )(terms, residual, gate_scale.reshape(1, -1))


def shards(queries, key_rows, value_rows, windows, residual, out_weight, gate_scale):
    packed, block = pack(windows, queries, key_rows, value_rows)
    first, second = swap_times(block, False), swap_times(block, True)
    pair_asks, middle_asks = swap_pair(packed), swap_middle(packed)
    mix, stats, held_weight = attend_own(packed, pair_asks, block, out_weight)
    for_pair = attend_pair(pair_asks, first, second, mix, stats)
    for_middle = attend_middle(middle_asks, block, first, second, for_pair)
    mix, stats = attend_last(packed, first, second, mix, stats, swap_pair(for_pair))
    terms = project(mix, stats, swap_middle(for_middle), held_weight)
    terms = lax.all_to_all(terms, "head", 0, 0)
    return finish(terms, residual, gate_scale)


def solution(mesh):
    return jax.shard_map(
        shards,
        mesh=mesh,
        in_specs=(
            P("tile", "head"),
            P("tile", "head"),
            P("tile", "head"),
            P("tile", None),
            P("tile", "head"),
            P("head", None),
            P("head"),
        ),
        out_specs=P("tile", "head"),
        check_vma=False,
    )
```

```python
import functools

import jax
import jax.numpy as jnp
from jax import lax
from jax.experimental import pallas as pl
from jax.experimental.pallas import tpu as pltpu
from jax.sharding import PartitionSpec as P

HD = 128
HEIGHT_TILES = 4
SIDE = 16
LOG2E = 1.4426950408889634
MASKED = -1e30
LAST_FLOPS = 400_000_000
MESH_AXES = ("tile", "head")
VMEM = pltpu.VMEM
SMEM = pltpu.SMEM


def params(megabytes):
    return pltpu.CompilerParams(vmem_limit_bytes=megabytes * 1024 * 1024)


def places():
    tiles = lax.axis_size("tile")
    return [(tile, *divmod(tile, HEIGHT_TILES), tiles // HEIGHT_TILES) for tile in range(tiles)]


def swap_times(block, later):
    route = []
    for tile, time, height, times in places():
        partner = time + 1 if time % 2 == int(not later) else time - 1
        if 0 <= partner < times:
            route.append((tile, partner * HEIGHT_TILES + height))
    return lax.ppermute(block, "tile", route)


def swap_pair(block):
    return lax.ppermute(block, "tile", [(tile, tile ^ 1) for tile, *_ in places()])


def swap_middle(block):
    route = [(tile, tile + (1 if height == 1 else -1)) for tile, _, height, _ in places() if height in (1, 2)]
    return lax.ppermute(block, "tile", route)


def pack_kernel(windows_ref, q_ref, k_ref, v_ref, packed_ref, block_ref):
    rows = q_ref.shape[0]
    block_ref[:rows] = k_ref[...]
    block_ref[rows:] = v_ref[...]
    packed_ref[:rows] = q_ref[...]
    for axis in (0, 1):
        extent = windows_ref[0, axis].astype(jnp.float32)
        packed_ref[rows:, axis * HD : (axis + 1) * HD] = jnp.full((SIDE, HD), extent, jnp.float32).astype(packed_ref.dtype)
    packed_ref[rows:, 2 * HD :] = jnp.zeros((SIDE, q_ref.shape[1] - 2 * HD), packed_ref.dtype)


def pack(windows, queries, key_rows, value_rows):
    rows, width = queries.shape
    whole = pl.BlockSpec(memory_space=VMEM)
    return pl.pallas_call(
        pack_kernel,
        out_shape=(
            jax.ShapeDtypeStruct((rows + SIDE, width), queries.dtype),
            jax.ShapeDtypeStruct((2 * rows, width), queries.dtype),
        ),
        in_specs=[pl.BlockSpec(memory_space=SMEM)] + [whole] * 3,
        out_specs=(whole, whole),
        name="pack",
    )(windows, queries, key_rows, value_rows)


def column(values, index):
    return values[:, index : index + 1]


def split_float(value):
    high = value.astype(jnp.bfloat16).astype(jnp.float32)
    rest = value - high
    middle = rest.astype(jnp.bfloat16).astype(jnp.float32)
    return high, middle, (rest - middle).astype(jnp.bfloat16).astype(jnp.float32)


def wide_window(ref, rows, axis=0):
    return jnp.max(ref[rows:, axis * HD : (axis + 1) * HD].astype(jnp.float32)) > 0.5


def has_first():
    time = lax.axis_index("tile") // HEIGHT_TILES
    return (time > 0) & (time < lax.axis_size("tile") // HEIGHT_TILES - 1)


def block_bias(wide, stage):
    return jnp.where(wide & has_first() if stage == 1 else wide, 0.0, MASKED)


def raw_scores(query, keys):
    return lax.dot_general(query, keys, (((1,), (1,)), ((), ())), preferred_element_type=jnp.float32)


def put_message(ref, head, mix, stats, row):
    rows = mix.shape[0]
    low = head * HD
    line = lax.broadcasted_iota(jnp.int32, (8, rows), 0)
    ref[:rows, low : low + HD] = mix.astype(ref.dtype)
    side = jnp.zeros((8, rows), jnp.float32)
    for index, piece in enumerate(split_float(stats[row : row + 1]) + split_float(stats[row + 1 : row + 2])):
        side = jnp.where(line == index, piece, side)
    ref[rows:, low : low + HD] = jnp.concatenate([side[:, :HD], side[:, HD:]], axis=0).astype(ref.dtype)


def message_stats(ref, head, rows):
    side = ref[rows:, head * HD : (head + 1) * HD].astype(jnp.float32)
    side = jnp.concatenate([side[:8], side[8:]], axis=1)
    return side[0:1] + side[1:2] + side[2:3], side[3:4] + side[4:5] + side[5:6]


def message_columns(ref, head, rows):
    line = lax.broadcasted_iota(jnp.int32, (8, rows), 0)
    largest, total = message_stats(ref, head, rows)
    columns = jnp.transpose(jnp.where(line == 0, largest, jnp.where(line == 1, total, 0.0)))
    return [jnp.broadcast_to(column(columns, index), (rows, HD)) for index in (0, 1)]


def attend(query, blocks, biases, low, old=None):
    rows = blocks[0].shape[0] // 2
    scale = HD**-0.5 * LOG2E
    spread = lambda value: jnp.broadcast_to(value, (rows, HD))
    parts = [raw_scores(query, block[:rows, low : low + HD]) for block in blocks]
    largest = None if old is None else old[0]
    for part, bias in zip(parts, biases):
        peak = spread(jnp.max(part, axis=1, keepdims=True)) * scale + bias
        largest = peak if largest is None else jnp.maximum(largest, peak)
    summed, mix = None, None
    for part, bias, block in zip(parts, biases, blocks):
        offset = jnp.concatenate([bias - largest] * (rows // HD), axis=1)
        weights = jnp.exp2(part * scale + offset)
        product = jnp.dot(weights.astype(block.dtype), block[rows:, low : low + HD], preferred_element_type=jnp.float32)
        summed = weights if summed is None else summed + weights
        mix = product if mix is None else mix + product
    total = spread(jnp.sum(summed, axis=1, keepdims=True))
    if old is not None:
        shrink = jnp.exp2(old[0] - largest)
        total, mix = total + old[1] * shrink, mix + old[2] * shrink
    return largest, total, mix


def row_stats(largest, total):
    lane = lax.broadcasted_iota(jnp.int32, largest.shape, 1)
    return jnp.transpose(jnp.where(lane == 0, largest, jnp.where(lane == 1, total, 0.0)))[:8]


def block_biases(query_ref, rows):
    wide = wide_window(query_ref, rows)
    return [block_bias(wide, stage) for stage in (1, 2)]


def own_kernel(query_ref, pair_ref, block_ref, weight_ref, mix_ref, stats_ref, held_ref, sem):
    copy = pltpu.make_async_copy(weight_ref, held_ref, sem)
    copy.start()
    rows, width = block_ref.shape[0] // 2, block_ref.shape[1]
    for place, ref in enumerate((query_ref, pair_ref)):
        for head in range(width // HD):
            low, index = head * HD, 2 * head + place
            largest, total, mix = attend(ref[:rows, low : low + HD], [block_ref], [0.0], low)
            mix_ref[index], stats_ref[2 * index], stats_ref[2 * index + 1] = mix, largest, total
    copy.wait()


def attend_own(queries, pair, block, out_weight):
    rows, width = block.shape[0] // 2, block.shape[1]
    heads = width // HD
    whole = pl.BlockSpec(memory_space=VMEM)
    return pl.pallas_call(
        own_kernel,
        out_shape=(
            jax.ShapeDtypeStruct((2 * heads, rows, HD), jnp.float32),
            jax.ShapeDtypeStruct((4 * heads, rows, HD), jnp.float32),
            jax.ShapeDtypeStruct(out_weight.shape, out_weight.dtype),
        ),
        in_specs=[whole] * 3 + [pl.BlockSpec(memory_space=pl.ANY)],
        out_specs=(whole,) * 3,
        scratch_shapes=[pltpu.SemaphoreType.DMA],
        compiler_params=params(24),
        cost_estimate=pl.CostEstimate(flops=0, bytes_accessed=0, transcendentals=0),
        name="attend_own",
    )(queries, pair, block, out_weight)


def old_parts(mix_ref, stats_ref, head, place):
    index = 2 * head + place
    return stats_ref[2 * index], stats_ref[2 * index + 1], mix_ref[index]


def pair_kernel(query_ref, first_ref, second_ref, mix_ref, stats_ref, out_ref):
    rows, width = first_ref.shape[0] // 2, first_ref.shape[1]
    biases = block_biases(query_ref, rows)
    for head in range(width // HD):
        low = head * HD
        old = old_parts(mix_ref, stats_ref, head, 1)
        largest, total, mix = attend(query_ref[:rows, low : low + HD], [first_ref, second_ref], biases, low, old)
        put_message(out_ref, head, mix, row_stats(largest, total), 0)


def attend_pair(query, first, second, mix, stats):
    whole = pl.BlockSpec(memory_space=VMEM)
    return pl.pallas_call(
        pair_kernel,
        out_shape=jax.ShapeDtypeStruct(query.shape, jnp.bfloat16),
        in_specs=[whole] * 5,
        out_specs=whole,
        compiler_params=params(24),
        cost_estimate=pl.CostEstimate(flops=400_000_000, bytes_accessed=2_000_000, transcendentals=0),
        name="attend_pair",
    )(query, first, second, mix, stats)


def middle_kernel(query_ref, own_ref, first_ref, second_ref, pair_ref, out_ref, same_pair_ref):
    same_pair_ref[...] = pair_ref[...]
    rows, width = own_ref.shape[0] // 2, own_ref.shape[1]
    height = lax.axis_index("tile") % HEIGHT_TILES
    inside = (height > 0) & (height < HEIGHT_TILES - 1)

    @pl.when(inside)
    def compute():
        biases = [0.0] + block_biases(query_ref, rows)
        blocks = [own_ref, first_ref, second_ref]
        for head in range(width // HD):
            low = head * HD
            largest, total, mix = attend(query_ref[:rows, low : low + HD], blocks, biases, low)
            put_message(out_ref, head, mix, row_stats(largest, total), 0)

    @pl.when(jnp.logical_not(inside))
    def skip():
        out_ref[...] = jnp.zeros_like(out_ref)


def attend_middle(query, own, first, second, for_pair):
    whole = pl.BlockSpec(memory_space=VMEM)
    return pl.pallas_call(
        middle_kernel,
        out_shape=(jax.ShapeDtypeStruct(query.shape, jnp.bfloat16),) * 2,
        in_specs=[whole] * 5,
        out_specs=(whole, whole),
        compiler_params=params(24),
        cost_estimate=pl.CostEstimate(flops=600_000_000, bytes_accessed=2_000_000, transcendentals=0),
        name="attend_middle",
    )(query, own, first, second, for_pair)


def last_kernel(query_ref, first_ref, second_ref, old_mix_ref, old_stats_ref, message_ref, mix_ref, stats_ref):
    rows, width = first_ref.shape[0] // 2, first_ref.shape[1]
    wide = wide_window(query_ref, rows, 1)
    biases = block_biases(query_ref, rows)
    for head in range(width // HD):
        low = head * HD
        old = old_parts(old_mix_ref, old_stats_ref, head, 0)
        largest, total, mix = attend(query_ref[:rows, low : low + HD], [first_ref, second_ref], biases, low, old)
        their_largest, their_total = message_columns(message_ref, head, rows)
        peak = jnp.maximum(largest, jnp.where(wide, their_largest, MASKED))
        shrink, share = jnp.exp2(largest - peak), jnp.where(wide, jnp.exp2(their_largest - peak), 0.0)
        stats = row_stats(peak, total * shrink + their_total * share)
        mix_ref[:, low : low + HD] = mix * shrink + message_ref[:rows, low : low + HD].astype(jnp.float32) * share
        line = lax.broadcasted_iota(jnp.int32, stats.shape, 0)
        stats_ref[head] = jnp.where(line == 2, jnp.where(wide, 1.0, 0.0), stats)


def attend_last(queries, first, second, mix, stats, message):
    rows, width = first.shape[0] // 2, first.shape[1]
    whole = pl.BlockSpec(memory_space=VMEM)
    return pl.pallas_call(
        last_kernel,
        out_shape=(
            jax.ShapeDtypeStruct((rows, width), jnp.float32),
            jax.ShapeDtypeStruct((width // HD, 8, rows), jnp.float32),
        ),
        in_specs=[whole] * 6,
        out_specs=(whole, whole),
        compiler_params=params(24),
        cost_estimate=pl.CostEstimate(flops=LAST_FLOPS, bytes_accessed=2_000_000, transcendentals=0),
        name="attend_last",
    )(queries, first, second, mix, stats, message)


def project_kernel(own_ref, stats_ref, middle_ref, weight_ref, out_ref, held_ref, sems):
    rows, width = own_ref.shape
    heads = width // HD
    height = lax.axis_index("tile") % HEIGHT_TILES
    inside = jnp.where((height > 0) & (height < HEIGHT_TILES - 1), 1.0, 0.0)
    line = lax.broadcasted_iota(jnp.int32, (8, rows), 0)
    shares = jnp.zeros((8, rows), jnp.float32)
    for head in range(heads):
        stats = stats_ref[head]
        their_largest, their_total = message_stats(middle_ref, head, rows)
        valid = stats[2:3] * inside > 0.5
        peak = jnp.maximum(stats[0:1], jnp.where(valid, their_largest, MASKED))
        shrink = jnp.exp2(stats[0:1] - peak)
        share = jnp.where(valid, jnp.exp2(their_largest - peak), 0.0)
        whole = stats[1:2] * shrink + their_total * share
        shares = jnp.where(line == 2 * head, shrink / whole, shares)
        shares = jnp.where(line == 2 * head + 1, share / whole, shares)
    shares = jnp.transpose(shares)
    merged = []
    for head in range(heads):
        low = head * HD
        value = own_ref[:, low : low + HD] * column(shares, 2 * head)
        value += middle_ref[:rows, low : low + HD].astype(jnp.float32) * column(shares, 2 * head + 1)
        merged.append(value.astype(jnp.bfloat16))
    attention = jnp.concatenate(merged, axis=1)
    copies = []
    for group in range(out_ref.shape[0]):
        held_ref[group] = jnp.dot(
            attention, weight_ref[:, group * width : (group + 1) * width], preferred_element_type=jnp.float32
        ).astype(held_ref.dtype)
        copies.append(pltpu.make_async_copy(held_ref.at[group], out_ref.at[group], sems.at[group]))
        copies[-1].start()
    for copy in copies:
        copy.wait()


def project(own, stats, middle, out_weight):
    rows, width = own.shape
    groups = out_weight.shape[1] // width
    whole = pl.BlockSpec(memory_space=VMEM)
    shape = (groups, rows, width)
    return pl.pallas_call(
        project_kernel,
        out_shape=jax.ShapeDtypeStruct(shape, jnp.bfloat16),
        in_specs=[whole] * 4,
        out_specs=pl.BlockSpec(memory_space=pl.ANY),
        scratch_shapes=[pltpu.VMEM(shape, jnp.bfloat16), pltpu.SemaphoreType.DMA((groups,))],
        compiler_params=params(24),
        cost_estimate=pl.CostEstimate(flops=2 * groups * rows * width * width, bytes_accessed=5_000_000, transcendentals=0),
        name="project",
    )(own, stats, middle, out_weight)


def finish_kernel(terms_ref, residual_ref, gate_ref, out_ref):
    total = jnp.sum(terms_ref[...].astype(jnp.float32), axis=0)
    out_ref[...] = (residual_ref[...].astype(jnp.float32) + gate_ref[...] * total).astype(out_ref.dtype)


def finish(terms, residual, gate_scale):
    whole = pl.BlockSpec(memory_space=VMEM)
    return pl.pallas_call(
        finish_kernel,
        out_shape=jax.ShapeDtypeStruct(residual.shape, residual.dtype),
        in_specs=[whole] * 3,
        out_specs=whole,
        compiler_params=params(24),
        cost_estimate=pl.CostEstimate(flops=10 * terms.size, bytes_accessed=2_000_000, transcendentals=0),
        name="finish",
    )(terms, residual, gate_scale.reshape(1, -1))


def shards(queries, key_rows, value_rows, windows, residual, out_weight, gate_scale):
    packed, block = pack(windows, queries, key_rows, value_rows)
    first, second = swap_times(block, False), swap_times(block, True)
    pair_asks, middle_asks = swap_pair(packed), swap_middle(packed)
    mix, stats, held_weight = attend_own(packed, pair_asks, block, out_weight)
    for_pair = attend_pair(pair_asks, first, second, mix, stats)
    for_middle, for_pair = attend_middle(middle_asks, block, first, second, for_pair)
    mix, stats = attend_last(packed, first, second, mix, stats, swap_pair(for_pair))
    terms = project(mix, stats, swap_middle(for_middle), held_weight)
    terms = lax.all_to_all(terms, "head", 0, 0)
    return finish(terms, residual, gate_scale)


def solution(mesh):
    return jax.shard_map(
        shards,
        mesh=mesh,
        in_specs=(
            P("tile", "head"),
            P("tile", "head"),
            P("tile", "head"),
            P("tile", None),
            P("tile", "head"),
            P("head", None),
            P("head"),
        ),
        out_specs=P("tile", "head"),
        check_vma=False,
    )
```

```python
import functools

import jax
import jax.numpy as jnp
import numpy as np
from jax import lax
from jax.experimental import pallas as pl
from jax.experimental.pallas import tpu as pltpu
from jax.sharding import PartitionSpec as P

HD = 128
HEIGHT_TILES = 4
SIDE = 16
LOG2E = 1.4426950408889634
MASKED = -1e30
LAST_FLOPS = 8_000_000_000
MESH_AXES = ("tile", "head")
VMEM = pltpu.VMEM
SMEM = pltpu.SMEM


def params(megabytes):
    return pltpu.CompilerParams(vmem_limit_bytes=megabytes * 1024 * 1024)


def places():
    tiles = lax.axis_size("tile")
    return [(tile, *divmod(tile, HEIGHT_TILES), tiles // HEIGHT_TILES) for tile in range(tiles)]


def swap_times(block, later):
    route = []
    for tile, time, height, times in places():
        partner = time + 1 if time % 2 == int(not later) else time - 1
        if 0 <= partner < times:
            route.append((tile, partner * HEIGHT_TILES + height))
    return lax.ppermute(block, "tile", route)


def swap_pair(block):
    return lax.ppermute(block, "tile", [(tile, tile ^ 1) for tile, *_ in places()])


def swap_middle(block):
    route = [(tile, tile + (1 if height == 1 else -1)) for tile, _, height, _ in places() if height in (1, 2)]
    return lax.ppermute(block, "tile", route)


def swap_far(block):
    return lax.ppermute(block, "far", [(0, 1), (1, 0)])


def split_weight_kernel(weight_ref, mine_ref, theirs_ref):
    width = mine_ref.shape[1]
    far = lax.axis_index("far")
    mine_ref[...] = weight_ref[:, pl.ds(pl.multiple_of(far * width, HD), width)]
    theirs_ref[...] = weight_ref[:, pl.ds(pl.multiple_of((1 - far) * width, HD), width)]


def split_weight(out_weight):
    rows, features = out_weight.shape
    whole = pl.BlockSpec(memory_space=VMEM)
    return pl.pallas_call(
        split_weight_kernel,
        out_shape=(jax.ShapeDtypeStruct((rows, features // 2), out_weight.dtype),) * 2,
        in_specs=[whole],
        out_specs=(whole,) * 2,
        compiler_params=params(24),
        cost_estimate=pl.CostEstimate(flops=0, bytes_accessed=0, transcendentals=0),
        name="split_weight",
    )(out_weight)


def pack_kernel(windows_ref, q_ref, k_ref, v_ref, packed_ref, block_ref):
    rows = q_ref.shape[0]
    block_ref[:rows] = k_ref[...]
    block_ref[rows:] = v_ref[...]
    packed_ref[:rows] = q_ref[...]
    for axis in (0, 1):
        extent = windows_ref[0, axis].astype(jnp.float32)
        packed_ref[rows:, axis * HD : (axis + 1) * HD] = jnp.full((SIDE, HD), extent, jnp.float32).astype(packed_ref.dtype)
    packed_ref[rows:, 2 * HD :] = jnp.zeros((SIDE, q_ref.shape[1] - 2 * HD), packed_ref.dtype)


def pack(windows, queries, key_rows, value_rows):
    rows, width = queries.shape
    whole = pl.BlockSpec(memory_space=VMEM)
    return pl.pallas_call(
        pack_kernel,
        out_shape=(
            jax.ShapeDtypeStruct((rows + SIDE, width), queries.dtype),
            jax.ShapeDtypeStruct((2 * rows, width), queries.dtype),
        ),
        in_specs=[pl.BlockSpec(memory_space=SMEM)] + [whole] * 3,
        out_specs=(whole, whole),
        name="pack",
    )(windows, queries, key_rows, value_rows)


def column(values, index):
    return values[:, index : index + 1]


def split_float(value):
    high = value.astype(jnp.bfloat16).astype(jnp.float32)
    rest = value - high
    middle = rest.astype(jnp.bfloat16).astype(jnp.float32)
    return high, middle, (rest - middle).astype(jnp.bfloat16).astype(jnp.float32)


def wide_window(ref, rows, axis=0):
    return jnp.max(ref[rows:, axis * HD : (axis + 1) * HD].astype(jnp.float32)) > 0.5


def has_first():
    time = lax.axis_index("tile") // HEIGHT_TILES
    return (time > 0) & (time < lax.axis_size("tile") // HEIGHT_TILES - 1)


def block_bias(wide, stage):
    return jnp.where(wide & has_first() if stage == 1 else wide, 0.0, MASKED)


def raw_scores(query, keys):
    return lax.dot_general(query, keys, (((1,), (1,)), ((), ())), preferred_element_type=jnp.float32)


def put_message(ref, head, mix, stats, row):
    rows = mix.shape[0]
    low = head * HD
    line = lax.broadcasted_iota(jnp.int32, (8, rows), 0)
    ref[:rows, low : low + HD] = mix.astype(ref.dtype)
    side = jnp.zeros((8, rows), jnp.float32)
    for index, piece in enumerate(split_float(stats[row : row + 1]) + split_float(stats[row + 1 : row + 2])):
        side = jnp.where(line == index, piece, side)
    ref[rows:, low : low + HD] = jnp.concatenate([side[:, :HD], side[:, HD:]], axis=0).astype(ref.dtype)


def message_stats(ref, head, rows):
    side = ref[rows:, head * HD : (head + 1) * HD].astype(jnp.float32)
    side = jnp.concatenate([side[:8], side[8:]], axis=1)
    return side[0:1] + side[1:2] + side[2:3], side[3:4] + side[4:5] + side[5:6]


def message_columns(ref, head, rows):
    line = lax.broadcasted_iota(jnp.int32, (8, rows), 0)
    largest, total = message_stats(ref, head, rows)
    columns = jnp.transpose(jnp.where(line == 0, largest, jnp.where(line == 1, total, 0.0)))
    return [jnp.broadcast_to(column(columns, index), (rows, HD)) for index in (0, 1)]


def attend(query, blocks, biases, low, old=None):
    rows = blocks[0].shape[0] // 2
    scale = HD**-0.5 * LOG2E
    spread = lambda value: jnp.broadcast_to(value, (rows, HD))
    parts = [raw_scores(query, block[:rows, low : low + HD]) for block in blocks]
    largest = None if old is None else old[0]
    for part, bias in zip(parts, biases):
        peak = spread(jnp.max(part, axis=1, keepdims=True)) * scale + bias
        largest = peak if largest is None else jnp.maximum(largest, peak)
    summed, mix = None, None
    for part, bias, block in zip(parts, biases, blocks):
        offset = jnp.concatenate([bias - largest] * (rows // HD), axis=1)
        weights = jnp.exp2(part * scale + offset)
        product = jnp.dot(weights.astype(block.dtype), block[rows:, low : low + HD], preferred_element_type=jnp.float32)
        summed = weights if summed is None else summed + weights
        mix = product if mix is None else mix + product
    total = spread(jnp.sum(summed, axis=1, keepdims=True))
    if old is not None:
        shrink = jnp.exp2(old[0] - largest)
        total, mix = total + old[1] * shrink, mix + old[2] * shrink
    return largest, total, mix


def row_stats(largest, total):
    lane = lax.broadcasted_iota(jnp.int32, largest.shape, 1)
    return jnp.transpose(jnp.where(lane == 0, largest, jnp.where(lane == 1, total, 0.0)))[:8]


def block_biases(query_ref, rows):
    wide = wide_window(query_ref, rows)
    return [block_bias(wide, stage) for stage in (1, 2)]


def own_kernel(query_ref, pair_ref, block_ref, mix_ref, stats_ref):
    rows, width = block_ref.shape[0] // 2, block_ref.shape[1]
    for place, ref in enumerate((query_ref, pair_ref)):
        for head in range(width // HD):
            low, index = head * HD, 2 * head + place
            largest, total, mix = attend(ref[:rows, low : low + HD], [block_ref], [0.0], low)
            mix_ref[index], stats_ref[2 * index], stats_ref[2 * index + 1] = mix, largest, total


def attend_own(queries, pair, block):
    rows, width = block.shape[0] // 2, block.shape[1]
    heads = width // HD
    whole = pl.BlockSpec(memory_space=VMEM)
    return pl.pallas_call(
        own_kernel,
        out_shape=(
            jax.ShapeDtypeStruct((2 * heads, rows, HD), jnp.float32),
            jax.ShapeDtypeStruct((4 * heads, rows, HD), jnp.float32),
        ),
        in_specs=[whole] * 3,
        out_specs=(whole,) * 2,
        compiler_params=params(24),
        cost_estimate=pl.CostEstimate(flops=0, bytes_accessed=0, transcendentals=0),
        name="attend_own",
    )(queries, pair, block)


def old_parts(mix_ref, stats_ref, head, place):
    index = 2 * head + place
    return stats_ref[2 * index], stats_ref[2 * index + 1], mix_ref[index]


def pair_kernel(query_ref, first_ref, second_ref, mix_ref, stats_ref, out_ref):
    rows, width = first_ref.shape[0] // 2, first_ref.shape[1]
    biases = block_biases(query_ref, rows)
    for head in range(width // HD):
        low = head * HD
        old = old_parts(mix_ref, stats_ref, head, 1)
        largest, total, mix = attend(query_ref[:rows, low : low + HD], [first_ref, second_ref], biases, low, old)
        put_message(out_ref, head, mix, row_stats(largest, total), 0)


def attend_pair(query, first, second, mix, stats):
    whole = pl.BlockSpec(memory_space=VMEM)
    return pl.pallas_call(
        pair_kernel,
        out_shape=jax.ShapeDtypeStruct(query.shape, jnp.bfloat16),
        in_specs=[whole] * 5,
        out_specs=whole,
        compiler_params=params(24),
        cost_estimate=pl.CostEstimate(flops=400_000_000, bytes_accessed=2_000_000, transcendentals=0),
        name="attend_pair",
    )(query, first, second, mix, stats)


def middle_kernel(query_ref, own_ref, first_ref, second_ref, after_ref, out_ref):
    rows, width = own_ref.shape[0] // 2, own_ref.shape[1]
    height = lax.axis_index("tile") % HEIGHT_TILES
    inside = (height > 0) & (height < HEIGHT_TILES - 1)

    @pl.when(inside)
    def compute():
        biases = [0.0] + block_biases(query_ref, rows)
        blocks = [own_ref, first_ref, second_ref]
        for head in range(width // HD):
            low = head * HD
            largest, total, mix = attend(query_ref[:rows, low : low + HD], blocks, biases, low)
            put_message(out_ref, head, mix, row_stats(largest, total), 0)

    @pl.when(jnp.logical_not(inside))
    def skip():
        out_ref[...] = jnp.zeros_like(out_ref)


def attend_middle(query, own, first, second, after):
    whole = pl.BlockSpec(memory_space=VMEM)
    return pl.pallas_call(
        middle_kernel,
        out_shape=jax.ShapeDtypeStruct(query.shape, jnp.bfloat16),
        in_specs=[whole] * 4 + [pl.BlockSpec(memory_space=pl.ANY)],
        out_specs=whole,
        compiler_params=params(24),
        cost_estimate=pl.CostEstimate(flops=600_000_000, bytes_accessed=2_000_000, transcendentals=0),
        name="attend_middle",
    )(query, own, first, second, after)


def last_kernel(query_ref, first_ref, second_ref, old_mix_ref, old_stats_ref, message_ref, mix_ref, stats_ref):
    rows, width = first_ref.shape[0] // 2, first_ref.shape[1]
    wide = wide_window(query_ref, rows, 1)
    biases = block_biases(query_ref, rows)
    for head in range(width // HD):
        low = head * HD
        old = old_parts(old_mix_ref, old_stats_ref, head, 0)
        largest, total, mix = attend(query_ref[:rows, low : low + HD], [first_ref, second_ref], biases, low, old)
        their_largest, their_total = message_columns(message_ref, head, rows)
        peak = jnp.maximum(largest, jnp.where(wide, their_largest, MASKED))
        shrink, share = jnp.exp2(largest - peak), jnp.where(wide, jnp.exp2(their_largest - peak), 0.0)
        stats = row_stats(peak, total * shrink + their_total * share)
        mix_ref[:, low : low + HD] = mix * shrink + message_ref[:rows, low : low + HD].astype(jnp.float32) * share
        line = lax.broadcasted_iota(jnp.int32, stats.shape, 0)
        stats_ref[head] = jnp.where(line == 2, jnp.where(wide, 1.0, 0.0), stats)


def attend_last(queries, first, second, mix, stats, message):
    rows, width = first.shape[0] // 2, first.shape[1]
    whole = pl.BlockSpec(memory_space=VMEM)
    return pl.pallas_call(
        last_kernel,
        out_shape=(
            jax.ShapeDtypeStruct((rows, width), jnp.float32),
            jax.ShapeDtypeStruct((width // HD, 8, rows), jnp.float32),
        ),
        in_specs=[whole] * 6,
        out_specs=(whole, whole),
        compiler_params=params(24),
        cost_estimate=pl.CostEstimate(flops=LAST_FLOPS, bytes_accessed=2_000_000, transcendentals=0),
        name="attend_last",
    )(queries, first, second, mix, stats, message)


def merge_kernel(own_ref, stats_ref, middle_ref, out_ref):
    rows, width = own_ref.shape
    heads = width // HD
    height = lax.axis_index("tile") % HEIGHT_TILES
    inside = jnp.where((height > 0) & (height < HEIGHT_TILES - 1), 1.0, 0.0)
    line = lax.broadcasted_iota(jnp.int32, (8, rows), 0)
    shares = jnp.zeros((8, rows), jnp.float32)
    for head in range(heads):
        stats = stats_ref[head]
        their_largest, their_total = message_stats(middle_ref, head, rows)
        valid = stats[2:3] * inside > 0.5
        peak = jnp.maximum(stats[0:1], jnp.where(valid, their_largest, MASKED))
        shrink = jnp.exp2(stats[0:1] - peak)
        share = jnp.where(valid, jnp.exp2(their_largest - peak), 0.0)
        whole = stats[1:2] * shrink + their_total * share
        shares = jnp.where(line == 2 * head, shrink / whole, shares)
        shares = jnp.where(line == 2 * head + 1, share / whole, shares)
    shares = jnp.transpose(shares)
    for head in range(heads):
        low = head * HD
        value = own_ref[:, low : low + HD] * column(shares, 2 * head)
        value += middle_ref[:rows, low : low + HD].astype(jnp.float32) * column(shares, 2 * head + 1)
        out_ref[:, low : low + HD] = value.astype(out_ref.dtype)


def merge(own, stats, middle):
    whole = pl.BlockSpec(memory_space=VMEM)
    return pl.pallas_call(
        merge_kernel,
        out_shape=jax.ShapeDtypeStruct(own.shape, jnp.bfloat16),
        in_specs=[whole] * 3,
        out_specs=whole,
        compiler_params=params(24),
        name="merge",
    )(own, stats, middle)


def project_kernel(mine_ref, theirs_ref, my_weight_ref, their_weight_ref, out_ref, held_ref, sems):
    width = mine_ref.shape[1]
    copies = []
    for group in range(out_ref.shape[0]):
        low = group * width
        held_ref[group] = (
            jnp.dot(mine_ref[...], my_weight_ref[:, low : low + width], preferred_element_type=jnp.float32)
            + jnp.dot(theirs_ref[...], their_weight_ref[:, low : low + width], preferred_element_type=jnp.float32)
        ).astype(held_ref.dtype)
        copies.append(pltpu.make_async_copy(held_ref.at[group], out_ref.at[group], sems.at[group]))
        copies[-1].start()
    for copy in copies:
        copy.wait()


def project(mine, theirs, my_weight, their_weight):
    rows, width = mine.shape
    groups = my_weight.shape[1] // width
    whole = pl.BlockSpec(memory_space=VMEM)
    shape = (groups, rows, width)
    return pl.pallas_call(
        project_kernel,
        out_shape=jax.ShapeDtypeStruct(shape, jnp.bfloat16),
        in_specs=[whole] * 4,
        out_specs=pl.BlockSpec(memory_space=pl.ANY),
        scratch_shapes=[pltpu.VMEM(shape, jnp.bfloat16), pltpu.SemaphoreType.DMA((groups,))],
        compiler_params=params(24),
        cost_estimate=pl.CostEstimate(flops=4 * groups * rows * width * width, bytes_accessed=5_000_000, transcendentals=0),
        name="project",
    )(mine, theirs, my_weight, their_weight)


def finish_kernel(terms_ref, residual_ref, gate_ref, out_ref):
    total = jnp.sum(terms_ref[...].astype(jnp.float32), axis=0)
    out_ref[...] = (residual_ref[...].astype(jnp.float32) + gate_ref[...] * total).astype(out_ref.dtype)


def finish(terms, residual, gate_scale):
    whole = pl.BlockSpec(memory_space=VMEM)
    return pl.pallas_call(
        finish_kernel,
        out_shape=jax.ShapeDtypeStruct(residual.shape, residual.dtype),
        in_specs=[whole] * 3,
        out_specs=whole,
        compiler_params=params(24),
        cost_estimate=pl.CostEstimate(flops=10 * terms.size, bytes_accessed=2_000_000, transcendentals=0),
        name="finish",
    )(terms, residual, gate_scale.reshape(1, -1))


def shards(queries, key_rows, value_rows, windows, residual, out_weight, gate_scale):
    packed, block = pack(windows, queries, key_rows, value_rows)
    first, second = swap_times(block, False), swap_times(block, True)
    pair_asks, middle_asks = swap_pair(packed), swap_middle(packed)
    my_weight, to_send = split_weight(out_weight)
    their_weight = swap_far(to_send)
    mix, stats = attend_own(packed, pair_asks, block)
    for_pair = attend_pair(pair_asks, first, second, mix, stats)
    for_middle = attend_middle(middle_asks, block, first, second, for_pair)
    mix, stats = attend_last(packed, first, second, mix, stats, swap_pair(for_pair))
    attention = merge(mix, stats, swap_middle(for_middle))
    terms = project(attention, swap_far(attention), my_weight, their_weight)
    terms = lax.all_to_all(terms, "group", 0, 0)
    return finish(terms, residual, gate_scale)


def solution(mesh):
    devices = np.asarray(mesh.devices)
    tiles, heads = devices.shape
    split = jax.sharding.Mesh(devices.reshape(tiles, 2, heads // 2), ("tile", "far", "group"))
    head = ("far", "group")
    return jax.shard_map(
        shards,
        mesh=split,
        in_specs=(
            P("tile", head),
            P("tile", head),
            P("tile", head),
            P("tile", None),
            P("tile", head),
            P(head, None),
            P(head),
        ),
        out_specs=P("tile", head),
        check_vma=False,
    )
```

```python
import functools

import jax
import jax.numpy as jnp
import numpy as np
from jax import lax
from jax.experimental import pallas as pl
from jax.experimental.pallas import tpu as pltpu
from jax.sharding import PartitionSpec as P

HD = 128
HEIGHT_TILES = 4
SIDE = 16
LOG2E = 1.4426950408889634
MASKED = -1e30
LAST_FLOPS = 6_000_000_000
MESH_AXES = ("tile", "head")
VMEM = pltpu.VMEM
SMEM = pltpu.SMEM


def params(megabytes):
    return pltpu.CompilerParams(vmem_limit_bytes=megabytes * 1024 * 1024)


def places():
    tiles = lax.axis_size("tile")
    return [(tile, *divmod(tile, HEIGHT_TILES), tiles // HEIGHT_TILES) for tile in range(tiles)]


def swap_times(block, later):
    route = []
    for tile, time, height, times in places():
        partner = time + 1 if time % 2 == int(not later) else time - 1
        if 0 <= partner < times:
            route.append((tile, partner * HEIGHT_TILES + height))
    return lax.ppermute(block, "tile", route)


def swap_pair(block):
    return lax.ppermute(block, "tile", [(tile, tile ^ 1) for tile, *_ in places()])


def swap_middle(block):
    route = [(tile, tile + (1 if height == 1 else -1)) for tile, _, height, _ in places() if height in (1, 2)]
    return lax.ppermute(block, "tile", route)


def swap_far(block):
    return lax.ppermute(block, "far", [(0, 1), (1, 0)])


def split_weight_kernel(weight_ref, mine_ref, theirs_ref):
    width, half = mine_ref.shape[1], theirs_ref.shape[1]
    far = lax.axis_index("far")
    core = lax.rem(lax.axis_index("tile"), 2)
    mine_ref[...] = weight_ref[:, pl.ds(pl.multiple_of(far * width, HD), width)]
    theirs_ref[...] = weight_ref[:, pl.ds(pl.multiple_of((1 - far) * width + core * half, HD), half)]


def split_weight(out_weight):
    rows, features = out_weight.shape
    whole = pl.BlockSpec(memory_space=VMEM)
    return pl.pallas_call(
        split_weight_kernel,
        out_shape=(
            jax.ShapeDtypeStruct((rows, features // 2), out_weight.dtype),
            jax.ShapeDtypeStruct((rows, features // 4), out_weight.dtype),
        ),
        in_specs=[whole],
        out_specs=(whole,) * 2,
        compiler_params=params(24),
        cost_estimate=pl.CostEstimate(flops=0, bytes_accessed=0, transcendentals=0),
        name="split_weight",
    )(out_weight)


def pack_kernel(windows_ref, q_ref, k_ref, v_ref, packed_ref, block_ref):
    rows = q_ref.shape[0]
    block_ref[:rows] = k_ref[...]
    block_ref[rows:] = v_ref[...]
    packed_ref[:rows] = q_ref[...]
    for axis in (0, 1):
        extent = windows_ref[0, axis].astype(jnp.float32)
        packed_ref[rows:, axis * HD : (axis + 1) * HD] = jnp.full((SIDE, HD), extent, jnp.float32).astype(packed_ref.dtype)
    packed_ref[rows:, 2 * HD :] = jnp.zeros((SIDE, q_ref.shape[1] - 2 * HD), packed_ref.dtype)


def pack(windows, queries, key_rows, value_rows):
    rows, width = queries.shape
    whole = pl.BlockSpec(memory_space=VMEM)
    return pl.pallas_call(
        pack_kernel,
        out_shape=(
            jax.ShapeDtypeStruct((rows + SIDE, width), queries.dtype),
            jax.ShapeDtypeStruct((2 * rows, width), queries.dtype),
        ),
        in_specs=[pl.BlockSpec(memory_space=SMEM)] + [whole] * 3,
        out_specs=(whole, whole),
        name="pack",
    )(windows, queries, key_rows, value_rows)


def column(values, index):
    return values[:, index : index + 1]


def split_float(value):
    high = value.astype(jnp.bfloat16).astype(jnp.float32)
    rest = value - high
    middle = rest.astype(jnp.bfloat16).astype(jnp.float32)
    return high, middle, (rest - middle).astype(jnp.bfloat16).astype(jnp.float32)


def wide_window(ref, rows, axis=0):
    return jnp.max(ref[rows:, axis * HD : (axis + 1) * HD].astype(jnp.float32)) > 0.5


def has_first():
    time = lax.axis_index("tile") // HEIGHT_TILES
    return (time > 0) & (time < lax.axis_size("tile") // HEIGHT_TILES - 1)


def block_bias(wide, stage):
    return jnp.where(wide & has_first() if stage == 1 else wide, 0.0, MASKED)


def raw_scores(query, keys):
    return lax.dot_general(query, keys, (((1,), (1,)), ((), ())), preferred_element_type=jnp.float32)


def put_message(ref, head, mix, stats, row):
    rows = mix.shape[0]
    low = head * HD
    line = lax.broadcasted_iota(jnp.int32, (8, rows), 0)
    ref[:rows, low : low + HD] = mix.astype(ref.dtype)
    side = jnp.zeros((8, rows), jnp.float32)
    for index, piece in enumerate(split_float(stats[row : row + 1]) + split_float(stats[row + 1 : row + 2])):
        side = jnp.where(line == index, piece, side)
    ref[rows:, low : low + HD] = jnp.concatenate([side[:, :HD], side[:, HD:]], axis=0).astype(ref.dtype)


def message_stats(ref, head, rows):
    side = ref[rows:, head * HD : (head + 1) * HD].astype(jnp.float32)
    side = jnp.concatenate([side[:8], side[8:]], axis=1)
    return side[0:1] + side[1:2] + side[2:3], side[3:4] + side[4:5] + side[5:6]


def message_columns(ref, head, rows):
    line = lax.broadcasted_iota(jnp.int32, (8, rows), 0)
    largest, total = message_stats(ref, head, rows)
    columns = jnp.transpose(jnp.where(line == 0, largest, jnp.where(line == 1, total, 0.0)))
    return [jnp.broadcast_to(column(columns, index), (rows, HD)) for index in (0, 1)]


def attend(query, blocks, biases, low, old=None):
    rows = blocks[0].shape[0] // 2
    scale = HD**-0.5 * LOG2E
    spread = lambda value: jnp.broadcast_to(value, (rows, HD))
    parts = [raw_scores(query, block[:rows, low : low + HD]) for block in blocks]
    largest = None if old is None else old[0]
    for part, bias in zip(parts, biases):
        peak = spread(jnp.max(part, axis=1, keepdims=True)) * scale + bias
        largest = peak if largest is None else jnp.maximum(largest, peak)
    summed, mix = None, None
    for part, bias, block in zip(parts, biases, blocks):
        offset = jnp.concatenate([bias - largest] * (rows // HD), axis=1)
        weights = jnp.exp2(part * scale + offset)
        product = jnp.dot(weights.astype(block.dtype), block[rows:, low : low + HD], preferred_element_type=jnp.float32)
        summed = weights if summed is None else summed + weights
        mix = product if mix is None else mix + product
    total = spread(jnp.sum(summed, axis=1, keepdims=True))
    if old is not None:
        shrink = jnp.exp2(old[0] - largest)
        total, mix = total + old[1] * shrink, mix + old[2] * shrink
    return largest, total, mix


def row_stats(largest, total):
    lane = lax.broadcasted_iota(jnp.int32, largest.shape, 1)
    return jnp.transpose(jnp.where(lane == 0, largest, jnp.where(lane == 1, total, 0.0)))[:8]


def block_biases(query_ref, rows):
    wide = wide_window(query_ref, rows)
    return [block_bias(wide, stage) for stage in (1, 2)]


def own_kernel(query_ref, pair_ref, block_ref, mix_ref, stats_ref):
    rows, width = block_ref.shape[0] // 2, block_ref.shape[1]
    for place, ref in enumerate((query_ref, pair_ref)):
        for head in range(width // HD):
            low, index = head * HD, 2 * head + place
            largest, total, mix = attend(ref[:rows, low : low + HD], [block_ref], [0.0], low)
            mix_ref[index], stats_ref[2 * index], stats_ref[2 * index + 1] = mix, largest, total


def attend_own(queries, pair, block):
    rows, width = block.shape[0] // 2, block.shape[1]
    heads = width // HD
    whole = pl.BlockSpec(memory_space=VMEM)
    return pl.pallas_call(
        own_kernel,
        out_shape=(
            jax.ShapeDtypeStruct((2 * heads, rows, HD), jnp.float32),
            jax.ShapeDtypeStruct((4 * heads, rows, HD), jnp.float32),
        ),
        in_specs=[whole] * 3,
        out_specs=(whole,) * 2,
        compiler_params=params(24),
        cost_estimate=pl.CostEstimate(flops=0, bytes_accessed=0, transcendentals=0),
        name="attend_own",
    )(queries, pair, block)


def old_parts(mix_ref, stats_ref, head, place):
    index = 2 * head + place
    return stats_ref[2 * index], stats_ref[2 * index + 1], mix_ref[index]


def pair_kernel(query_ref, first_ref, second_ref, mix_ref, stats_ref, out_ref):
    rows, width = first_ref.shape[0] // 2, first_ref.shape[1]
    biases = block_biases(query_ref, rows)
    for head in range(width // HD):
        low = head * HD
        old = old_parts(mix_ref, stats_ref, head, 1)
        largest, total, mix = attend(query_ref[:rows, low : low + HD], [first_ref, second_ref], biases, low, old)
        put_message(out_ref, head, mix, row_stats(largest, total), 0)


def attend_pair(query, first, second, mix, stats):
    whole = pl.BlockSpec(memory_space=VMEM)
    return pl.pallas_call(
        pair_kernel,
        out_shape=jax.ShapeDtypeStruct(query.shape, jnp.bfloat16),
        in_specs=[whole] * 5,
        out_specs=whole,
        compiler_params=params(24),
        cost_estimate=pl.CostEstimate(flops=400_000_000, bytes_accessed=2_000_000, transcendentals=0),
        name="attend_pair",
    )(query, first, second, mix, stats)


def middle_kernel(query_ref, own_ref, first_ref, second_ref, after_ref, out_ref):
    rows, width = own_ref.shape[0] // 2, own_ref.shape[1]
    height = lax.axis_index("tile") % HEIGHT_TILES
    inside = (height > 0) & (height < HEIGHT_TILES - 1)

    @pl.when(inside)
    def compute():
        biases = [0.0] + block_biases(query_ref, rows)
        blocks = [own_ref, first_ref, second_ref]
        for head in range(width // HD):
            low = head * HD
            largest, total, mix = attend(query_ref[:rows, low : low + HD], blocks, biases, low)
            put_message(out_ref, head, mix, row_stats(largest, total), 0)

    @pl.when(jnp.logical_not(inside))
    def skip():
        out_ref[...] = jnp.zeros_like(out_ref)


def attend_middle(query, own, first, second, after):
    whole = pl.BlockSpec(memory_space=VMEM)
    return pl.pallas_call(
        middle_kernel,
        out_shape=jax.ShapeDtypeStruct(query.shape, jnp.bfloat16),
        in_specs=[whole] * 4 + [pl.BlockSpec(memory_space=pl.ANY)],
        out_specs=whole,
        compiler_params=params(24),
        cost_estimate=pl.CostEstimate(flops=600_000_000, bytes_accessed=2_000_000, transcendentals=0),
        name="attend_middle",
    )(query, own, first, second, after)


def last_kernel(query_ref, first_ref, second_ref, old_mix_ref, old_stats_ref, message_ref, mix_ref, stats_ref):
    rows, width = first_ref.shape[0] // 2, first_ref.shape[1]
    wide = wide_window(query_ref, rows, 1)
    biases = block_biases(query_ref, rows)
    for head in range(width // HD):
        low = head * HD
        old = old_parts(old_mix_ref, old_stats_ref, head, 0)
        largest, total, mix = attend(query_ref[:rows, low : low + HD], [first_ref, second_ref], biases, low, old)
        their_largest, their_total = message_columns(message_ref, head, rows)
        peak = jnp.maximum(largest, jnp.where(wide, their_largest, MASKED))
        shrink, share = jnp.exp2(largest - peak), jnp.where(wide, jnp.exp2(their_largest - peak), 0.0)
        stats = row_stats(peak, total * shrink + their_total * share)
        mix_ref[:, low : low + HD] = mix * shrink + message_ref[:rows, low : low + HD].astype(jnp.float32) * share
        line = lax.broadcasted_iota(jnp.int32, stats.shape, 0)
        stats_ref[head] = jnp.where(line == 2, jnp.where(wide, 1.0, 0.0), stats)


def attend_last(queries, first, second, mix, stats, message):
    rows, width = first.shape[0] // 2, first.shape[1]
    whole = pl.BlockSpec(memory_space=VMEM)
    return pl.pallas_call(
        last_kernel,
        out_shape=(
            jax.ShapeDtypeStruct((rows, width), jnp.float32),
            jax.ShapeDtypeStruct((width // HD, 8, rows), jnp.float32),
        ),
        in_specs=[whole] * 6,
        out_specs=(whole, whole),
        compiler_params=params(24),
        cost_estimate=pl.CostEstimate(flops=LAST_FLOPS, bytes_accessed=2_000_000, transcendentals=0),
        name="attend_last",
    )(queries, first, second, mix, stats, message)


def merge_kernel(own_ref, stats_ref, middle_ref, out_ref):
    rows, width = own_ref.shape
    heads = width // HD
    height = lax.axis_index("tile") % HEIGHT_TILES
    inside = jnp.where((height > 0) & (height < HEIGHT_TILES - 1), 1.0, 0.0)
    line = lax.broadcasted_iota(jnp.int32, (8, rows), 0)
    shares = jnp.zeros((8, rows), jnp.float32)
    for head in range(heads):
        stats = stats_ref[head]
        their_largest, their_total = message_stats(middle_ref, head, rows)
        valid = stats[2:3] * inside > 0.5
        peak = jnp.maximum(stats[0:1], jnp.where(valid, their_largest, MASKED))
        shrink = jnp.exp2(stats[0:1] - peak)
        share = jnp.where(valid, jnp.exp2(their_largest - peak), 0.0)
        whole = stats[1:2] * shrink + their_total * share
        shares = jnp.where(line == 2 * head, shrink / whole, shares)
        shares = jnp.where(line == 2 * head + 1, share / whole, shares)
    shares = jnp.transpose(shares)
    for head in range(heads):
        low = head * HD
        value = own_ref[:, low : low + HD] * column(shares, 2 * head)
        value += middle_ref[:rows, low : low + HD].astype(jnp.float32) * column(shares, 2 * head + 1)
        out_ref[:, low : low + HD] = value.astype(out_ref.dtype)


def merge(own, stats, middle):
    whole = pl.BlockSpec(memory_space=VMEM)
    return pl.pallas_call(
        merge_kernel,
        out_shape=jax.ShapeDtypeStruct(own.shape, jnp.bfloat16),
        in_specs=[whole] * 3,
        out_specs=whole,
        compiler_params=params(24),
        name="merge",
    )(own, stats, middle)


def project_kernel(mine_ref, theirs_ref, my_weight_ref, this_ref, other_ref, out_ref, held_ref, sems):
    width, half = mine_ref.shape[1], this_ref.shape[1]
    core = lax.rem(lax.axis_index("tile"), 2)
    copies = []
    for group in range(out_ref.shape[0]):
        low = group * width
        side, start = divmod(low, half)
        their_weight = jnp.where(side == core, this_ref[:, start : start + width], other_ref[:, start : start + width])
        held_ref[group] = (
            jnp.dot(mine_ref[...], my_weight_ref[:, low : low + width], preferred_element_type=jnp.float32)
            + jnp.dot(theirs_ref[...], their_weight, preferred_element_type=jnp.float32)
        ).astype(held_ref.dtype)
        copies.append(pltpu.make_async_copy(held_ref.at[group], out_ref.at[group], sems.at[group]))
        copies[-1].start()
    for copy in copies:
        copy.wait()


def project(mine, theirs, my_weight, this_half, other_half):
    rows, width = mine.shape
    groups = my_weight.shape[1] // width
    whole = pl.BlockSpec(memory_space=VMEM)
    shape = (groups, rows, width)
    return pl.pallas_call(
        project_kernel,
        out_shape=jax.ShapeDtypeStruct(shape, jnp.bfloat16),
        in_specs=[whole] * 5,
        out_specs=pl.BlockSpec(memory_space=pl.ANY),
        scratch_shapes=[pltpu.VMEM(shape, jnp.bfloat16), pltpu.SemaphoreType.DMA((groups,))],
        compiler_params=params(24),
        cost_estimate=pl.CostEstimate(flops=4 * groups * rows * width * width, bytes_accessed=5_000_000, transcendentals=0),
        name="project",
    )(mine, theirs, my_weight, this_half, other_half)


def finish_kernel(terms_ref, residual_ref, gate_ref, out_ref):
    total = jnp.sum(terms_ref[...].astype(jnp.float32), axis=0)
    out_ref[...] = (residual_ref[...].astype(jnp.float32) + gate_ref[...] * total).astype(out_ref.dtype)


def finish(terms, residual, gate_scale):
    whole = pl.BlockSpec(memory_space=VMEM)
    return pl.pallas_call(
        finish_kernel,
        out_shape=jax.ShapeDtypeStruct(residual.shape, residual.dtype),
        in_specs=[whole] * 3,
        out_specs=whole,
        compiler_params=params(24),
        cost_estimate=pl.CostEstimate(flops=10 * terms.size, bytes_accessed=2_000_000, transcendentals=0),
        name="finish",
    )(terms, residual, gate_scale.reshape(1, -1))


def shards(queries, key_rows, value_rows, windows, residual, out_weight, gate_scale):
    packed, block = pack(windows, queries, key_rows, value_rows)
    first, second = swap_times(block, False), swap_times(block, True)
    pair_asks, middle_asks = swap_pair(packed), swap_middle(packed)
    my_weight, to_send = split_weight(out_weight)
    this_half = swap_far(to_send)
    mix, stats = attend_own(packed, pair_asks, block)
    for_pair = attend_pair(pair_asks, first, second, mix, stats)
    for_middle = attend_middle(middle_asks, block, first, second, for_pair)
    mix, stats = attend_last(packed, first, second, mix, stats, swap_pair(for_pair))
    attention = merge(mix, stats, swap_middle(for_middle))
    terms = project(attention, swap_far(attention), my_weight, this_half, swap_pair(this_half))
    terms = lax.all_to_all(terms, "group", 0, 0)
    return finish(terms, residual, gate_scale)


def solution(mesh):
    devices = np.asarray(mesh.devices)
    tiles, heads = devices.shape
    split = jax.sharding.Mesh(devices.reshape(tiles, 2, heads // 2), ("tile", "far", "group"))
    head = ("far", "group")
    return jax.shard_map(
        shards,
        mesh=split,
        in_specs=(
            P("tile", head),
            P("tile", head),
            P("tile", head),
            P("tile", None),
            P("tile", head),
            P(head, None),
            P(head),
        ),
        out_specs=P("tile", head),
        check_vma=False,
    )
```

```python
import functools

import jax
import jax.numpy as jnp
import numpy as np
from jax import lax
from jax.experimental import pallas as pl
from jax.experimental.pallas import tpu as pltpu
from jax.sharding import PartitionSpec as P

HD = 128
HEIGHT_TILES = 4
SIDE = 16
LOG2E = 1.4426950408889634
MASKED = -1e30
LAST_FLOPS = 400_000_000
MIDDLE_FLOPS = 6000_000_000
MESH_AXES = ("tile", "head")
VMEM = pltpu.VMEM
SMEM = pltpu.SMEM


def params(megabytes):
    return pltpu.CompilerParams(vmem_limit_bytes=megabytes * 1024 * 1024)


def places():
    tiles = lax.axis_size("tile")
    return [(tile, *divmod(tile, HEIGHT_TILES), tiles // HEIGHT_TILES) for tile in range(tiles)]


def swap_times(block, later):
    route = []
    for tile, time, height, times in places():
        partner = time + 1 if time % 2 == int(not later) else time - 1
        if 0 <= partner < times:
            route.append((tile, partner * HEIGHT_TILES + height))
    return lax.ppermute(block, "tile", route)


def swap_pair(block):
    return lax.ppermute(block, "tile", [(tile, tile ^ 1) for tile, *_ in places()])


def swap_middle(block):
    route = [(tile, tile + (1 if height == 1 else -1)) for tile, _, height, _ in places() if height in (1, 2)]
    return lax.ppermute(block, "tile", route)


def swap_far(block):
    return lax.ppermute(block, "far", [(0, 1), (1, 0)])


def split_weight_kernel(weight_ref, mine_ref, theirs_ref):
    width, half = mine_ref.shape[1], theirs_ref.shape[1]
    far = lax.axis_index("far")
    core = lax.rem(lax.axis_index("tile"), 2)
    mine_ref[...] = weight_ref[:, pl.ds(pl.multiple_of(far * width, HD), width)]
    theirs_ref[...] = weight_ref[:, pl.ds(pl.multiple_of((1 - far) * width + core * half, HD), half)]


def split_weight(out_weight):
    rows, features = out_weight.shape
    whole = pl.BlockSpec(memory_space=VMEM)
    return pl.pallas_call(
        split_weight_kernel,
        out_shape=(
            jax.ShapeDtypeStruct((rows, features // 2), out_weight.dtype),
            jax.ShapeDtypeStruct((rows, features // 4), out_weight.dtype),
        ),
        in_specs=[whole],
        out_specs=(whole,) * 2,
        compiler_params=params(24),
        cost_estimate=pl.CostEstimate(flops=0, bytes_accessed=0, transcendentals=0),
        name="split_weight",
    )(out_weight)


def pack_kernel(windows_ref, q_ref, k_ref, v_ref, packed_ref, block_ref):
    rows = q_ref.shape[0]
    block_ref[:rows] = k_ref[...]
    block_ref[rows:] = v_ref[...]
    packed_ref[:rows] = q_ref[...]
    for axis in (0, 1):
        extent = windows_ref[0, axis].astype(jnp.float32)
        packed_ref[rows:, axis * HD : (axis + 1) * HD] = jnp.full((SIDE, HD), extent, jnp.float32).astype(packed_ref.dtype)
    packed_ref[rows:, 2 * HD :] = jnp.zeros((SIDE, q_ref.shape[1] - 2 * HD), packed_ref.dtype)


def pack(windows, queries, key_rows, value_rows):
    rows, width = queries.shape
    whole = pl.BlockSpec(memory_space=VMEM)
    return pl.pallas_call(
        pack_kernel,
        out_shape=(
            jax.ShapeDtypeStruct((rows + SIDE, width), queries.dtype),
            jax.ShapeDtypeStruct((2 * rows, width), queries.dtype),
        ),
        in_specs=[pl.BlockSpec(memory_space=SMEM)] + [whole] * 3,
        out_specs=(whole, whole),
        name="pack",
    )(windows, queries, key_rows, value_rows)


def column(values, index):
    return values[:, index : index + 1]


def split_float(value):
    high = value.astype(jnp.bfloat16).astype(jnp.float32)
    rest = value - high
    middle = rest.astype(jnp.bfloat16).astype(jnp.float32)
    return high, middle, (rest - middle).astype(jnp.bfloat16).astype(jnp.float32)


def wide_window(ref, rows, axis=0):
    return jnp.max(ref[rows:, axis * HD : (axis + 1) * HD].astype(jnp.float32)) > 0.5


def has_first():
    time = lax.axis_index("tile") // HEIGHT_TILES
    return (time > 0) & (time < lax.axis_size("tile") // HEIGHT_TILES - 1)


def block_bias(wide, stage):
    return jnp.where(wide & has_first() if stage == 1 else wide, 0.0, MASKED)


def raw_scores(query, keys):
    return lax.dot_general(query, keys, (((1,), (1,)), ((), ())), preferred_element_type=jnp.float32)


def put_message(ref, head, mix, stats, row):
    rows = mix.shape[0]
    low = head * HD
    line = lax.broadcasted_iota(jnp.int32, (8, rows), 0)
    ref[:rows, low : low + HD] = mix.astype(ref.dtype)
    side = jnp.zeros((8, rows), jnp.float32)
    for index, piece in enumerate(split_float(stats[row : row + 1]) + split_float(stats[row + 1 : row + 2])):
        side = jnp.where(line == index, piece, side)
    ref[rows:, low : low + HD] = jnp.concatenate([side[:, :HD], side[:, HD:]], axis=0).astype(ref.dtype)


def message_stats(ref, head, rows):
    side = ref[rows:, head * HD : (head + 1) * HD].astype(jnp.float32)
    side = jnp.concatenate([side[:8], side[8:]], axis=1)
    return side[0:1] + side[1:2] + side[2:3], side[3:4] + side[4:5] + side[5:6]


def message_columns(ref, head, rows):
    line = lax.broadcasted_iota(jnp.int32, (8, rows), 0)
    largest, total = message_stats(ref, head, rows)
    columns = jnp.transpose(jnp.where(line == 0, largest, jnp.where(line == 1, total, 0.0)))
    return [jnp.broadcast_to(column(columns, index), (rows, HD)) for index in (0, 1)]


def attend(query, blocks, biases, low, old=None):
    rows = blocks[0].shape[0] // 2
    scale = HD**-0.5 * LOG2E
    spread = lambda value: jnp.broadcast_to(value, (rows, HD))
    parts = [raw_scores(query, block[:rows, low : low + HD]) for block in blocks]
    largest = None if old is None else old[0]
    for part, bias in zip(parts, biases):
        peak = spread(jnp.max(part, axis=1, keepdims=True)) * scale + bias
        largest = peak if largest is None else jnp.maximum(largest, peak)
    summed, mix = None, None
    for part, bias, block in zip(parts, biases, blocks):
        offset = jnp.concatenate([bias - largest] * (rows // HD), axis=1)
        weights = jnp.exp2(part * scale + offset)
        product = jnp.dot(weights.astype(block.dtype), block[rows:, low : low + HD], preferred_element_type=jnp.float32)
        summed = weights if summed is None else summed + weights
        mix = product if mix is None else mix + product
    total = spread(jnp.sum(summed, axis=1, keepdims=True))
    if old is not None:
        shrink = jnp.exp2(old[0] - largest)
        total, mix = total + old[1] * shrink, mix + old[2] * shrink
    return largest, total, mix


def row_stats(largest, total):
    lane = lax.broadcasted_iota(jnp.int32, largest.shape, 1)
    return jnp.transpose(jnp.where(lane == 0, largest, jnp.where(lane == 1, total, 0.0)))[:8]


def block_biases(query_ref, rows):
    wide = wide_window(query_ref, rows)
    return [block_bias(wide, stage) for stage in (1, 2)]


def own_kernel(query_ref, pair_ref, block_ref, mix_ref, stats_ref):
    rows, width = block_ref.shape[0] // 2, block_ref.shape[1]
    for place, ref in enumerate((query_ref, pair_ref)):
        for head in range(width // HD):
            low, index = head * HD, 2 * head + place
            largest, total, mix = attend(ref[:rows, low : low + HD], [block_ref], [0.0], low)
            mix_ref[index], stats_ref[2 * index], stats_ref[2 * index + 1] = mix, largest, total


def attend_own(queries, pair, block):
    rows, width = block.shape[0] // 2, block.shape[1]
    heads = width // HD
    whole = pl.BlockSpec(memory_space=VMEM)
    return pl.pallas_call(
        own_kernel,
        out_shape=(
            jax.ShapeDtypeStruct((2 * heads, rows, HD), jnp.float32),
            jax.ShapeDtypeStruct((4 * heads, rows, HD), jnp.float32),
        ),
        in_specs=[whole] * 3,
        out_specs=(whole,) * 2,
        compiler_params=params(24),
        cost_estimate=pl.CostEstimate(flops=0, bytes_accessed=0, transcendentals=0),
        name="attend_own",
    )(queries, pair, block)


def old_parts(mix_ref, stats_ref, head, place):
    index = 2 * head + place
    return stats_ref[2 * index], stats_ref[2 * index + 1], mix_ref[index]


def pair_kernel(query_ref, first_ref, second_ref, mix_ref, stats_ref, out_ref):
    rows, width = first_ref.shape[0] // 2, first_ref.shape[1]
    biases = block_biases(query_ref, rows)
    for head in range(width // HD):
        low = head * HD
        old = old_parts(mix_ref, stats_ref, head, 1)
        largest, total, mix = attend(query_ref[:rows, low : low + HD], [first_ref, second_ref], biases, low, old)
        put_message(out_ref, head, mix, row_stats(largest, total), 0)


def attend_pair(query, first, second, mix, stats):
    whole = pl.BlockSpec(memory_space=VMEM)
    return pl.pallas_call(
        pair_kernel,
        out_shape=jax.ShapeDtypeStruct(query.shape, jnp.bfloat16),
        in_specs=[whole] * 5,
        out_specs=whole,
        compiler_params=params(24),
        cost_estimate=pl.CostEstimate(flops=4_000_000_000, bytes_accessed=2_000_000, transcendentals=0),
        name="attend_pair",
    )(query, first, second, mix, stats)


def middle_kernel(query_ref, own_ref, first_ref, second_ref, after_ref, out_ref):
    rows, width = own_ref.shape[0] // 2, own_ref.shape[1]
    height = lax.axis_index("tile") % HEIGHT_TILES
    inside = (height > 0) & (height < HEIGHT_TILES - 1)

    @pl.when(inside)
    def compute():
        biases = [0.0] + block_biases(query_ref, rows)
        blocks = [own_ref, first_ref, second_ref]
        for head in range(width // HD):
            low = head * HD
            largest, total, mix = attend(query_ref[:rows, low : low + HD], blocks, biases, low)
            put_message(out_ref, head, mix, row_stats(largest, total), 0)

    @pl.when(jnp.logical_not(inside))
    def skip():
        out_ref[...] = jnp.zeros_like(out_ref)


def attend_middle(query, own, first, second, after):
    whole = pl.BlockSpec(memory_space=VMEM)
    return pl.pallas_call(
        middle_kernel,
        out_shape=jax.ShapeDtypeStruct(query.shape, jnp.bfloat16),
        in_specs=[whole] * 4 + [pl.BlockSpec(memory_space=pl.ANY)],
        out_specs=whole,
        compiler_params=params(24),
        cost_estimate=pl.CostEstimate(flops=MIDDLE_FLOPS, bytes_accessed=2_000_000, transcendentals=0),
        name="attend_middle",
    )(query, own, first, second, after)


def last_kernel(query_ref, first_ref, second_ref, old_mix_ref, old_stats_ref, message_ref, after_ref, mix_ref, stats_ref):
    rows, width = first_ref.shape[0] // 2, first_ref.shape[1]
    wide = wide_window(query_ref, rows, 1)
    biases = block_biases(query_ref, rows)
    for head in range(width // HD):
        low = head * HD
        old = old_parts(old_mix_ref, old_stats_ref, head, 0)
        largest, total, mix = attend(query_ref[:rows, low : low + HD], [first_ref, second_ref], biases, low, old)
        their_largest, their_total = message_columns(message_ref, head, rows)
        peak = jnp.maximum(largest, jnp.where(wide, their_largest, MASKED))
        shrink, share = jnp.exp2(largest - peak), jnp.where(wide, jnp.exp2(their_largest - peak), 0.0)
        stats = row_stats(peak, total * shrink + their_total * share)
        mix_ref[:, low : low + HD] = mix * shrink + message_ref[:rows, low : low + HD].astype(jnp.float32) * share
        line = lax.broadcasted_iota(jnp.int32, stats.shape, 0)
        stats_ref[head] = jnp.where(line == 2, jnp.where(wide, 1.0, 0.0), stats)


def attend_last(queries, first, second, mix, stats, message, after):
    rows, width = first.shape[0] // 2, first.shape[1]
    whole = pl.BlockSpec(memory_space=VMEM)
    return pl.pallas_call(
        last_kernel,
        out_shape=(
            jax.ShapeDtypeStruct((rows, width), jnp.float32),
            jax.ShapeDtypeStruct((width // HD, 8, rows), jnp.float32),
        ),
        in_specs=[whole] * 6 + [pl.BlockSpec(memory_space=pl.ANY)],
        out_specs=(whole, whole),
        compiler_params=params(24),
        cost_estimate=pl.CostEstimate(flops=LAST_FLOPS, bytes_accessed=2_000_000, transcendentals=0),
        name="attend_last",
    )(queries, first, second, mix, stats, message, after)


def merge_kernel(own_ref, stats_ref, middle_ref, out_ref):
    rows, width = own_ref.shape
    heads = width // HD
    height = lax.axis_index("tile") % HEIGHT_TILES
    inside = jnp.where((height > 0) & (height < HEIGHT_TILES - 1), 1.0, 0.0)
    line = lax.broadcasted_iota(jnp.int32, (8, rows), 0)
    shares = jnp.zeros((8, rows), jnp.float32)
    for head in range(heads):
        stats = stats_ref[head]
        their_largest, their_total = message_stats(middle_ref, head, rows)
        valid = stats[2:3] * inside > 0.5
        peak = jnp.maximum(stats[0:1], jnp.where(valid, their_largest, MASKED))
        shrink = jnp.exp2(stats[0:1] - peak)
        share = jnp.where(valid, jnp.exp2(their_largest - peak), 0.0)
        whole = stats[1:2] * shrink + their_total * share
        shares = jnp.where(line == 2 * head, shrink / whole, shares)
        shares = jnp.where(line == 2 * head + 1, share / whole, shares)
    shares = jnp.transpose(shares)
    for head in range(heads):
        low = head * HD
        value = own_ref[:, low : low + HD] * column(shares, 2 * head)
        value += middle_ref[:rows, low : low + HD].astype(jnp.float32) * column(shares, 2 * head + 1)
        out_ref[:, low : low + HD] = value.astype(out_ref.dtype)


def merge(own, stats, middle):
    whole = pl.BlockSpec(memory_space=VMEM)
    return pl.pallas_call(
        merge_kernel,
        out_shape=jax.ShapeDtypeStruct(own.shape, jnp.bfloat16),
        in_specs=[whole] * 3,
        out_specs=whole,
        compiler_params=params(24),
        name="merge",
    )(own, stats, middle)


def project_kernel(mine_ref, theirs_ref, my_weight_ref, this_ref, other_ref, out_ref, held_ref, sems):
    width, half = mine_ref.shape[1], this_ref.shape[1]
    core = lax.rem(lax.axis_index("tile"), 2)
    copies = []
    for group in range(out_ref.shape[0]):
        low = group * width
        side, start = divmod(low, half)
        their_weight = jnp.where(side == core, this_ref[:, start : start + width], other_ref[:, start : start + width])
        held_ref[group] = (
            jnp.dot(mine_ref[...], my_weight_ref[:, low : low + width], preferred_element_type=jnp.float32)
            + jnp.dot(theirs_ref[...], their_weight, preferred_element_type=jnp.float32)
        ).astype(held_ref.dtype)
        copies.append(pltpu.make_async_copy(held_ref.at[group], out_ref.at[group], sems.at[group]))
        copies[-1].start()
    for copy in copies:
        copy.wait()


def project(mine, theirs, my_weight, this_half, other_half):
    rows, width = mine.shape
    groups = my_weight.shape[1] // width
    whole = pl.BlockSpec(memory_space=VMEM)
    shape = (groups, rows, width)
    return pl.pallas_call(
        project_kernel,
        out_shape=jax.ShapeDtypeStruct(shape, jnp.bfloat16),
        in_specs=[whole] * 5,
        out_specs=pl.BlockSpec(memory_space=pl.ANY),
        scratch_shapes=[pltpu.VMEM(shape, jnp.bfloat16), pltpu.SemaphoreType.DMA((groups,))],
        compiler_params=params(24),
        cost_estimate=pl.CostEstimate(flops=4 * groups * rows * width * width, bytes_accessed=5_000_000, transcendentals=0),
        name="project",
    )(mine, theirs, my_weight, this_half, other_half)


def finish_kernel(terms_ref, residual_ref, gate_ref, out_ref):
    total = jnp.sum(terms_ref[...].astype(jnp.float32), axis=0)
    out_ref[...] = (residual_ref[...].astype(jnp.float32) + gate_ref[...] * total).astype(out_ref.dtype)


def finish(terms, residual, gate_scale):
    whole = pl.BlockSpec(memory_space=VMEM)
    return pl.pallas_call(
        finish_kernel,
        out_shape=jax.ShapeDtypeStruct(residual.shape, residual.dtype),
        in_specs=[whole] * 3,
        out_specs=whole,
        compiler_params=params(24),
        cost_estimate=pl.CostEstimate(flops=10 * terms.size, bytes_accessed=2_000_000, transcendentals=0),
        name="finish",
    )(terms, residual, gate_scale.reshape(1, -1))


def shards(queries, key_rows, value_rows, windows, residual, out_weight, gate_scale):
    packed, block = pack(windows, queries, key_rows, value_rows)
    first, second = swap_times(block, False), swap_times(block, True)
    pair_asks, middle_asks = swap_pair(packed), swap_middle(packed)
    my_weight, to_send = split_weight(out_weight)
    this_half = swap_far(to_send)
    mix, stats = attend_own(packed, pair_asks, block)
    for_pair = attend_pair(pair_asks, first, second, mix, stats)
    for_middle = attend_middle(middle_asks, block, first, second, for_pair)
    other_half = swap_pair(this_half)
    mix, stats = attend_last(packed, first, second, mix, stats, swap_pair(for_pair), other_half)
    attention = merge(mix, stats, swap_middle(for_middle))
    terms = project(attention, swap_far(attention), my_weight, this_half, other_half)
    terms = lax.all_to_all(terms, "group", 0, 0)
    return finish(terms, residual, gate_scale)


def solution(mesh):
    devices = np.asarray(mesh.devices)
    tiles, heads = devices.shape
    split = jax.sharding.Mesh(devices.reshape(tiles, 2, heads // 2), ("tile", "far", "group"))
    head = ("far", "group")
    return jax.shard_map(
        shards,
        mesh=split,
        in_specs=(
            P("tile", head),
            P("tile", head),
            P("tile", head),
            P("tile", None),
            P("tile", head),
            P(head, None),
            P(head),
        ),
        out_specs=P("tile", head),
        check_vma=False,
    )
```

```python
import functools

import jax
import jax.numpy as jnp
import numpy as np
from jax import lax
from jax.experimental import pallas as pl
from jax.experimental.pallas import tpu as pltpu
from jax.sharding import PartitionSpec as P

HD = 128
HEIGHT_TILES = 4
SIDE = 16
LOG2E = 1.4426950408889634
MASKED = -1e30
LAST_FLOPS = 400_000_000
MIDDLE_FLOPS = 6000_000_000
MESH_AXES = ("tile", "head")
VMEM = pltpu.VMEM
SMEM = pltpu.SMEM


def params(megabytes):
    return pltpu.CompilerParams(vmem_limit_bytes=megabytes * 1024 * 1024)


def places():
    tiles = lax.axis_size("tile")
    return [(tile, *divmod(tile, HEIGHT_TILES), tiles // HEIGHT_TILES) for tile in range(tiles)]


def swap_times(block, later):
    route = []
    for tile, time, height, times in places():
        partner = time + 1 if time % 2 == int(not later) else time - 1
        if 0 <= partner < times:
            route.append((tile, partner * HEIGHT_TILES + height))
    return lax.ppermute(block, "tile", route)


def swap_pair(block):
    return lax.ppermute(block, "tile", [(tile, tile ^ 1) for tile, *_ in places()])


def swap_middle(block):
    route = [(tile, tile + (1 if height == 1 else -1)) for tile, _, height, _ in places() if height in (1, 2)]
    return lax.ppermute(block, "tile", route)


def swap_far(block):
    return lax.ppermute(block, "far", [(0, 1), (1, 0)])


def split_weight_kernel(weight_ref, mine_ref, theirs_ref):
    width, half = mine_ref.shape[1], theirs_ref.shape[1]
    far = lax.axis_index("far")
    core = lax.rem(lax.axis_index("tile"), 2)
    mine_ref[...] = weight_ref[:, pl.ds(pl.multiple_of(far * width, HD), width)]
    theirs_ref[...] = weight_ref[:, pl.ds(pl.multiple_of((1 - far) * width + core * half, HD), half)]


def split_weight(out_weight):
    rows, features = out_weight.shape
    whole = pl.BlockSpec(memory_space=VMEM)
    return pl.pallas_call(
        split_weight_kernel,
        out_shape=(
            jax.ShapeDtypeStruct((rows, features // 2), out_weight.dtype),
            jax.ShapeDtypeStruct((rows, features // 4), out_weight.dtype),
        ),
        in_specs=[whole],
        out_specs=(whole,) * 2,
        compiler_params=params(24),
        cost_estimate=pl.CostEstimate(flops=0, bytes_accessed=0, transcendentals=0),
        name="split_weight",
    )(out_weight)


def pack_kernel(windows_ref, q_ref, k_ref, v_ref, packed_ref, block_ref):
    rows = q_ref.shape[0]
    block_ref[:rows] = k_ref[...]
    block_ref[rows:] = v_ref[...]
    packed_ref[:rows] = q_ref[...]
    for axis in (0, 1):
        extent = windows_ref[0, axis].astype(jnp.float32)
        packed_ref[rows:, axis * HD : (axis + 1) * HD] = jnp.full((SIDE, HD), extent, jnp.float32).astype(packed_ref.dtype)
    packed_ref[rows:, 2 * HD :] = jnp.zeros((SIDE, q_ref.shape[1] - 2 * HD), packed_ref.dtype)


def pack(windows, queries, key_rows, value_rows):
    rows, width = queries.shape
    whole = pl.BlockSpec(memory_space=VMEM)
    return pl.pallas_call(
        pack_kernel,
        out_shape=(
            jax.ShapeDtypeStruct((rows + SIDE, width), queries.dtype),
            jax.ShapeDtypeStruct((2 * rows, width), queries.dtype),
        ),
        in_specs=[pl.BlockSpec(memory_space=SMEM)] + [whole] * 3,
        out_specs=(whole, whole),
        name="pack",
    )(windows, queries, key_rows, value_rows)


def column(values, index):
    return values[:, index : index + 1]


def split_float(value):
    high = value.astype(jnp.bfloat16).astype(jnp.float32)
    rest = value - high
    middle = rest.astype(jnp.bfloat16).astype(jnp.float32)
    return high, middle, (rest - middle).astype(jnp.bfloat16).astype(jnp.float32)


def wide_window(ref, rows, axis=0):
    return jnp.max(ref[rows:, axis * HD : (axis + 1) * HD].astype(jnp.float32)) > 0.5


def has_first():
    time = lax.axis_index("tile") // HEIGHT_TILES
    return (time > 0) & (time < lax.axis_size("tile") // HEIGHT_TILES - 1)


def block_bias(wide, stage):
    return jnp.where(wide & has_first() if stage == 1 else wide, 0.0, MASKED)


def raw_scores(query, keys):
    return lax.dot_general(query, keys, (((1,), (1,)), ((), ())), preferred_element_type=jnp.float32)


def put_message(ref, head, mix, stats, row):
    rows = mix.shape[0]
    low = head * HD
    line = lax.broadcasted_iota(jnp.int32, (8, rows), 0)
    ref[:rows, low : low + HD] = mix.astype(ref.dtype)
    side = jnp.zeros((8, rows), jnp.float32)
    for index, piece in enumerate(split_float(stats[row : row + 1]) + split_float(stats[row + 1 : row + 2])):
        side = jnp.where(line == index, piece, side)
    ref[rows:, low : low + HD] = jnp.concatenate([side[:, :HD], side[:, HD:]], axis=0).astype(ref.dtype)


def message_stats(ref, head, rows):
    side = ref[rows:, head * HD : (head + 1) * HD].astype(jnp.float32)
    side = jnp.concatenate([side[:8], side[8:]], axis=1)
    return side[0:1] + side[1:2] + side[2:3], side[3:4] + side[4:5] + side[5:6]


def message_columns(ref, head, rows):
    line = lax.broadcasted_iota(jnp.int32, (8, rows), 0)
    largest, total = message_stats(ref, head, rows)
    columns = jnp.transpose(jnp.where(line == 0, largest, jnp.where(line == 1, total, 0.0)))
    return [jnp.broadcast_to(column(columns, index), (rows, HD)) for index in (0, 1)]


def attend(query, blocks, biases, low, old=None):
    rows = blocks[0].shape[0] // 2
    scale = HD**-0.5 * LOG2E
    spread = lambda value: jnp.broadcast_to(value, (rows, HD))
    parts = [raw_scores(query, block[:rows, low : low + HD]) for block in blocks]
    largest = None if old is None else old[0]
    for part, bias in zip(parts, biases):
        peak = spread(jnp.max(part, axis=1, keepdims=True)) * scale + bias
        largest = peak if largest is None else jnp.maximum(largest, peak)
    summed, mix = None, None
    for part, bias, block in zip(parts, biases, blocks):
        offset = jnp.concatenate([bias - largest] * (rows // HD), axis=1)
        weights = jnp.exp2(part * scale + offset)
        product = jnp.dot(weights.astype(block.dtype), block[rows:, low : low + HD], preferred_element_type=jnp.float32)
        summed = weights if summed is None else summed + weights
        mix = product if mix is None else mix + product
    total = spread(jnp.sum(summed, axis=1, keepdims=True))
    if old is not None:
        shrink = jnp.exp2(old[0] - largest)
        total, mix = total + old[1] * shrink, mix + old[2] * shrink
    return largest, total, mix


def row_stats(largest, total):
    lane = lax.broadcasted_iota(jnp.int32, largest.shape, 1)
    return jnp.transpose(jnp.where(lane == 0, largest, jnp.where(lane == 1, total, 0.0)))[:8]


def block_biases(query_ref, rows):
    wide = wide_window(query_ref, rows)
    return [block_bias(wide, stage) for stage in (1, 2)]


def own_kernel(query_ref, pair_ref, block_ref, mix_ref, stats_ref):
    rows, width = block_ref.shape[0] // 2, block_ref.shape[1]
    for place, ref in enumerate((query_ref, pair_ref)):
        for head in range(width // HD):
            low, index = head * HD, 2 * head + place
            largest, total, mix = attend(ref[:rows, low : low + HD], [block_ref], [0.0], low)
            mix_ref[index], stats_ref[2 * index], stats_ref[2 * index + 1] = mix, largest, total


def attend_own(queries, pair, block):
    rows, width = block.shape[0] // 2, block.shape[1]
    heads = width // HD
    whole = pl.BlockSpec(memory_space=VMEM)
    return pl.pallas_call(
        own_kernel,
        out_shape=(
            jax.ShapeDtypeStruct((2 * heads, rows, HD), jnp.float32),
            jax.ShapeDtypeStruct((4 * heads, rows, HD), jnp.float32),
        ),
        in_specs=[whole] * 3,
        out_specs=(whole,) * 2,
        compiler_params=params(24),
        cost_estimate=pl.CostEstimate(flops=0, bytes_accessed=0, transcendentals=0),
        name="attend_own",
    )(queries, pair, block)


def old_parts(mix_ref, stats_ref, head, place):
    index = 2 * head + place
    return stats_ref[2 * index], stats_ref[2 * index + 1], mix_ref[index]


def pair_kernel(query_ref, first_ref, second_ref, mix_ref, stats_ref, out_ref):
    rows, width = first_ref.shape[0] // 2, first_ref.shape[1]
    biases = block_biases(query_ref, rows)
    for head in range(width // HD):
        low = head * HD
        old = old_parts(mix_ref, stats_ref, head, 1)
        largest, total, mix = attend(query_ref[:rows, low : low + HD], [first_ref, second_ref], biases, low, old)
        put_message(out_ref, head, mix, row_stats(largest, total), 0)


def attend_pair(query, first, second, mix, stats):
    whole = pl.BlockSpec(memory_space=VMEM)
    return pl.pallas_call(
        pair_kernel,
        out_shape=jax.ShapeDtypeStruct(query.shape, jnp.bfloat16),
        in_specs=[whole] * 5,
        out_specs=whole,
        compiler_params=params(24),
        cost_estimate=pl.CostEstimate(flops=4_000_000_000, bytes_accessed=2_000_000, transcendentals=0),
        name="attend_pair",
    )(query, first, second, mix, stats)


def middle_kernel(query_ref, own_ref, first_ref, second_ref, after_ref, out_ref):
    rows, width = own_ref.shape[0] // 2, own_ref.shape[1]
    height = lax.axis_index("tile") % HEIGHT_TILES
    inside = (height > 0) & (height < HEIGHT_TILES - 1)

    @pl.when(inside)
    def compute():
        biases = [0.0] + block_biases(query_ref, rows)
        blocks = [own_ref, first_ref, second_ref]
        for head in range(width // HD):
            low = head * HD
            largest, total, mix = attend(query_ref[:rows, low : low + HD], blocks, biases, low)
            put_message(out_ref, head, mix, row_stats(largest, total), 0)

    @pl.when(jnp.logical_not(inside))
    def skip():
        out_ref[...] = jnp.zeros_like(out_ref)


def attend_middle(query, own, first, second, after):
    whole = pl.BlockSpec(memory_space=VMEM)
    return pl.pallas_call(
        middle_kernel,
        out_shape=jax.ShapeDtypeStruct(query.shape, jnp.bfloat16),
        in_specs=[whole] * 4 + [pl.BlockSpec(memory_space=pl.ANY)],
        out_specs=whole,
        compiler_params=params(24),
        cost_estimate=pl.CostEstimate(flops=MIDDLE_FLOPS, bytes_accessed=2_000_000, transcendentals=0),
        name="attend_middle",
    )(query, own, first, second, after)


def last_kernel(query_ref, first_ref, second_ref, old_mix_ref, old_stats_ref, message_ref, after_ref, mix_ref, stats_ref):
    rows, width = first_ref.shape[0] // 2, first_ref.shape[1]
    wide = wide_window(query_ref, rows, 1)
    biases = block_biases(query_ref, rows)
    for head in range(width // HD):
        low = head * HD
        old = old_parts(old_mix_ref, old_stats_ref, head, 0)
        largest, total, mix = attend(query_ref[:rows, low : low + HD], [first_ref, second_ref], biases, low, old)
        their_largest, their_total = message_columns(message_ref, head, rows)
        peak = jnp.maximum(largest, jnp.where(wide, their_largest, MASKED))
        shrink, share = jnp.exp2(largest - peak), jnp.where(wide, jnp.exp2(their_largest - peak), 0.0)
        stats = row_stats(peak, total * shrink + their_total * share)
        mix_ref[:, low : low + HD] = mix * shrink + message_ref[:rows, low : low + HD].astype(jnp.float32) * share
        line = lax.broadcasted_iota(jnp.int32, stats.shape, 0)
        stats_ref[head] = jnp.where(line == 2, jnp.where(wide, 1.0, 0.0), stats)


def attend_last(queries, first, second, mix, stats, message, after):
    rows, width = first.shape[0] // 2, first.shape[1]
    whole = pl.BlockSpec(memory_space=VMEM)
    return pl.pallas_call(
        last_kernel,
        out_shape=(
            jax.ShapeDtypeStruct((rows, width), jnp.float32),
            jax.ShapeDtypeStruct((width // HD, 8, rows), jnp.float32),
        ),
        in_specs=[whole] * 6 + [pl.BlockSpec(memory_space=pl.ANY)],
        out_specs=(whole, whole),
        compiler_params=params(24),
        cost_estimate=pl.CostEstimate(flops=LAST_FLOPS, bytes_accessed=2_000_000, transcendentals=0),
        name="attend_last",
    )(queries, first, second, mix, stats, message, after)


def merge_kernel(own_ref, stats_ref, middle_ref, out_ref):
    rows, width = own_ref.shape
    heads = width // HD
    height = lax.axis_index("tile") % HEIGHT_TILES
    inside = jnp.where((height > 0) & (height < HEIGHT_TILES - 1), 1.0, 0.0)
    line = lax.broadcasted_iota(jnp.int32, (8, rows), 0)
    shares = jnp.zeros((8, rows), jnp.float32)
    for head in range(heads):
        stats = stats_ref[head]
        their_largest, their_total = message_stats(middle_ref, head, rows)
        valid = stats[2:3] * inside > 0.5
        peak = jnp.maximum(stats[0:1], jnp.where(valid, their_largest, MASKED))
        shrink = jnp.exp2(stats[0:1] - peak)
        share = jnp.where(valid, jnp.exp2(their_largest - peak), 0.0)
        whole = stats[1:2] * shrink + their_total * share
        shares = jnp.where(line == 2 * head, shrink / whole, shares)
        shares = jnp.where(line == 2 * head + 1, share / whole, shares)
    shares = jnp.transpose(shares)
    for head in range(heads):
        low = head * HD
        value = own_ref[:, low : low + HD] * column(shares, 2 * head)
        value += middle_ref[:rows, low : low + HD].astype(jnp.float32) * column(shares, 2 * head + 1)
        out_ref[:, low : low + HD] = value.astype(out_ref.dtype)


def merge(own, stats, middle):
    whole = pl.BlockSpec(memory_space=VMEM)
    return pl.pallas_call(
        merge_kernel,
        out_shape=jax.ShapeDtypeStruct(own.shape, jnp.bfloat16),
        in_specs=[whole] * 3,
        out_specs=whole,
        compiler_params=params(24),
        name="merge",
    )(own, stats, middle)


def project_mine_kernel(mine_ref, weight_ref, out_ref):
    width = mine_ref.shape[1]
    for group in range(out_ref.shape[0]):
        low = group * width
        out_ref[group] = jnp.dot(mine_ref[...], weight_ref[:, low : low + width], preferred_element_type=jnp.float32)


def project_mine(mine, my_weight):
    rows, width = mine.shape
    groups = my_weight.shape[1] // width
    whole = pl.BlockSpec(memory_space=VMEM)
    return pl.pallas_call(
        project_mine_kernel,
        out_shape=jax.ShapeDtypeStruct((groups, rows, width), jnp.float32),
        in_specs=[whole] * 2,
        out_specs=whole,
        compiler_params=params(24),
        cost_estimate=pl.CostEstimate(flops=2 * groups * rows * width * width, bytes_accessed=0, transcendentals=0),
        name="project_mine",
    )(mine, my_weight)


def project_kernel(mine_ref, theirs_ref, this_ref, other_ref, out_ref, held_ref, sems):
    width, half = theirs_ref.shape[1], this_ref.shape[1]
    core = lax.rem(lax.axis_index("tile"), 2)
    copies = []
    for group in range(out_ref.shape[0]):
        side, start = divmod(group * width, half)
        their_weight = jnp.where(side == core, this_ref[:, start : start + width], other_ref[:, start : start + width])
        product = jnp.dot(theirs_ref[...], their_weight, preferred_element_type=jnp.float32)
        held_ref[group] = (mine_ref[group] + product).astype(held_ref.dtype)
        copies.append(pltpu.make_async_copy(held_ref.at[group], out_ref.at[group], sems.at[group]))
        copies[-1].start()
    for copy in copies:
        copy.wait()


def project(mine, theirs, this_half, other_half):
    whole = pl.BlockSpec(memory_space=VMEM)
    return pl.pallas_call(
        project_kernel,
        out_shape=jax.ShapeDtypeStruct(mine.shape, jnp.bfloat16),
        in_specs=[whole] * 4,
        out_specs=pl.BlockSpec(memory_space=pl.ANY),
        scratch_shapes=[pltpu.VMEM(mine.shape, jnp.bfloat16), pltpu.SemaphoreType.DMA((mine.shape[0],))],
        compiler_params=params(24),
        cost_estimate=pl.CostEstimate(flops=300_000_000, bytes_accessed=5_000_000, transcendentals=0),
        name="project",
    )(mine, theirs, this_half, other_half)


def finish_kernel(terms_ref, residual_ref, gate_ref, out_ref):
    total = jnp.sum(terms_ref[...].astype(jnp.float32), axis=0)
    out_ref[...] = (residual_ref[...].astype(jnp.float32) + gate_ref[...] * total).astype(out_ref.dtype)


def finish(terms, residual, gate_scale):
    whole = pl.BlockSpec(memory_space=VMEM)
    return pl.pallas_call(
        finish_kernel,
        out_shape=jax.ShapeDtypeStruct(residual.shape, residual.dtype),
        in_specs=[whole] * 3,
        out_specs=whole,
        compiler_params=params(24),
        cost_estimate=pl.CostEstimate(flops=10 * terms.size, bytes_accessed=2_000_000, transcendentals=0),
        name="finish",
    )(terms, residual, gate_scale.reshape(1, -1))


def shards(queries, key_rows, value_rows, windows, residual, out_weight, gate_scale):
    packed, block = pack(windows, queries, key_rows, value_rows)
    first, second = swap_times(block, False), swap_times(block, True)
    pair_asks, middle_asks = swap_pair(packed), swap_middle(packed)
    my_weight, to_send = split_weight(out_weight)
    this_half = swap_far(to_send)
    mix, stats = attend_own(packed, pair_asks, block)
    for_pair = attend_pair(pair_asks, first, second, mix, stats)
    for_middle = attend_middle(middle_asks, block, first, second, for_pair)
    other_half = swap_pair(this_half)
    mix, stats = attend_last(packed, first, second, mix, stats, swap_pair(for_pair), other_half)
    attention = merge(mix, stats, swap_middle(for_middle))
    mine = project_mine(attention, my_weight)
    terms = project(mine, swap_far(attention), this_half, other_half)
    terms = lax.all_to_all(terms, "group", 0, 0)
    return finish(terms, residual, gate_scale)


def solution(mesh):
    devices = np.asarray(mesh.devices)
    tiles, heads = devices.shape
    split = jax.sharding.Mesh(devices.reshape(tiles, 2, heads // 2), ("tile", "far", "group"))
    head = ("far", "group")
    return jax.shard_map(
        shards,
        mesh=split,
        in_specs=(
            P("tile", head),
            P("tile", head),
            P("tile", head),
            P("tile", None),
            P("tile", head),
            P(head, None),
            P(head),
        ),
        out_specs=P("tile", head),
        check_vma=False,
    )
```

```python
import functools

import jax
import jax.numpy as jnp
import numpy as np
from jax import lax
from jax.experimental import pallas as pl
from jax.experimental.pallas import tpu as pltpu
from jax.sharding import PartitionSpec as P

HD = 128
HEIGHT_TILES = 4
SIDE = 16
LOG2E = 1.4426950408889634
MASKED = -1e30
LAST_FLOPS = 400_000_000
MIDDLE_FLOPS = 600_000_000
PAIR_FLOPS = 400_000_000
HERE_FLOPS = 3_000_000_000
MESH_AXES = ("tile", "head")
VMEM = pltpu.VMEM
SMEM = pltpu.SMEM


def params(megabytes):
    return pltpu.CompilerParams(vmem_limit_bytes=megabytes * 1024 * 1024)


def places():
    tiles = lax.axis_size("tile")
    return [(tile, *divmod(tile, HEIGHT_TILES), tiles // HEIGHT_TILES) for tile in range(tiles)]


def swap_times(block, later):
    route = []
    for tile, time, height, times in places():
        partner = time + 1 if time % 2 == int(not later) else time - 1
        if 0 <= partner < times:
            route.append((tile, partner * HEIGHT_TILES + height))
    return lax.ppermute(block, "tile", route)


def swap_pair(block):
    return lax.ppermute(block, "tile", [(tile, tile ^ 1) for tile, *_ in places()])


def swap_middle(block):
    route = [(tile, tile + (1 if height == 1 else -1)) for tile, _, height, _ in places() if height in (1, 2)]
    return lax.ppermute(block, "tile", route)


def swap_far(block):
    return lax.ppermute(block, "far", [(0, 1), (1, 0)])


def split_weight_kernel(weight_ref, mine_ref, theirs_ref):
    width, half = mine_ref.shape[1], theirs_ref.shape[1]
    far = lax.axis_index("far")
    core = lax.rem(lax.axis_index("tile"), 2)
    mine_ref[...] = weight_ref[:, pl.ds(pl.multiple_of(far * width, HD), width)]
    theirs_ref[...] = weight_ref[:, pl.ds(pl.multiple_of((1 - far) * width + core * half, HD), half)]


def split_weight(out_weight):
    rows, features = out_weight.shape
    whole = pl.BlockSpec(memory_space=VMEM)
    return pl.pallas_call(
        split_weight_kernel,
        out_shape=(
            jax.ShapeDtypeStruct((rows, features // 2), out_weight.dtype),
            jax.ShapeDtypeStruct((rows, features // 4), out_weight.dtype),
        ),
        in_specs=[whole],
        out_specs=(whole,) * 2,
        compiler_params=params(24),
        cost_estimate=pl.CostEstimate(flops=0, bytes_accessed=0, transcendentals=0),
        name="split_weight",
    )(out_weight)


def pack_kernel(windows_ref, q_ref, k_ref, v_ref, packed_ref, block_ref):
    rows = q_ref.shape[0]
    block_ref[:rows] = k_ref[...]
    block_ref[rows:] = v_ref[...]
    packed_ref[:rows] = q_ref[...]
    for axis in (0, 1):
        extent = windows_ref[0, axis].astype(jnp.float32)
        packed_ref[rows:, axis * HD : (axis + 1) * HD] = jnp.full((SIDE, HD), extent, jnp.float32).astype(packed_ref.dtype)
    packed_ref[rows:, 2 * HD :] = jnp.zeros((SIDE, q_ref.shape[1] - 2 * HD), packed_ref.dtype)


def pack(windows, queries, key_rows, value_rows):
    rows, width = queries.shape
    whole = pl.BlockSpec(memory_space=VMEM)
    return pl.pallas_call(
        pack_kernel,
        out_shape=(
            jax.ShapeDtypeStruct((rows + SIDE, width), queries.dtype),
            jax.ShapeDtypeStruct((2 * rows, width), queries.dtype),
        ),
        in_specs=[pl.BlockSpec(memory_space=SMEM)] + [whole] * 3,
        out_specs=(whole, whole),
        name="pack",
    )(windows, queries, key_rows, value_rows)


def column(values, index):
    return values[:, index : index + 1]


def split_float(value):
    high = value.astype(jnp.bfloat16).astype(jnp.float32)
    rest = value - high
    middle = rest.astype(jnp.bfloat16).astype(jnp.float32)
    return high, middle, (rest - middle).astype(jnp.bfloat16).astype(jnp.float32)


def wide_window(ref, rows, axis=0):
    return jnp.max(ref[rows:, axis * HD : (axis + 1) * HD].astype(jnp.float32)) > 0.5


def has_first():
    time = lax.axis_index("tile") // HEIGHT_TILES
    return (time > 0) & (time < lax.axis_size("tile") // HEIGHT_TILES - 1)


def block_bias(wide, stage):
    return jnp.where(wide & has_first() if stage == 1 else wide, 0.0, MASKED)


def raw_scores(query, keys):
    return lax.dot_general(query, keys, (((1,), (1,)), ((), ())), preferred_element_type=jnp.float32)


def put_message(ref, head, mix, stats, row):
    rows = mix.shape[0]
    low = head * HD
    line = lax.broadcasted_iota(jnp.int32, (8, rows), 0)
    ref[:rows, low : low + HD] = mix.astype(ref.dtype)
    side = jnp.zeros((8, rows), jnp.float32)
    for index, piece in enumerate(split_float(stats[row : row + 1]) + split_float(stats[row + 1 : row + 2])):
        side = jnp.where(line == index, piece, side)
    ref[rows : rows + SIDE, low : low + HD] = jnp.concatenate([side[:, :HD], side[:, HD:]], axis=0).astype(ref.dtype)


def message_stats(ref, head, rows):
    side = ref[rows : rows + SIDE, head * HD : (head + 1) * HD].astype(jnp.float32)
    side = jnp.concatenate([side[:8], side[8:]], axis=1)
    return side[0:1] + side[1:2] + side[2:3], side[3:4] + side[4:5] + side[5:6]


def message_columns(ref, head, rows):
    line = lax.broadcasted_iota(jnp.int32, (8, rows), 0)
    largest, total = message_stats(ref, head, rows)
    columns = jnp.transpose(jnp.where(line == 0, largest, jnp.where(line == 1, total, 0.0)))
    return [jnp.broadcast_to(column(columns, index), (rows, HD)) for index in (0, 1)]


def attend(query, blocks, biases, low, old=None):
    rows = blocks[0].shape[0] // 2
    scale = HD**-0.5 * LOG2E
    spread = lambda value: jnp.broadcast_to(value, (rows, HD))
    parts = [raw_scores(query, block[:rows, low : low + HD]) for block in blocks]
    largest = None if old is None else old[0]
    for part, bias in zip(parts, biases):
        peak = spread(jnp.max(part, axis=1, keepdims=True)) * scale + bias
        largest = peak if largest is None else jnp.maximum(largest, peak)
    summed, mix = None, None
    for part, bias, block in zip(parts, biases, blocks):
        offset = jnp.concatenate([bias - largest] * (rows // HD), axis=1)
        weights = jnp.exp2(part * scale + offset)
        product = jnp.dot(weights.astype(block.dtype), block[rows:, low : low + HD], preferred_element_type=jnp.float32)
        summed = weights if summed is None else summed + weights
        mix = product if mix is None else mix + product
    total = spread(jnp.sum(summed, axis=1, keepdims=True))
    if old is not None:
        shrink = jnp.exp2(old[0] - largest)
        total, mix = total + old[1] * shrink, mix + old[2] * shrink
    return largest, total, mix


def row_stats(largest, total):
    lane = lax.broadcasted_iota(jnp.int32, largest.shape, 1)
    return jnp.transpose(jnp.where(lane == 0, largest, jnp.where(lane == 1, total, 0.0)))[:8]


def block_biases(query_ref, rows):
    wide = wide_window(query_ref, rows)
    return [block_bias(wide, stage) for stage in (1, 2)]


def own_kernel(query_ref, pair_ref, block_ref, mix_ref, stats_ref):
    rows, width = block_ref.shape[0] // 2, block_ref.shape[1]
    for place, ref in enumerate((query_ref, pair_ref)):
        for head in range(width // HD):
            low, index = head * HD, 2 * head + place
            largest, total, mix = attend(ref[:rows, low : low + HD], [block_ref], [0.0], low)
            mix_ref[index], stats_ref[2 * index], stats_ref[2 * index + 1] = mix, largest, total


def attend_own(queries, pair, block):
    rows, width = block.shape[0] // 2, block.shape[1]
    heads = width // HD
    whole = pl.BlockSpec(memory_space=VMEM)
    return pl.pallas_call(
        own_kernel,
        out_shape=(
            jax.ShapeDtypeStruct((2 * heads, rows, HD), jnp.float32),
            jax.ShapeDtypeStruct((4 * heads, rows, HD), jnp.float32),
        ),
        in_specs=[whole] * 3,
        out_specs=(whole,) * 2,
        compiler_params=params(24),
        cost_estimate=pl.CostEstimate(flops=0, bytes_accessed=0, transcendentals=0),
        name="attend_own",
    )(queries, pair, block)


def old_parts(mix_ref, stats_ref, head, place):
    index = 2 * head + place
    return stats_ref[2 * index], stats_ref[2 * index + 1], mix_ref[index]


def here_kernel(*refs):
    refs[-1][...] = jnp.zeros_like(refs[-1])


def all_here(*arrays):
    return pl.pallas_call(
        here_kernel,
        out_shape=jax.ShapeDtypeStruct((8, HD), jnp.float32),
        in_specs=[pl.BlockSpec(memory_space=pl.ANY)] * len(arrays),
        out_specs=pl.BlockSpec(memory_space=VMEM),
        compiler_params=params(4),
        cost_estimate=pl.CostEstimate(flops=HERE_FLOPS, bytes_accessed=0, transcendentals=0),
        name="all_here",
    )(*arrays)


def half_rows(weight_shape, rows, width):
    return [rows + SIDE + part * weight_shape[0] for part in range(weight_shape[1] // width)]


def pair_kernel(query_ref, first_ref, second_ref, mix_ref, stats_ref, weight_ref, after_ref, out_ref):
    rows, width = first_ref.shape[0] // 2, first_ref.shape[1]
    for part, start in enumerate(half_rows(weight_ref.shape, rows, width)):
        out_ref[start : start + weight_ref.shape[0]] = weight_ref[:, part * width : (part + 1) * width]
    biases = block_biases(query_ref, rows)
    for head in range(width // HD):
        low = head * HD
        old = old_parts(mix_ref, stats_ref, head, 1)
        largest, total, mix = attend(query_ref[:rows, low : low + HD], [first_ref, second_ref], biases, low, old)
        put_message(out_ref, head, mix, row_stats(largest, total), 0)


def attend_pair(query, first, second, mix, stats, weight, after):
    rows, width = query.shape
    whole = pl.BlockSpec(memory_space=VMEM)
    return pl.pallas_call(
        pair_kernel,
        out_shape=jax.ShapeDtypeStruct((rows + weight.size // width, width), jnp.bfloat16),
        in_specs=[whole] * 6 + [pl.BlockSpec(memory_space=pl.ANY)],
        out_specs=whole,
        compiler_params=params(24),
        cost_estimate=pl.CostEstimate(flops=PAIR_FLOPS, bytes_accessed=2_000_000, transcendentals=0),
        name="attend_pair",
    )(query, first, second, mix, stats, weight, after)


def middle_kernel(query_ref, own_ref, first_ref, second_ref, after_ref, out_ref):
    rows, width = own_ref.shape[0] // 2, own_ref.shape[1]
    height = lax.axis_index("tile") % HEIGHT_TILES
    inside = (height > 0) & (height < HEIGHT_TILES - 1)

    @pl.when(inside)
    def compute():
        biases = [0.0] + block_biases(query_ref, rows)
        blocks = [own_ref, first_ref, second_ref]
        for head in range(width // HD):
            low = head * HD
            largest, total, mix = attend(query_ref[:rows, low : low + HD], blocks, biases, low)
            put_message(out_ref, head, mix, row_stats(largest, total), 0)

    @pl.when(jnp.logical_not(inside))
    def skip():
        out_ref[...] = jnp.zeros_like(out_ref)


def attend_middle(query, own, first, second, after):
    whole = pl.BlockSpec(memory_space=VMEM)
    return pl.pallas_call(
        middle_kernel,
        out_shape=jax.ShapeDtypeStruct(query.shape, jnp.bfloat16),
        in_specs=[whole] * 4 + [pl.BlockSpec(memory_space=pl.ANY)],
        out_specs=whole,
        compiler_params=params(24),
        cost_estimate=pl.CostEstimate(flops=MIDDLE_FLOPS, bytes_accessed=2_000_000, transcendentals=0),
        name="attend_middle",
    )(query, own, first, second, after)


def last_kernel(query_ref, first_ref, second_ref, old_mix_ref, old_stats_ref, message_ref, mix_ref, stats_ref):
    rows, width = first_ref.shape[0] // 2, first_ref.shape[1]
    wide = wide_window(query_ref, rows, 1)
    biases = block_biases(query_ref, rows)
    for head in range(width // HD):
        low = head * HD
        old = old_parts(old_mix_ref, old_stats_ref, head, 0)
        largest, total, mix = attend(query_ref[:rows, low : low + HD], [first_ref, second_ref], biases, low, old)
        their_largest, their_total = message_columns(message_ref, head, rows)
        peak = jnp.maximum(largest, jnp.where(wide, their_largest, MASKED))
        shrink, share = jnp.exp2(largest - peak), jnp.where(wide, jnp.exp2(their_largest - peak), 0.0)
        stats = row_stats(peak, total * shrink + their_total * share)
        mix_ref[:, low : low + HD] = mix * shrink + message_ref[:rows, low : low + HD].astype(jnp.float32) * share
        line = lax.broadcasted_iota(jnp.int32, stats.shape, 0)
        stats_ref[head] = jnp.where(line == 2, jnp.where(wide, 1.0, 0.0), stats)


def attend_last(queries, first, second, mix, stats, message):
    rows, width = first.shape[0] // 2, first.shape[1]
    whole = pl.BlockSpec(memory_space=VMEM)
    return pl.pallas_call(
        last_kernel,
        out_shape=(
            jax.ShapeDtypeStruct((rows, width), jnp.float32),
            jax.ShapeDtypeStruct((width // HD, 8, rows), jnp.float32),
        ),
        in_specs=[whole] * 6,
        out_specs=(whole, whole),
        compiler_params=params(24),
        cost_estimate=pl.CostEstimate(flops=LAST_FLOPS, bytes_accessed=2_000_000, transcendentals=0),
        name="attend_last",
    )(queries, first, second, mix, stats, message)


def merge_kernel(own_ref, stats_ref, middle_ref, out_ref):
    rows, width = own_ref.shape
    heads = width // HD
    height = lax.axis_index("tile") % HEIGHT_TILES
    inside = jnp.where((height > 0) & (height < HEIGHT_TILES - 1), 1.0, 0.0)
    line = lax.broadcasted_iota(jnp.int32, (8, rows), 0)
    shares = jnp.zeros((8, rows), jnp.float32)
    for head in range(heads):
        stats = stats_ref[head]
        their_largest, their_total = message_stats(middle_ref, head, rows)
        valid = stats[2:3] * inside > 0.5
        peak = jnp.maximum(stats[0:1], jnp.where(valid, their_largest, MASKED))
        shrink = jnp.exp2(stats[0:1] - peak)
        share = jnp.where(valid, jnp.exp2(their_largest - peak), 0.0)
        whole = stats[1:2] * shrink + their_total * share
        shares = jnp.where(line == 2 * head, shrink / whole, shares)
        shares = jnp.where(line == 2 * head + 1, share / whole, shares)
    shares = jnp.transpose(shares)
    for head in range(heads):
        low = head * HD
        value = own_ref[:, low : low + HD] * column(shares, 2 * head)
        value += middle_ref[:rows, low : low + HD].astype(jnp.float32) * column(shares, 2 * head + 1)
        out_ref[:, low : low + HD] = value.astype(out_ref.dtype)


def merge(own, stats, middle):
    whole = pl.BlockSpec(memory_space=VMEM)
    return pl.pallas_call(
        merge_kernel,
        out_shape=jax.ShapeDtypeStruct(own.shape, jnp.bfloat16),
        in_specs=[whole] * 3,
        out_specs=whole,
        compiler_params=params(24),
        name="merge",
    )(own, stats, middle)


def project_mine_kernel(mine_ref, weight_ref, out_ref):
    width = mine_ref.shape[1]
    for group in range(out_ref.shape[0]):
        low = group * width
        out_ref[group] = jnp.dot(mine_ref[...], weight_ref[:, low : low + width], preferred_element_type=jnp.float32)


def project_mine(mine, my_weight):
    rows, width = mine.shape
    groups = my_weight.shape[1] // width
    whole = pl.BlockSpec(memory_space=VMEM)
    return pl.pallas_call(
        project_mine_kernel,
        out_shape=jax.ShapeDtypeStruct((groups, rows, width), jnp.float32),
        in_specs=[whole] * 2,
        out_specs=whole,
        compiler_params=params(24),
        cost_estimate=pl.CostEstimate(flops=2 * groups * rows * width * width, bytes_accessed=0, transcendentals=0),
        name="project_mine",
    )(mine, my_weight)


def project_kernel(mine_ref, theirs_ref, this_ref, other_ref, out_ref, held_ref, sems):
    rows, width = theirs_ref.shape
    core = lax.rem(lax.axis_index("tile"), 2)
    starts = half_rows(this_ref.shape, rows, width)
    copies = []
    for group in range(out_ref.shape[0]):
        side, part = divmod(group, len(starts))
        this = this_ref[:, part * width : (part + 1) * width]
        other = other_ref[starts[part] : starts[part] + this.shape[0]]
        their_weight = jnp.where(side == core, this, other)
        product = jnp.dot(theirs_ref[...], their_weight, preferred_element_type=jnp.float32)
        held_ref[group] = (mine_ref[group] + product).astype(held_ref.dtype)
        copies.append(pltpu.make_async_copy(held_ref.at[group], out_ref.at[group], sems.at[group]))
        copies[-1].start()
    for copy in copies:
        copy.wait()


def project(mine, theirs, this_half, pair_message):
    whole = pl.BlockSpec(memory_space=VMEM)
    return pl.pallas_call(
        project_kernel,
        out_shape=jax.ShapeDtypeStruct(mine.shape, jnp.bfloat16),
        in_specs=[whole] * 4,
        out_specs=pl.BlockSpec(memory_space=pl.ANY),
        scratch_shapes=[pltpu.VMEM(mine.shape, jnp.bfloat16), pltpu.SemaphoreType.DMA((mine.shape[0],))],
        compiler_params=params(24),
        cost_estimate=pl.CostEstimate(flops=300_000_000, bytes_accessed=5_000_000, transcendentals=0),
        name="project",
    )(mine, theirs, this_half, pair_message)


def finish_kernel(terms_ref, residual_ref, gate_ref, out_ref):
    total = jnp.sum(terms_ref[...].astype(jnp.float32), axis=0)
    out_ref[...] = (residual_ref[...].astype(jnp.float32) + gate_ref[...] * total).astype(out_ref.dtype)


def finish(terms, residual, gate_scale):
    whole = pl.BlockSpec(memory_space=VMEM)
    return pl.pallas_call(
        finish_kernel,
        out_shape=jax.ShapeDtypeStruct(residual.shape, residual.dtype),
        in_specs=[whole] * 3,
        out_specs=whole,
        compiler_params=params(24),
        cost_estimate=pl.CostEstimate(flops=10 * terms.size, bytes_accessed=2_000_000, transcendentals=0),
        name="finish",
    )(terms, residual, gate_scale.reshape(1, -1))


def shards(queries, key_rows, value_rows, windows, residual, out_weight, gate_scale):
    packed, block = pack(windows, queries, key_rows, value_rows)
    first, second = swap_times(block, False), swap_times(block, True)
    pair_asks, middle_asks = swap_pair(packed), swap_middle(packed)
    my_weight, to_send = split_weight(out_weight)
    this_half = swap_far(to_send)
    mix, stats = attend_own(packed, pair_asks, block)
    here = all_here(first, second, middle_asks)
    for_pair = attend_pair(pair_asks, first, second, mix, stats, this_half, here)
    for_middle = attend_middle(middle_asks, block, first, second, for_pair)
    from_pair = swap_pair(for_pair)
    mix, stats = attend_last(packed, first, second, mix, stats, from_pair)
    attention = merge(mix, stats, swap_middle(for_middle))
    mine = project_mine(attention, my_weight)
    terms = project(mine, swap_far(attention), this_half, from_pair)
    terms = lax.all_to_all(terms, "group", 0, 0)
    return finish(terms, residual, gate_scale)


def solution(mesh):
    devices = np.asarray(mesh.devices)
    tiles, heads = devices.shape
    split = jax.sharding.Mesh(devices.reshape(tiles, 2, heads // 2), ("tile", "far", "group"))
    head = ("far", "group")
    return jax.shard_map(
        shards,
        mesh=split,
        in_specs=(
            P("tile", head),
            P("tile", head),
            P("tile", head),
            P("tile", None),
            P("tile", head),
            P(head, None),
            P(head),
        ),
        out_specs=P("tile", head),
        check_vma=False,
    )
```

```python
import functools

import jax
import jax.numpy as jnp
import numpy as np
from jax import lax
from jax.experimental import pallas as pl
from jax.experimental.pallas import tpu as pltpu
from jax.sharding import PartitionSpec as P

HD = 128
HEIGHT_TILES = 4
SIDE = 16
LOG2E = 1.4426950408889634
MASKED = -1e30
LAST_FLOPS = 400_000_000
MIDDLE_FLOPS = 600_000_000
PAIR_FLOPS = 400_000_000
HERE_FLOPS = 3_000_000_000
MESH_AXES = ("tile", "head")
VMEM = pltpu.VMEM
SMEM = pltpu.SMEM


def params(megabytes):
    return pltpu.CompilerParams(vmem_limit_bytes=megabytes * 1024 * 1024)


def places():
    tiles = lax.axis_size("tile")
    return [(tile, *divmod(tile, HEIGHT_TILES), tiles // HEIGHT_TILES) for tile in range(tiles)]


def swap_times(block, later):
    route = []
    for tile, time, height, times in places():
        partner = time + 1 if time % 2 == int(not later) else time - 1
        if 0 <= partner < times:
            route.append((tile, partner * HEIGHT_TILES + height))
    return lax.ppermute(block, "tile", route)


def swap_pair(block):
    return lax.ppermute(block, "tile", [(tile, tile ^ 1) for tile, *_ in places()])


def swap_middle(block):
    route = [(tile, tile + (1 if height == 1 else -1)) for tile, _, height, _ in places() if height in (1, 2)]
    return lax.ppermute(block, "tile", route)


def swap_far(block):
    return lax.ppermute(block, "far", [(0, 1), (1, 0)])


def copy_columns(weight_ref, start, out_ref, sem):
    return pltpu.make_async_copy(weight_ref.at[:, pl.ds(pl.multiple_of(start, HD), out_ref.shape[1])], out_ref, sem)


def split_weight_kernel(weight_ref, theirs_ref, sem):
    half = theirs_ref.shape[1]
    core = lax.rem(lax.axis_index("tile"), 2)
    copy = copy_columns(weight_ref, ((1 - lax.axis_index("far")) * 2 + core) * half, theirs_ref, sem)
    copy.start()
    copy.wait()


def split_weight(out_weight):
    rows, features = out_weight.shape
    return pl.pallas_call(
        split_weight_kernel,
        out_shape=jax.ShapeDtypeStruct((rows, features // 4), out_weight.dtype),
        in_specs=[pl.BlockSpec(memory_space=pl.ANY)],
        out_specs=pl.BlockSpec(memory_space=VMEM),
        scratch_shapes=[pltpu.SemaphoreType.DMA],
        compiler_params=params(24),
        cost_estimate=pl.CostEstimate(flops=0, bytes_accessed=0, transcendentals=0),
        name="split_weight",
    )(pltpu.with_memory_space_constraint(out_weight, pltpu.HBM))


def pack_kernel(windows_ref, q_ref, k_ref, v_ref, packed_ref, block_ref):
    rows = q_ref.shape[0]
    block_ref[:rows] = k_ref[...]
    block_ref[rows:] = v_ref[...]
    packed_ref[:rows] = q_ref[...]
    for axis in (0, 1):
        extent = windows_ref[0, axis].astype(jnp.float32)
        packed_ref[rows:, axis * HD : (axis + 1) * HD] = jnp.full((SIDE, HD), extent, jnp.float32).astype(packed_ref.dtype)
    packed_ref[rows:, 2 * HD :] = jnp.zeros((SIDE, q_ref.shape[1] - 2 * HD), packed_ref.dtype)


def pack(windows, queries, key_rows, value_rows):
    rows, width = queries.shape
    whole = pl.BlockSpec(memory_space=VMEM)
    return pl.pallas_call(
        pack_kernel,
        out_shape=(
            jax.ShapeDtypeStruct((rows + SIDE, width), queries.dtype),
            jax.ShapeDtypeStruct((2 * rows, width), queries.dtype),
        ),
        in_specs=[pl.BlockSpec(memory_space=SMEM)] + [whole] * 3,
        out_specs=(whole, whole),
        name="pack",
    )(windows, queries, key_rows, value_rows)


def column(values, index):
    return values[:, index : index + 1]


def split_float(value):
    high = value.astype(jnp.bfloat16).astype(jnp.float32)
    rest = value - high
    middle = rest.astype(jnp.bfloat16).astype(jnp.float32)
    return high, middle, (rest - middle).astype(jnp.bfloat16).astype(jnp.float32)


def wide_window(ref, rows, axis=0):
    return jnp.max(ref[rows:, axis * HD : (axis + 1) * HD].astype(jnp.float32)) > 0.5


def has_first():
    time = lax.axis_index("tile") // HEIGHT_TILES
    return (time > 0) & (time < lax.axis_size("tile") // HEIGHT_TILES - 1)


def block_bias(wide, stage):
    return jnp.where(wide & has_first() if stage == 1 else wide, 0.0, MASKED)


def raw_scores(query, keys):
    return lax.dot_general(query, keys, (((1,), (1,)), ((), ())), preferred_element_type=jnp.float32)


def put_message(ref, head, mix, stats, row):
    rows = mix.shape[0]
    low = head * HD
    line = lax.broadcasted_iota(jnp.int32, (8, rows), 0)
    ref[:rows, low : low + HD] = mix.astype(ref.dtype)
    side = jnp.zeros((8, rows), jnp.float32)
    for index, piece in enumerate(split_float(stats[row : row + 1]) + split_float(stats[row + 1 : row + 2])):
        side = jnp.where(line == index, piece, side)
    ref[rows : rows + SIDE, low : low + HD] = jnp.concatenate([side[:, :HD], side[:, HD:]], axis=0).astype(ref.dtype)


def message_stats(ref, head, rows):
    side = ref[rows : rows + SIDE, head * HD : (head + 1) * HD].astype(jnp.float32)
    side = jnp.concatenate([side[:8], side[8:]], axis=1)
    return side[0:1] + side[1:2] + side[2:3], side[3:4] + side[4:5] + side[5:6]


def message_columns(ref, head, rows):
    line = lax.broadcasted_iota(jnp.int32, (8, rows), 0)
    largest, total = message_stats(ref, head, rows)
    columns = jnp.transpose(jnp.where(line == 0, largest, jnp.where(line == 1, total, 0.0)))
    return [jnp.broadcast_to(column(columns, index), (rows, HD)) for index in (0, 1)]


def attend(query, blocks, biases, low, old=None):
    rows = blocks[0].shape[0] // 2
    scale = HD**-0.5 * LOG2E
    spread = lambda value: jnp.broadcast_to(value, (rows, HD))
    parts = [raw_scores(query, block[:rows, low : low + HD]) for block in blocks]
    largest = None if old is None else old[0]
    for part, bias in zip(parts, biases):
        peak = spread(jnp.max(part, axis=1, keepdims=True)) * scale + bias
        largest = peak if largest is None else jnp.maximum(largest, peak)
    summed, mix = None, None
    for part, bias, block in zip(parts, biases, blocks):
        offset = jnp.concatenate([bias - largest] * (rows // HD), axis=1)
        weights = jnp.exp2(part * scale + offset)
        product = jnp.dot(weights.astype(block.dtype), block[rows:, low : low + HD], preferred_element_type=jnp.float32)
        summed = weights if summed is None else summed + weights
        mix = product if mix is None else mix + product
    total = spread(jnp.sum(summed, axis=1, keepdims=True))
    if old is not None:
        shrink = jnp.exp2(old[0] - largest)
        total, mix = total + old[1] * shrink, mix + old[2] * shrink
    return largest, total, mix


def row_stats(largest, total):
    lane = lax.broadcasted_iota(jnp.int32, largest.shape, 1)
    return jnp.transpose(jnp.where(lane == 0, largest, jnp.where(lane == 1, total, 0.0)))[:8]


def block_biases(query_ref, rows):
    wide = wide_window(query_ref, rows)
    return [block_bias(wide, stage) for stage in (1, 2)]


def own_kernel(query_ref, pair_ref, block_ref, weight_ref, mix_ref, stats_ref, mine_ref, sem):
    copy = copy_columns(weight_ref, lax.axis_index("far") * mine_ref.shape[1], mine_ref, sem)
    copy.start()
    rows, width = block_ref.shape[0] // 2, block_ref.shape[1]
    for place, ref in enumerate((query_ref, pair_ref)):
        for head in range(width // HD):
            low, index = head * HD, 2 * head + place
            largest, total, mix = attend(ref[:rows, low : low + HD], [block_ref], [0.0], low)
            mix_ref[index], stats_ref[2 * index], stats_ref[2 * index + 1] = mix, largest, total
    copy.wait()


def attend_own(queries, pair, block, out_weight):
    rows, width = block.shape[0] // 2, block.shape[1]
    heads = width // HD
    whole = pl.BlockSpec(memory_space=VMEM)
    return pl.pallas_call(
        own_kernel,
        out_shape=(
            jax.ShapeDtypeStruct((2 * heads, rows, HD), jnp.float32),
            jax.ShapeDtypeStruct((4 * heads, rows, HD), jnp.float32),
            jax.ShapeDtypeStruct((out_weight.shape[0], out_weight.shape[1] // 2), out_weight.dtype),
        ),
        in_specs=[whole] * 3 + [pl.BlockSpec(memory_space=pl.ANY)],
        out_specs=(whole,) * 3,
        scratch_shapes=[pltpu.SemaphoreType.DMA],
        compiler_params=params(24),
        cost_estimate=pl.CostEstimate(flops=0, bytes_accessed=0, transcendentals=0),
        name="attend_own",
    )(queries, pair, block, pltpu.with_memory_space_constraint(out_weight, pltpu.HBM))


def old_parts(mix_ref, stats_ref, head, place):
    index = 2 * head + place
    return stats_ref[2 * index], stats_ref[2 * index + 1], mix_ref[index]


def here_kernel(*refs):
    refs[-1][...] = jnp.zeros_like(refs[-1])


def all_here(*arrays):
    return pl.pallas_call(
        here_kernel,
        out_shape=jax.ShapeDtypeStruct((8, HD), jnp.float32),
        in_specs=[pl.BlockSpec(memory_space=pl.ANY)] * len(arrays),
        out_specs=pl.BlockSpec(memory_space=VMEM),
        compiler_params=params(4),
        cost_estimate=pl.CostEstimate(flops=HERE_FLOPS, bytes_accessed=0, transcendentals=0),
        name="all_here",
    )(*arrays)


def half_rows(weight_shape, rows, width):
    return [rows + SIDE + part * weight_shape[0] for part in range(weight_shape[1] // width)]


def pair_kernel(query_ref, first_ref, second_ref, mix_ref, stats_ref, weight_ref, after_ref, out_ref):
    rows, width = first_ref.shape[0] // 2, first_ref.shape[1]
    for part, start in enumerate(half_rows(weight_ref.shape, rows, width)):
        out_ref[start : start + weight_ref.shape[0]] = weight_ref[:, part * width : (part + 1) * width]
    biases = block_biases(query_ref, rows)
    for head in range(width // HD):
        low = head * HD
        old = old_parts(mix_ref, stats_ref, head, 1)
        largest, total, mix = attend(query_ref[:rows, low : low + HD], [first_ref, second_ref], biases, low, old)
        put_message(out_ref, head, mix, row_stats(largest, total), 0)


def attend_pair(query, first, second, mix, stats, weight, after):
    rows, width = query.shape
    whole = pl.BlockSpec(memory_space=VMEM)
    return pl.pallas_call(
        pair_kernel,
        out_shape=jax.ShapeDtypeStruct((rows + weight.size // width, width), jnp.bfloat16),
        in_specs=[whole] * 6 + [pl.BlockSpec(memory_space=pl.ANY)],
        out_specs=whole,
        compiler_params=params(24),
        cost_estimate=pl.CostEstimate(flops=PAIR_FLOPS, bytes_accessed=2_000_000, transcendentals=0),
        name="attend_pair",
    )(query, first, second, mix, stats, weight, after)


def middle_kernel(query_ref, own_ref, first_ref, second_ref, after_ref, out_ref):
    rows, width = own_ref.shape[0] // 2, own_ref.shape[1]
    height = lax.axis_index("tile") % HEIGHT_TILES
    inside = (height > 0) & (height < HEIGHT_TILES - 1)

    @pl.when(inside)
    def compute():
        biases = [0.0] + block_biases(query_ref, rows)
        blocks = [own_ref, first_ref, second_ref]
        for head in range(width // HD):
            low = head * HD
            largest, total, mix = attend(query_ref[:rows, low : low + HD], blocks, biases, low)
            put_message(out_ref, head, mix, row_stats(largest, total), 0)

    @pl.when(jnp.logical_not(inside))
    def skip():
        out_ref[...] = jnp.zeros_like(out_ref)


def attend_middle(query, own, first, second, after):
    whole = pl.BlockSpec(memory_space=VMEM)
    return pl.pallas_call(
        middle_kernel,
        out_shape=jax.ShapeDtypeStruct(query.shape, jnp.bfloat16),
        in_specs=[whole] * 4 + [pl.BlockSpec(memory_space=pl.ANY)],
        out_specs=whole,
        compiler_params=params(24),
        cost_estimate=pl.CostEstimate(flops=MIDDLE_FLOPS, bytes_accessed=2_000_000, transcendentals=0),
        name="attend_middle",
    )(query, own, first, second, after)


def last_kernel(query_ref, first_ref, second_ref, old_mix_ref, old_stats_ref, message_ref, mix_ref, stats_ref):
    rows, width = first_ref.shape[0] // 2, first_ref.shape[1]
    wide = wide_window(query_ref, rows, 1)
    biases = block_biases(query_ref, rows)
    for head in range(width // HD):
        low = head * HD
        old = old_parts(old_mix_ref, old_stats_ref, head, 0)
        largest, total, mix = attend(query_ref[:rows, low : low + HD], [first_ref, second_ref], biases, low, old)
        their_largest, their_total = message_columns(message_ref, head, rows)
        peak = jnp.maximum(largest, jnp.where(wide, their_largest, MASKED))
        shrink, share = jnp.exp2(largest - peak), jnp.where(wide, jnp.exp2(their_largest - peak), 0.0)
        stats = row_stats(peak, total * shrink + their_total * share)
        mix_ref[:, low : low + HD] = mix * shrink + message_ref[:rows, low : low + HD].astype(jnp.float32) * share
        line = lax.broadcasted_iota(jnp.int32, stats.shape, 0)
        stats_ref[head] = jnp.where(line == 2, jnp.where(wide, 1.0, 0.0), stats)


def attend_last(queries, first, second, mix, stats, message):
    rows, width = first.shape[0] // 2, first.shape[1]
    whole = pl.BlockSpec(memory_space=VMEM)
    return pl.pallas_call(
        last_kernel,
        out_shape=(
            jax.ShapeDtypeStruct((rows, width), jnp.float32),
            jax.ShapeDtypeStruct((width // HD, 8, rows), jnp.float32),
        ),
        in_specs=[whole] * 6,
        out_specs=(whole, whole),
        compiler_params=params(24),
        cost_estimate=pl.CostEstimate(flops=LAST_FLOPS, bytes_accessed=2_000_000, transcendentals=0),
        name="attend_last",
    )(queries, first, second, mix, stats, message)


def merge_kernel(own_ref, stats_ref, middle_ref, out_ref):
    rows, width = own_ref.shape
    heads = width // HD
    height = lax.axis_index("tile") % HEIGHT_TILES
    inside = jnp.where((height > 0) & (height < HEIGHT_TILES - 1), 1.0, 0.0)
    line = lax.broadcasted_iota(jnp.int32, (8, rows), 0)
    shares = jnp.zeros((8, rows), jnp.float32)
    for head in range(heads):
        stats = stats_ref[head]
        their_largest, their_total = message_stats(middle_ref, head, rows)
        valid = stats[2:3] * inside > 0.5
        peak = jnp.maximum(stats[0:1], jnp.where(valid, their_largest, MASKED))
        shrink = jnp.exp2(stats[0:1] - peak)
        share = jnp.where(valid, jnp.exp2(their_largest - peak), 0.0)
        whole = stats[1:2] * shrink + their_total * share
        shares = jnp.where(line == 2 * head, shrink / whole, shares)
        shares = jnp.where(line == 2 * head + 1, share / whole, shares)
    shares = jnp.transpose(shares)
    for head in range(heads):
        low = head * HD
        value = own_ref[:, low : low + HD] * column(shares, 2 * head)
        value += middle_ref[:rows, low : low + HD].astype(jnp.float32) * column(shares, 2 * head + 1)
        out_ref[:, low : low + HD] = value.astype(out_ref.dtype)


def merge(own, stats, middle):
    whole = pl.BlockSpec(memory_space=VMEM)
    return pl.pallas_call(
        merge_kernel,
        out_shape=jax.ShapeDtypeStruct(own.shape, jnp.bfloat16),
        in_specs=[whole] * 3,
        out_specs=whole,
        compiler_params=params(24),
        name="merge",
    )(own, stats, middle)


def project_mine_kernel(mine_ref, weight_ref, out_ref):
    width = mine_ref.shape[1]
    for group in range(out_ref.shape[0]):
        low = group * width
        out_ref[group] = jnp.dot(mine_ref[...], weight_ref[:, low : low + width], preferred_element_type=jnp.float32)


def project_mine(mine, my_weight):
    rows, width = mine.shape
    groups = my_weight.shape[1] // width
    whole = pl.BlockSpec(memory_space=VMEM)
    return pl.pallas_call(
        project_mine_kernel,
        out_shape=jax.ShapeDtypeStruct((groups, rows, width), jnp.float32),
        in_specs=[whole] * 2,
        out_specs=whole,
        compiler_params=params(24),
        cost_estimate=pl.CostEstimate(flops=2 * groups * rows * width * width, bytes_accessed=0, transcendentals=0),
        name="project_mine",
    )(mine, my_weight)


def project_kernel(mine_ref, theirs_ref, this_ref, other_ref, out_ref, held_ref, sems):
    rows, width = theirs_ref.shape
    core = lax.rem(lax.axis_index("tile"), 2)
    starts = half_rows(this_ref.shape, rows, width)
    copies = []
    for group in range(out_ref.shape[0]):
        side, part = divmod(group, len(starts))
        this = this_ref[:, part * width : (part + 1) * width]
        other = other_ref[starts[part] : starts[part] + this.shape[0]]
        their_weight = jnp.where(side == core, this, other)
        product = jnp.dot(theirs_ref[...], their_weight, preferred_element_type=jnp.float32)
        held_ref[group] = (mine_ref[group] + product).astype(held_ref.dtype)
        copies.append(pltpu.make_async_copy(held_ref.at[group], out_ref.at[group], sems.at[group]))
        copies[-1].start()
    for copy in copies:
        copy.wait()


def project(mine, theirs, this_half, pair_message):
    whole = pl.BlockSpec(memory_space=VMEM)
    return pl.pallas_call(
        project_kernel,
        out_shape=jax.ShapeDtypeStruct(mine.shape, jnp.bfloat16),
        in_specs=[whole] * 4,
        out_specs=pl.BlockSpec(memory_space=pl.ANY),
        scratch_shapes=[pltpu.VMEM(mine.shape, jnp.bfloat16), pltpu.SemaphoreType.DMA((mine.shape[0],))],
        compiler_params=params(24),
        cost_estimate=pl.CostEstimate(flops=300_000_000, bytes_accessed=5_000_000, transcendentals=0),
        name="project",
    )(mine, theirs, this_half, pair_message)


def finish_kernel(terms_ref, residual_ref, gate_ref, out_ref):
    total = jnp.sum(terms_ref[...].astype(jnp.float32), axis=0)
    out_ref[...] = (residual_ref[...].astype(jnp.float32) + gate_ref[...] * total).astype(out_ref.dtype)


def finish(terms, residual, gate_scale):
    whole = pl.BlockSpec(memory_space=VMEM)
    return pl.pallas_call(
        finish_kernel,
        out_shape=jax.ShapeDtypeStruct(residual.shape, residual.dtype),
        in_specs=[whole] * 3,
        out_specs=whole,
        compiler_params=params(24),
        cost_estimate=pl.CostEstimate(flops=10 * terms.size, bytes_accessed=2_000_000, transcendentals=0),
        name="finish",
    )(terms, residual, gate_scale.reshape(1, -1))


def shards(queries, key_rows, value_rows, windows, residual, out_weight, gate_scale):
    packed, block = pack(windows, queries, key_rows, value_rows)
    first, second = swap_times(block, False), swap_times(block, True)
    pair_asks, middle_asks = swap_pair(packed), swap_middle(packed)
    this_half = swap_far(split_weight(out_weight))
    mix, stats, my_weight = attend_own(packed, pair_asks, block, out_weight)
    here = all_here(first, second, middle_asks)
    for_pair = attend_pair(pair_asks, first, second, mix, stats, this_half, here)
    for_middle = attend_middle(middle_asks, block, first, second, for_pair)
    from_pair = swap_pair(for_pair)
    mix, stats = attend_last(packed, first, second, mix, stats, from_pair)
    attention = merge(mix, stats, swap_middle(for_middle))
    mine = project_mine(attention, my_weight)
    terms = project(mine, swap_far(attention), this_half, from_pair)
    terms = lax.all_to_all(terms, "group", 0, 0)
    return finish(terms, residual, gate_scale)


def solution(mesh):
    devices = np.asarray(mesh.devices)
    tiles, heads = devices.shape
    split = jax.sharding.Mesh(devices.reshape(tiles, 2, heads // 2), ("tile", "far", "group"))
    head = ("far", "group")
    return jax.shard_map(
        shards,
        mesh=split,
        in_specs=(
            P("tile", head),
            P("tile", head),
            P("tile", head),
            P("tile", None),
            P("tile", head),
            P(head, None),
            P(head),
        ),
        out_specs=P("tile", head),
        check_vma=False,
    )
```

```python
import functools

import jax
import jax.numpy as jnp
import numpy as np
from jax import lax
from jax.experimental import pallas as pl
from jax.experimental.pallas import tpu as pltpu
from jax.sharding import PartitionSpec as P

HD = 128
HEIGHT_TILES = 4
SIDE = 16
LOG2E = 1.4426950408889634
MASKED = -1e30
LAST_FLOPS = 400_000_000
MIDDLE_FLOPS = 600_000_000
PAIR_FLOPS = 400_000_000
HERE_FLOPS = 3_000_000_000
MESH_AXES = ("tile", "head")
VMEM = pltpu.VMEM
SMEM = pltpu.SMEM


def params(megabytes):
    return pltpu.CompilerParams(vmem_limit_bytes=megabytes * 1024 * 1024)


def places():
    tiles = lax.axis_size("tile")
    return [(tile, *divmod(tile, HEIGHT_TILES), tiles // HEIGHT_TILES) for tile in range(tiles)]


def swap_times(block, later):
    route = []
    for tile, time, height, times in places():
        partner = time + 1 if time % 2 == int(not later) else time - 1
        if 0 <= partner < times:
            route.append((tile, partner * HEIGHT_TILES + height))
    return lax.ppermute(block, "tile", route)


def swap_pair(block):
    return lax.ppermute(block, "tile", [(tile, tile ^ 1) for tile, *_ in places()])


def swap_middle(block):
    route = [(tile, tile + (1 if height == 1 else -1)) for tile, _, height, _ in places() if height in (1, 2)]
    return lax.ppermute(block, "tile", route)


def swap_far(block):
    return lax.ppermute(block, "far", [(0, 1), (1, 0)])


def copy_columns(weight_ref, start, out_ref, sem):
    return pltpu.make_async_copy(weight_ref.at[:, pl.ds(pl.multiple_of(start, HD), out_ref.shape[1])], out_ref, sem)


def split_weight_kernel(weight_ref, theirs_ref, sem):
    half = theirs_ref.shape[1]
    core = lax.rem(lax.axis_index("tile"), 2)
    copy = copy_columns(weight_ref, ((1 - lax.axis_index("far")) * 2 + core) * half, theirs_ref, sem)
    copy.start()
    copy.wait()


def split_weight(out_weight):
    rows, features = out_weight.shape
    return pl.pallas_call(
        split_weight_kernel,
        out_shape=jax.ShapeDtypeStruct((rows, features // 4), out_weight.dtype),
        in_specs=[pl.BlockSpec(memory_space=pl.ANY)],
        out_specs=pl.BlockSpec(memory_space=VMEM),
        scratch_shapes=[pltpu.SemaphoreType.DMA],
        compiler_params=params(24),
        cost_estimate=pl.CostEstimate(flops=0, bytes_accessed=0, transcendentals=0),
        name="split_weight",
    )(pltpu.with_memory_space_constraint(out_weight, pltpu.HBM))


def pack_kernel(windows_ref, q_ref, k_ref, v_ref, packed_ref, block_ref):
    rows = q_ref.shape[0]
    block_ref[:rows] = k_ref[...]
    block_ref[rows:] = v_ref[...]
    packed_ref[:rows] = q_ref[...]
    for axis in (0, 1):
        extent = windows_ref[0, axis].astype(jnp.float32)
        packed_ref[rows:, axis * HD : (axis + 1) * HD] = jnp.full((SIDE, HD), extent, jnp.float32).astype(packed_ref.dtype)
    packed_ref[rows:, 2 * HD :] = jnp.zeros((SIDE, q_ref.shape[1] - 2 * HD), packed_ref.dtype)


def pack(windows, queries, key_rows, value_rows):
    rows, width = queries.shape
    whole = pl.BlockSpec(memory_space=VMEM)
    return pl.pallas_call(
        pack_kernel,
        out_shape=(
            jax.ShapeDtypeStruct((rows + SIDE, width), queries.dtype),
            jax.ShapeDtypeStruct((2 * rows, width), queries.dtype),
        ),
        in_specs=[pl.BlockSpec(memory_space=SMEM)] + [whole] * 3,
        out_specs=(whole, whole),
        name="pack",
    )(windows, queries, key_rows, value_rows)


def column(values, index):
    return values[:, index : index + 1]


def split_float(value):
    high = value.astype(jnp.bfloat16).astype(jnp.float32)
    rest = value - high
    middle = rest.astype(jnp.bfloat16).astype(jnp.float32)
    return high, middle, (rest - middle).astype(jnp.bfloat16).astype(jnp.float32)


def wide_window(ref, rows, axis=0):
    return jnp.max(ref[rows:, axis * HD : (axis + 1) * HD].astype(jnp.float32)) > 0.5


def has_first():
    time = lax.axis_index("tile") // HEIGHT_TILES
    return (time > 0) & (time < lax.axis_size("tile") // HEIGHT_TILES - 1)


def block_bias(wide, stage):
    return jnp.where(wide & has_first() if stage == 1 else wide, 0.0, MASKED)


def raw_scores(query, keys):
    return lax.dot_general(query, keys, (((1,), (1,)), ((), ())), preferred_element_type=jnp.float32)


def put_message(ref, head, mix, stats, row):
    rows = mix.shape[0]
    low = head * HD
    line = lax.broadcasted_iota(jnp.int32, (8, rows), 0)
    ref[:rows, low : low + HD] = mix.astype(ref.dtype)
    side = jnp.zeros((8, rows), jnp.float32)
    for index, piece in enumerate(split_float(stats[row : row + 1]) + split_float(stats[row + 1 : row + 2])):
        side = jnp.where(line == index, piece, side)
    ref[rows : rows + SIDE, low : low + HD] = jnp.concatenate([side[:, :HD], side[:, HD:]], axis=0).astype(ref.dtype)


def message_stats(ref, head, rows):
    side = ref[rows : rows + SIDE, head * HD : (head + 1) * HD].astype(jnp.float32)
    side = jnp.concatenate([side[:8], side[8:]], axis=1)
    return side[0:1] + side[1:2] + side[2:3], side[3:4] + side[4:5] + side[5:6]


def message_columns(ref, head, rows):
    line = lax.broadcasted_iota(jnp.int32, (8, rows), 0)
    largest, total = message_stats(ref, head, rows)
    columns = jnp.transpose(jnp.where(line == 0, largest, jnp.where(line == 1, total, 0.0)))
    return [jnp.broadcast_to(column(columns, index), (rows, HD)) for index in (0, 1)]


def attend(query, blocks, biases, low, old=None):
    rows = blocks[0].shape[0] // 2
    scale = HD**-0.5 * LOG2E
    spread = lambda value: jnp.broadcast_to(value, (rows, HD))
    parts = [raw_scores(query, block[:rows, low : low + HD]) for block in blocks]
    largest = None if old is None else old[0]
    for part, bias in zip(parts, biases):
        peak = spread(jnp.max(part, axis=1, keepdims=True)) * scale + bias
        largest = peak if largest is None else jnp.maximum(largest, peak)
    summed, mix = None, None
    for part, bias, block in zip(parts, biases, blocks):
        offset = jnp.concatenate([bias - largest] * (rows // HD), axis=1)
        weights = jnp.exp2(part * scale + offset)
        product = jnp.dot(weights.astype(block.dtype), block[rows:, low : low + HD], preferred_element_type=jnp.float32)
        summed = weights if summed is None else summed + weights
        mix = product if mix is None else mix + product
    total = spread(jnp.sum(summed, axis=1, keepdims=True))
    if old is not None:
        shrink = jnp.exp2(old[0] - largest)
        total, mix = total + old[1] * shrink, mix + old[2] * shrink
    return largest, total, mix


def row_stats(largest, total):
    lane = lax.broadcasted_iota(jnp.int32, largest.shape, 1)
    return jnp.transpose(jnp.where(lane == 0, largest, jnp.where(lane == 1, total, 0.0)))[:8]


def block_biases(query_ref, rows):
    wide = wide_window(query_ref, rows)
    return [block_bias(wide, stage) for stage in (1, 2)]


def own_kernel(query_ref, block_ref, weight_ref, mix_ref, stats_ref, mine_ref, sem):
    copy = copy_columns(weight_ref, lax.axis_index("far") * mine_ref.shape[1], mine_ref, sem)
    copy.start()
    rows, width = block_ref.shape[0] // 2, block_ref.shape[1]
    for head in range(width // HD):
        low = head * HD
        largest, total, mix = attend(query_ref[:rows, low : low + HD], [block_ref], [0.0], low)
        mix_ref[head], stats_ref[2 * head], stats_ref[2 * head + 1] = mix, largest, total
    copy.wait()


def attend_own(queries, block, out_weight):
    rows, width = block.shape[0] // 2, block.shape[1]
    heads = width // HD
    whole = pl.BlockSpec(memory_space=VMEM)
    return pl.pallas_call(
        own_kernel,
        out_shape=(
            jax.ShapeDtypeStruct((heads, rows, HD), jnp.float32),
            jax.ShapeDtypeStruct((2 * heads, rows, HD), jnp.float32),
            jax.ShapeDtypeStruct((out_weight.shape[0], out_weight.shape[1] // 2), out_weight.dtype),
        ),
        in_specs=[whole] * 2 + [pl.BlockSpec(memory_space=pl.ANY)],
        out_specs=(whole,) * 3,
        scratch_shapes=[pltpu.SemaphoreType.DMA],
        compiler_params=params(24),
        cost_estimate=pl.CostEstimate(flops=0, bytes_accessed=0, transcendentals=0),
        name="attend_own",
    )(queries, block, pltpu.with_memory_space_constraint(out_weight, pltpu.HBM))


def here_kernel(*refs):
    refs[-1][...] = jnp.zeros_like(refs[-1])


def all_here(*arrays):
    return pl.pallas_call(
        here_kernel,
        out_shape=jax.ShapeDtypeStruct((8, HD), jnp.float32),
        in_specs=[pl.BlockSpec(memory_space=pl.ANY)] * len(arrays),
        out_specs=pl.BlockSpec(memory_space=VMEM),
        compiler_params=params(4),
        cost_estimate=pl.CostEstimate(flops=HERE_FLOPS, bytes_accessed=0, transcendentals=0),
        name="all_here",
    )(*arrays)


def half_rows(weight_shape, rows, width):
    return [rows + SIDE + part * weight_shape[0] for part in range(weight_shape[1] // width)]


def pair_kernel(query_ref, own_ref, first_ref, second_ref, weight_ref, after_ref, out_ref):
    rows, width = first_ref.shape[0] // 2, first_ref.shape[1]
    for part, start in enumerate(half_rows(weight_ref.shape, rows, width)):
        out_ref[start : start + weight_ref.shape[0]] = weight_ref[:, part * width : (part + 1) * width]
    biases = [0.0] + block_biases(query_ref, rows)
    blocks = [own_ref, first_ref, second_ref]
    for head in range(width // HD):
        low = head * HD
        largest, total, mix = attend(query_ref[:rows, low : low + HD], blocks, biases, low)
        put_message(out_ref, head, mix, row_stats(largest, total), 0)


def attend_pair(query, own, first, second, weight, after):
    rows, width = query.shape
    whole = pl.BlockSpec(memory_space=VMEM)
    return pl.pallas_call(
        pair_kernel,
        out_shape=jax.ShapeDtypeStruct((rows + weight.size // width, width), jnp.bfloat16),
        in_specs=[whole] * 5 + [pl.BlockSpec(memory_space=pl.ANY)],
        out_specs=whole,
        compiler_params=params(24),
        cost_estimate=pl.CostEstimate(flops=PAIR_FLOPS, bytes_accessed=2_000_000, transcendentals=0),
        name="attend_pair",
    )(query, own, first, second, weight, after)


def middle_kernel(query_ref, own_ref, first_ref, second_ref, after_ref, out_ref):
    rows, width = own_ref.shape[0] // 2, own_ref.shape[1]
    height = lax.axis_index("tile") % HEIGHT_TILES
    inside = (height > 0) & (height < HEIGHT_TILES - 1)

    @pl.when(inside)
    def compute():
        biases = [0.0] + block_biases(query_ref, rows)
        blocks = [own_ref, first_ref, second_ref]
        for head in range(width // HD):
            low = head * HD
            largest, total, mix = attend(query_ref[:rows, low : low + HD], blocks, biases, low)
            put_message(out_ref, head, mix, row_stats(largest, total), 0)

    @pl.when(jnp.logical_not(inside))
    def skip():
        out_ref[...] = jnp.zeros_like(out_ref)


def attend_middle(query, own, first, second, after):
    whole = pl.BlockSpec(memory_space=VMEM)
    return pl.pallas_call(
        middle_kernel,
        out_shape=jax.ShapeDtypeStruct(query.shape, jnp.bfloat16),
        in_specs=[whole] * 4 + [pl.BlockSpec(memory_space=pl.ANY)],
        out_specs=whole,
        compiler_params=params(24),
        cost_estimate=pl.CostEstimate(flops=MIDDLE_FLOPS, bytes_accessed=2_000_000, transcendentals=0),
        name="attend_middle",
    )(query, own, first, second, after)


def last_kernel(query_ref, first_ref, second_ref, old_mix_ref, old_stats_ref, message_ref, mix_ref, stats_ref):
    rows, width = first_ref.shape[0] // 2, first_ref.shape[1]
    wide = wide_window(query_ref, rows, 1)
    biases = block_biases(query_ref, rows)
    for head in range(width // HD):
        low = head * HD
        old = (old_stats_ref[2 * head], old_stats_ref[2 * head + 1], old_mix_ref[head])
        largest, total, mix = attend(query_ref[:rows, low : low + HD], [first_ref, second_ref], biases, low, old)
        their_largest, their_total = message_columns(message_ref, head, rows)
        peak = jnp.maximum(largest, jnp.where(wide, their_largest, MASKED))
        shrink, share = jnp.exp2(largest - peak), jnp.where(wide, jnp.exp2(their_largest - peak), 0.0)
        stats = row_stats(peak, total * shrink + their_total * share)
        mix_ref[:, low : low + HD] = mix * shrink + message_ref[:rows, low : low + HD].astype(jnp.float32) * share
        line = lax.broadcasted_iota(jnp.int32, stats.shape, 0)
        stats_ref[head] = jnp.where(line == 2, jnp.where(wide, 1.0, 0.0), stats)


def attend_last(queries, first, second, mix, stats, message):
    rows, width = first.shape[0] // 2, first.shape[1]
    whole = pl.BlockSpec(memory_space=VMEM)
    return pl.pallas_call(
        last_kernel,
        out_shape=(
            jax.ShapeDtypeStruct((rows, width), jnp.float32),
            jax.ShapeDtypeStruct((width // HD, 8, rows), jnp.float32),
        ),
        in_specs=[whole] * 6,
        out_specs=(whole, whole),
        compiler_params=params(24),
        cost_estimate=pl.CostEstimate(flops=LAST_FLOPS, bytes_accessed=2_000_000, transcendentals=0),
        name="attend_last",
    )(queries, first, second, mix, stats, message)


def merge_kernel(own_ref, stats_ref, middle_ref, out_ref):
    rows, width = own_ref.shape
    heads = width // HD
    height = lax.axis_index("tile") % HEIGHT_TILES
    inside = jnp.where((height > 0) & (height < HEIGHT_TILES - 1), 1.0, 0.0)
    line = lax.broadcasted_iota(jnp.int32, (8, rows), 0)
    shares = jnp.zeros((8, rows), jnp.float32)
    for head in range(heads):
        stats = stats_ref[head]
        their_largest, their_total = message_stats(middle_ref, head, rows)
        valid = stats[2:3] * inside > 0.5
        peak = jnp.maximum(stats[0:1], jnp.where(valid, their_largest, MASKED))
        shrink = jnp.exp2(stats[0:1] - peak)
        share = jnp.where(valid, jnp.exp2(their_largest - peak), 0.0)
        whole = stats[1:2] * shrink + their_total * share
        shares = jnp.where(line == 2 * head, shrink / whole, shares)
        shares = jnp.where(line == 2 * head + 1, share / whole, shares)
    shares = jnp.transpose(shares)
    for head in range(heads):
        low = head * HD
        value = own_ref[:, low : low + HD] * column(shares, 2 * head)
        value += middle_ref[:rows, low : low + HD].astype(jnp.float32) * column(shares, 2 * head + 1)
        out_ref[:, low : low + HD] = value.astype(out_ref.dtype)


def merge(own, stats, middle):
    whole = pl.BlockSpec(memory_space=VMEM)
    return pl.pallas_call(
        merge_kernel,
        out_shape=jax.ShapeDtypeStruct(own.shape, jnp.bfloat16),
        in_specs=[whole] * 3,
        out_specs=whole,
        compiler_params=params(24),
        name="merge",
    )(own, stats, middle)


def project_mine_kernel(mine_ref, weight_ref, out_ref):
    width = mine_ref.shape[1]
    for group in range(out_ref.shape[0]):
        low = group * width
        out_ref[group] = jnp.dot(mine_ref[...], weight_ref[:, low : low + width], preferred_element_type=jnp.float32)


def project_mine(mine, my_weight):
    rows, width = mine.shape
    groups = my_weight.shape[1] // width
    whole = pl.BlockSpec(memory_space=VMEM)
    return pl.pallas_call(
        project_mine_kernel,
        out_shape=jax.ShapeDtypeStruct((groups, rows, width), jnp.float32),
        in_specs=[whole] * 2,
        out_specs=whole,
        compiler_params=params(24),
        cost_estimate=pl.CostEstimate(flops=2 * groups * rows * width * width, bytes_accessed=0, transcendentals=0),
        name="project_mine",
    )(mine, my_weight)


def project_kernel(mine_ref, theirs_ref, this_ref, other_ref, out_ref, held_ref, sems):
    rows, width = theirs_ref.shape
    core = lax.rem(lax.axis_index("tile"), 2)
    starts = half_rows(this_ref.shape, rows, width)
    copies = []
    for group in range(out_ref.shape[0]):
        side, part = divmod(group, len(starts))
        this = this_ref[:, part * width : (part + 1) * width]
        other = other_ref[starts[part] : starts[part] + this.shape[0]]
        their_weight = jnp.where(side == core, this, other)
        product = jnp.dot(theirs_ref[...], their_weight, preferred_element_type=jnp.float32)
        held_ref[group] = (mine_ref[group] + product).astype(held_ref.dtype)
        copies.append(pltpu.make_async_copy(held_ref.at[group], out_ref.at[group], sems.at[group]))
        copies[-1].start()
    for copy in copies:
        copy.wait()


def project(mine, theirs, this_half, pair_message):
    whole = pl.BlockSpec(memory_space=VMEM)
    return pl.pallas_call(
        project_kernel,
        out_shape=jax.ShapeDtypeStruct(mine.shape, jnp.bfloat16),
        in_specs=[whole] * 4,
        out_specs=pl.BlockSpec(memory_space=pl.ANY),
        scratch_shapes=[pltpu.VMEM(mine.shape, jnp.bfloat16), pltpu.SemaphoreType.DMA((mine.shape[0],))],
        compiler_params=params(24),
        cost_estimate=pl.CostEstimate(flops=300_000_000, bytes_accessed=5_000_000, transcendentals=0),
        name="project",
    )(mine, theirs, this_half, pair_message)


def finish_kernel(terms_ref, residual_ref, gate_ref, out_ref):
    total = jnp.sum(terms_ref[...].astype(jnp.float32), axis=0)
    out_ref[...] = (residual_ref[...].astype(jnp.float32) + gate_ref[...] * total).astype(out_ref.dtype)


def finish(terms, residual, gate_scale):
    whole = pl.BlockSpec(memory_space=VMEM)
    return pl.pallas_call(
        finish_kernel,
        out_shape=jax.ShapeDtypeStruct(residual.shape, residual.dtype),
        in_specs=[whole] * 3,
        out_specs=whole,
        compiler_params=params(24),
        cost_estimate=pl.CostEstimate(flops=10 * terms.size, bytes_accessed=2_000_000, transcendentals=0),
        name="finish",
    )(terms, residual, gate_scale.reshape(1, -1))


def shards(queries, key_rows, value_rows, windows, residual, out_weight, gate_scale):
    packed, block = pack(windows, queries, key_rows, value_rows)
    first, second = swap_times(block, False), swap_times(block, True)
    pair_asks, middle_asks = swap_pair(packed), swap_middle(packed)
    this_half = swap_far(split_weight(out_weight))
    mix, stats, my_weight = attend_own(packed, block, out_weight)
    here = all_here(first, second, middle_asks, stats)
    for_pair = attend_pair(pair_asks, block, first, second, this_half, here)
    for_middle = attend_middle(middle_asks, block, first, second, for_pair)
    from_pair = swap_pair(for_pair)
    mix, stats = attend_last(packed, first, second, mix, stats, from_pair)
    attention = merge(mix, stats, swap_middle(for_middle))
    mine = project_mine(attention, my_weight)
    terms = project(mine, swap_far(attention), this_half, from_pair)
    terms = lax.all_to_all(terms, "group", 0, 0)
    return finish(terms, residual, gate_scale)


def solution(mesh):
    devices = np.asarray(mesh.devices)
    tiles, heads = devices.shape
    split = jax.sharding.Mesh(devices.reshape(tiles, 2, heads // 2), ("tile", "far", "group"))
    head = ("far", "group")
    return jax.shard_map(
        shards,
        mesh=split,
        in_specs=(
            P("tile", head),
            P("tile", head),
            P("tile", head),
            P("tile", None),
            P("tile", head),
            P(head, None),
            P(head),
        ),
        out_specs=P("tile", head),
        check_vma=False,
    )
```

```python
import functools

import jax
import jax.numpy as jnp
import numpy as np
from jax import lax
from jax.experimental import pallas as pl
from jax.experimental.pallas import tpu as pltpu
from jax.sharding import PartitionSpec as P

HD = 128
HEIGHT_TILES = 4
SIDE = 16
LOG2E = 1.4426950408889634
MASKED = -1e30
LAST_FLOPS = 400_000_000
MIDDLE_FLOPS = 600_000_000
PAIR_FLOPS = 400_000_000
HERE_FLOPS = 5_000_000_000
MESH_AXES = ("tile", "head")
VMEM = pltpu.VMEM
SMEM = pltpu.SMEM


def params(megabytes):
    return pltpu.CompilerParams(vmem_limit_bytes=megabytes * 1024 * 1024)


def places():
    tiles = lax.axis_size("tile")
    return [(tile, *divmod(tile, HEIGHT_TILES), tiles // HEIGHT_TILES) for tile in range(tiles)]


def swap_times(block, later):
    route = []
    for tile, time, height, times in places():
        partner = time + 1 if time % 2 == int(not later) else time - 1
        if 0 <= partner < times:
            route.append((tile, partner * HEIGHT_TILES + height))
    return lax.ppermute(block, "tile", route)


def swap_pair(block):
    return lax.ppermute(block, "tile", [(tile, tile ^ 1) for tile, *_ in places()])


def swap_middle(block):
    route = [(tile, tile + (1 if height == 1 else -1)) for tile, _, height, _ in places() if height in (1, 2)]
    return lax.ppermute(block, "tile", route)


def swap_far(block):
    return lax.ppermute(block, "far", [(0, 1), (1, 0)])


def copy_columns(weight_ref, start, out_ref, sem):
    return pltpu.make_async_copy(weight_ref.at[:, pl.ds(pl.multiple_of(start, HD), out_ref.shape[1])], out_ref, sem)


def split_weight_kernel(weight_ref, theirs_ref, sem):
    half = theirs_ref.shape[1]
    core = lax.rem(lax.axis_index("tile"), 2)
    copy = copy_columns(weight_ref, ((1 - lax.axis_index("far")) * 2 + core) * half, theirs_ref, sem)
    copy.start()
    copy.wait()


def split_weight(out_weight):
    rows, features = out_weight.shape
    return pl.pallas_call(
        split_weight_kernel,
        out_shape=jax.ShapeDtypeStruct((rows, features // 4), out_weight.dtype),
        in_specs=[pl.BlockSpec(memory_space=pl.ANY)],
        out_specs=pl.BlockSpec(memory_space=VMEM),
        scratch_shapes=[pltpu.SemaphoreType.DMA],
        compiler_params=params(24),
        cost_estimate=pl.CostEstimate(flops=0, bytes_accessed=0, transcendentals=0),
        name="split_weight",
    )(pltpu.with_memory_space_constraint(out_weight, pltpu.HBM))


def pack_kernel(windows_ref, q_ref, k_ref, v_ref, packed_ref, block_ref):
    rows = q_ref.shape[0]
    block_ref[:rows] = k_ref[...]
    block_ref[rows:] = v_ref[...]
    packed_ref[:rows] = q_ref[...]
    for axis in (0, 1):
        extent = windows_ref[0, axis].astype(jnp.float32)
        packed_ref[rows:, axis * HD : (axis + 1) * HD] = jnp.full((SIDE, HD), extent, jnp.float32).astype(packed_ref.dtype)
    packed_ref[rows:, 2 * HD :] = jnp.zeros((SIDE, q_ref.shape[1] - 2 * HD), packed_ref.dtype)


def pack(windows, queries, key_rows, value_rows):
    rows, width = queries.shape
    whole = pl.BlockSpec(memory_space=VMEM)
    return pl.pallas_call(
        pack_kernel,
        out_shape=(
            jax.ShapeDtypeStruct((rows + SIDE, width), queries.dtype),
            jax.ShapeDtypeStruct((2 * rows, width), queries.dtype),
        ),
        in_specs=[pl.BlockSpec(memory_space=SMEM)] + [whole] * 3,
        out_specs=(whole, whole),
        name="pack",
    )(windows, queries, key_rows, value_rows)


def column(values, index):
    return values[:, index : index + 1]


def split_float(value):
    high = value.astype(jnp.bfloat16).astype(jnp.float32)
    rest = value - high
    middle = rest.astype(jnp.bfloat16).astype(jnp.float32)
    return high, middle, (rest - middle).astype(jnp.bfloat16).astype(jnp.float32)


def wide_window(ref, rows, axis=0):
    return jnp.max(ref[rows:, axis * HD : (axis + 1) * HD].astype(jnp.float32)) > 0.5


def has_first():
    time = lax.axis_index("tile") // HEIGHT_TILES
    return (time > 0) & (time < lax.axis_size("tile") // HEIGHT_TILES - 1)


def block_bias(wide, stage):
    return jnp.where(wide & has_first() if stage == 1 else wide, 0.0, MASKED)


def raw_scores(query, keys):
    return lax.dot_general(query, keys, (((1,), (1,)), ((), ())), preferred_element_type=jnp.float32)


def put_message(ref, head, mix, stats, row):
    rows = mix.shape[0]
    low = head * HD
    line = lax.broadcasted_iota(jnp.int32, (8, rows), 0)
    ref[:rows, low : low + HD] = mix.astype(ref.dtype)
    side = jnp.zeros((8, rows), jnp.float32)
    for index, piece in enumerate(split_float(stats[row : row + 1]) + split_float(stats[row + 1 : row + 2])):
        side = jnp.where(line == index, piece, side)
    ref[rows : rows + SIDE, low : low + HD] = jnp.concatenate([side[:, :HD], side[:, HD:]], axis=0).astype(ref.dtype)


def message_stats(ref, head, rows):
    side = ref[rows : rows + SIDE, head * HD : (head + 1) * HD].astype(jnp.float32)
    side = jnp.concatenate([side[:8], side[8:]], axis=1)
    return side[0:1] + side[1:2] + side[2:3], side[3:4] + side[4:5] + side[5:6]


def message_columns(ref, head, rows):
    line = lax.broadcasted_iota(jnp.int32, (8, rows), 0)
    largest, total = message_stats(ref, head, rows)
    columns = jnp.transpose(jnp.where(line == 0, largest, jnp.where(line == 1, total, 0.0)))
    return [jnp.broadcast_to(column(columns, index), (rows, HD)) for index in (0, 1)]


def attend(query, blocks, biases, low, old=None):
    rows = blocks[0].shape[0] // 2
    scale = HD**-0.5 * LOG2E
    spread = lambda value: jnp.broadcast_to(value, (rows, HD))
    parts = [raw_scores(query, block[:rows, low : low + HD]) for block in blocks]
    largest = None if old is None else old[0]
    for part, bias in zip(parts, biases):
        peak = spread(jnp.max(part, axis=1, keepdims=True)) * scale + bias
        largest = peak if largest is None else jnp.maximum(largest, peak)
    summed, mix = None, None
    for part, bias, block in zip(parts, biases, blocks):
        offset = jnp.concatenate([bias - largest] * (rows // HD), axis=1)
        weights = jnp.exp2(part * scale + offset)
        product = jnp.dot(weights.astype(block.dtype), block[rows:, low : low + HD], preferred_element_type=jnp.float32)
        summed = weights if summed is None else summed + weights
        mix = product if mix is None else mix + product
    total = spread(jnp.sum(summed, axis=1, keepdims=True))
    if old is not None:
        shrink = jnp.exp2(old[0] - largest)
        total, mix = total + old[1] * shrink, mix + old[2] * shrink
    return largest, total, mix


def row_stats(largest, total):
    lane = lax.broadcasted_iota(jnp.int32, largest.shape, 1)
    return jnp.transpose(jnp.where(lane == 0, largest, jnp.where(lane == 1, total, 0.0)))[:8]


def block_biases(query_ref, rows):
    wide = wide_window(query_ref, rows)
    return [block_bias(wide, stage) for stage in (1, 2)]


def own_kernel(query_ref, block_ref, weight_ref, mix_ref, stats_ref, mine_ref, sem):
    copy = copy_columns(weight_ref, lax.axis_index("far") * mine_ref.shape[1], mine_ref, sem)
    copy.start()
    rows, width = block_ref.shape[0] // 2, block_ref.shape[1]
    for head in range(width // HD):
        low = head * HD
        largest, total, mix = attend(query_ref[:rows, low : low + HD], [block_ref], [0.0], low)
        mix_ref[head], stats_ref[2 * head], stats_ref[2 * head + 1] = mix, largest, total
    copy.wait()


def attend_own(queries, block, out_weight):
    rows, width = block.shape[0] // 2, block.shape[1]
    heads = width // HD
    whole = pl.BlockSpec(memory_space=VMEM)
    return pl.pallas_call(
        own_kernel,
        out_shape=(
            jax.ShapeDtypeStruct((heads, rows, HD), jnp.float32),
            jax.ShapeDtypeStruct((2 * heads, rows, HD), jnp.float32),
            jax.ShapeDtypeStruct((out_weight.shape[0], out_weight.shape[1] // 2), out_weight.dtype),
        ),
        in_specs=[whole] * 2 + [pl.BlockSpec(memory_space=pl.ANY)],
        out_specs=(whole,) * 3,
        scratch_shapes=[pltpu.SemaphoreType.DMA],
        compiler_params=params(24),
        cost_estimate=pl.CostEstimate(flops=0, bytes_accessed=0, transcendentals=0),
        name="attend_own",
    )(queries, block, pltpu.with_memory_space_constraint(out_weight, pltpu.HBM))


def here_kernel(*refs):
    refs[-1][...] = jnp.zeros_like(refs[-1])


def all_here(*arrays):
    return pl.pallas_call(
        here_kernel,
        out_shape=jax.ShapeDtypeStruct((8, HD), jnp.float32),
        in_specs=[pl.BlockSpec(memory_space=pl.ANY)] * len(arrays),
        out_specs=pl.BlockSpec(memory_space=VMEM),
        compiler_params=params(4),
        cost_estimate=pl.CostEstimate(flops=HERE_FLOPS, bytes_accessed=0, transcendentals=0),
        name="all_here",
    )(*arrays)


def half_rows(weight_shape, rows, width):
    return [rows + SIDE + part * weight_shape[0] for part in range(weight_shape[1] // width)]


def pair_kernel(query_ref, own_ref, first_ref, second_ref, weight_ref, after_ref, out_ref):
    rows, width = first_ref.shape[0] // 2, first_ref.shape[1]
    for part, start in enumerate(half_rows(weight_ref.shape, rows, width)):
        out_ref[start : start + weight_ref.shape[0]] = weight_ref[:, part * width : (part + 1) * width]
    biases = [0.0] + block_biases(query_ref, rows)
    blocks = [own_ref, first_ref, second_ref]
    for head in range(width // HD):
        low = head * HD
        largest, total, mix = attend(query_ref[:rows, low : low + HD], blocks, biases, low)
        put_message(out_ref, head, mix, row_stats(largest, total), 0)


def attend_pair(query, own, first, second, weight, after):
    rows, width = query.shape
    whole = pl.BlockSpec(memory_space=VMEM)
    return pl.pallas_call(
        pair_kernel,
        out_shape=jax.ShapeDtypeStruct((rows + weight.size // width, width), jnp.bfloat16),
        in_specs=[whole] * 5 + [pl.BlockSpec(memory_space=pl.ANY)],
        out_specs=whole,
        compiler_params=params(24),
        cost_estimate=pl.CostEstimate(flops=PAIR_FLOPS, bytes_accessed=2_000_000, transcendentals=0),
        name="attend_pair",
    )(query, own, first, second, weight, after)


def middle_kernel(query_ref, own_ref, first_ref, second_ref, after_ref, out_ref):
    rows, width = own_ref.shape[0] // 2, own_ref.shape[1]
    height = lax.axis_index("tile") % HEIGHT_TILES
    inside = (height > 0) & (height < HEIGHT_TILES - 1)

    @pl.when(inside)
    def compute():
        biases = [0.0] + block_biases(query_ref, rows)
        blocks = [own_ref, first_ref, second_ref]
        for head in range(width // HD):
            low = head * HD
            largest, total, mix = attend(query_ref[:rows, low : low + HD], blocks, biases, low)
            put_message(out_ref, head, mix, row_stats(largest, total), 0)

    @pl.when(jnp.logical_not(inside))
    def skip():
        out_ref[...] = jnp.zeros_like(out_ref)


def attend_middle(query, own, first, second, after):
    whole = pl.BlockSpec(memory_space=VMEM)
    return pl.pallas_call(
        middle_kernel,
        out_shape=jax.ShapeDtypeStruct(query.shape, jnp.bfloat16),
        in_specs=[whole] * 4 + [pl.BlockSpec(memory_space=pl.ANY)],
        out_specs=whole,
        compiler_params=params(24),
        cost_estimate=pl.CostEstimate(flops=MIDDLE_FLOPS, bytes_accessed=2_000_000, transcendentals=0),
        name="attend_middle",
    )(query, own, first, second, after)


def last_kernel(query_ref, first_ref, second_ref, old_mix_ref, old_stats_ref, message_ref, mix_ref, stats_ref):
    rows, width = first_ref.shape[0] // 2, first_ref.shape[1]
    wide = wide_window(query_ref, rows, 1)
    biases = block_biases(query_ref, rows)
    for head in range(width // HD):
        low = head * HD
        old = (old_stats_ref[2 * head], old_stats_ref[2 * head + 1], old_mix_ref[head])
        largest, total, mix = attend(query_ref[:rows, low : low + HD], [first_ref, second_ref], biases, low, old)
        their_largest, their_total = message_columns(message_ref, head, rows)
        peak = jnp.maximum(largest, jnp.where(wide, their_largest, MASKED))
        shrink, share = jnp.exp2(largest - peak), jnp.where(wide, jnp.exp2(their_largest - peak), 0.0)
        stats = row_stats(peak, total * shrink + their_total * share)
        mix_ref[:, low : low + HD] = mix * shrink + message_ref[:rows, low : low + HD].astype(jnp.float32) * share
        line = lax.broadcasted_iota(jnp.int32, stats.shape, 0)
        stats_ref[head] = jnp.where(line == 2, jnp.where(wide, 1.0, 0.0), stats)


def attend_last(queries, first, second, mix, stats, message):
    rows, width = first.shape[0] // 2, first.shape[1]
    whole = pl.BlockSpec(memory_space=VMEM)
    return pl.pallas_call(
        last_kernel,
        out_shape=(
            jax.ShapeDtypeStruct((rows, width), jnp.float32),
            jax.ShapeDtypeStruct((width // HD, 8, rows), jnp.float32),
        ),
        in_specs=[whole] * 6,
        out_specs=(whole, whole),
        compiler_params=params(24),
        cost_estimate=pl.CostEstimate(flops=LAST_FLOPS, bytes_accessed=2_000_000, transcendentals=0),
        name="attend_last",
    )(queries, first, second, mix, stats, message)


def merge_kernel(own_ref, stats_ref, middle_ref, out_ref):
    rows, width = own_ref.shape
    heads = width // HD
    height = lax.axis_index("tile") % HEIGHT_TILES
    inside = jnp.where((height > 0) & (height < HEIGHT_TILES - 1), 1.0, 0.0)
    line = lax.broadcasted_iota(jnp.int32, (8, rows), 0)
    shares = jnp.zeros((8, rows), jnp.float32)
    for head in range(heads):
        stats = stats_ref[head]
        their_largest, their_total = message_stats(middle_ref, head, rows)
        valid = stats[2:3] * inside > 0.5
        peak = jnp.maximum(stats[0:1], jnp.where(valid, their_largest, MASKED))
        shrink = jnp.exp2(stats[0:1] - peak)
        share = jnp.where(valid, jnp.exp2(their_largest - peak), 0.0)
        whole = stats[1:2] * shrink + their_total * share
        shares = jnp.where(line == 2 * head, shrink / whole, shares)
        shares = jnp.where(line == 2 * head + 1, share / whole, shares)
    shares = jnp.transpose(shares)
    for head in range(heads):
        low = head * HD
        value = own_ref[:, low : low + HD] * column(shares, 2 * head)
        value += middle_ref[:rows, low : low + HD].astype(jnp.float32) * column(shares, 2 * head + 1)
        out_ref[:, low : low + HD] = value.astype(out_ref.dtype)


def merge(own, stats, middle):
    whole = pl.BlockSpec(memory_space=VMEM)
    return pl.pallas_call(
        merge_kernel,
        out_shape=jax.ShapeDtypeStruct(own.shape, jnp.bfloat16),
        in_specs=[whole] * 3,
        out_specs=whole,
        compiler_params=params(24),
        name="merge",
    )(own, stats, middle)


def project_mine_kernel(mine_ref, weight_ref, out_ref):
    width = mine_ref.shape[1]
    for group in range(out_ref.shape[0]):
        low = group * width
        out_ref[group] = jnp.dot(mine_ref[...], weight_ref[:, low : low + width], preferred_element_type=jnp.float32)


def project_mine(mine, my_weight):
    rows, width = mine.shape
    groups = my_weight.shape[1] // width
    whole = pl.BlockSpec(memory_space=VMEM)
    return pl.pallas_call(
        project_mine_kernel,
        out_shape=jax.ShapeDtypeStruct((groups, rows, width), jnp.float32),
        in_specs=[whole] * 2,
        out_specs=whole,
        compiler_params=params(24),
        cost_estimate=pl.CostEstimate(flops=2 * groups * rows * width * width, bytes_accessed=0, transcendentals=0),
        name="project_mine",
    )(mine, my_weight)


def project_kernel(mine_ref, theirs_ref, this_ref, other_ref, out_ref, held_ref, sems):
    rows, width = theirs_ref.shape
    core = lax.rem(lax.axis_index("tile"), 2)
    starts = half_rows(this_ref.shape, rows, width)
    copies = []
    for group in range(out_ref.shape[0]):
        side, part = divmod(group, len(starts))
        this = this_ref[:, part * width : (part + 1) * width]
        other = other_ref[starts[part] : starts[part] + this.shape[0]]
        their_weight = jnp.where(side == core, this, other)
        product = jnp.dot(theirs_ref[...], their_weight, preferred_element_type=jnp.float32)
        held_ref[group] = (mine_ref[group] + product).astype(held_ref.dtype)
        copies.append(pltpu.make_async_copy(held_ref.at[group], out_ref.at[group], sems.at[group]))
        copies[-1].start()
    for copy in copies:
        copy.wait()


def project(mine, theirs, this_half, pair_message):
    whole = pl.BlockSpec(memory_space=VMEM)
    return pl.pallas_call(
        project_kernel,
        out_shape=jax.ShapeDtypeStruct(mine.shape, jnp.bfloat16),
        in_specs=[whole] * 4,
        out_specs=pl.BlockSpec(memory_space=pl.ANY),
        scratch_shapes=[pltpu.VMEM(mine.shape, jnp.bfloat16), pltpu.SemaphoreType.DMA((mine.shape[0],))],
        compiler_params=params(24),
        cost_estimate=pl.CostEstimate(flops=300_000_000, bytes_accessed=5_000_000, transcendentals=0),
        name="project",
    )(mine, theirs, this_half, pair_message)


def finish_kernel(terms_ref, residual_ref, gate_ref, out_ref):
    total = jnp.sum(terms_ref[...].astype(jnp.float32), axis=0)
    out_ref[...] = (residual_ref[...].astype(jnp.float32) + gate_ref[...] * total).astype(out_ref.dtype)


def finish(terms, residual, gate_scale):
    whole = pl.BlockSpec(memory_space=VMEM)
    return pl.pallas_call(
        finish_kernel,
        out_shape=jax.ShapeDtypeStruct(residual.shape, residual.dtype),
        in_specs=[whole] * 3,
        out_specs=whole,
        compiler_params=params(24),
        cost_estimate=pl.CostEstimate(flops=10 * terms.size, bytes_accessed=2_000_000, transcendentals=0),
        name="finish",
    )(terms, residual, gate_scale.reshape(1, -1))


def shards(queries, key_rows, value_rows, windows, residual, out_weight, gate_scale):
    packed, block = pack(windows, queries, key_rows, value_rows)
    first, second = swap_times(block, False), swap_times(block, True)
    pair_asks, middle_asks = swap_pair(packed), swap_middle(packed)
    this_half = swap_far(split_weight(out_weight))
    mix, stats, my_weight = attend_own(packed, block, out_weight)
    here = all_here(first, second, middle_asks, stats)
    for_pair = attend_pair(pair_asks, block, first, second, this_half, here)
    for_middle = attend_middle(middle_asks, block, first, second, for_pair)
    from_pair = swap_pair(for_pair)
    mix, stats = attend_last(packed, first, second, mix, stats, from_pair)
    attention = merge(mix, stats, swap_middle(for_middle))
    mine = project_mine(attention, my_weight)
    terms = project(mine, swap_far(attention), this_half, from_pair)
    terms = lax.all_to_all(terms, "group", 0, 0)
    return finish(terms, residual, gate_scale)


def solution(mesh):
    devices = np.asarray(mesh.devices)
    tiles, heads = devices.shape
    split = jax.sharding.Mesh(devices.reshape(tiles, 2, heads // 2), ("tile", "far", "group"))
    head = ("far", "group")
    return jax.shard_map(
        shards,
        mesh=split,
        in_specs=(
            P("tile", head),
            P("tile", head),
            P("tile", head),
            P("tile", None),
            P("tile", head),
            P(head, None),
            P(head),
        ),
        out_specs=P("tile", head),
        check_vma=False,
    )
```
